32 devices in a mesh: row: 8 (over z, x), col: 4 (over y, core).
Axes of the slice: x: 2, y: 2, z: 4, core: 2. Of those that a mesh axis runs over, the one named last changes fastest.
Arguments:
- query_nope: bfloat16 [8, 128, 128], P(None, 'row'), may hold values from -9 to 9
- query_rope: bfloat16 [8, 128, 64], P(None, 'row'), may hold values from -10 to 80
- key_up_weight: bfloat16 [128, 128, 512], P('row'), may hold values from -0.5 to 0.5
- value_up_weight: bfloat16 [128, 512, 128], P('row'), may hold values from -0.25 to 0.25
- latent_cache: bfloat16 [131072, 576], P(('row', 'col')), may hold values from -6 to 6
- lengths: int32 [8], replicated, may hold values from 1 to 16384, as said below
- page_table: int32 [8, 256], replicated, may hold values from -1 to 2047, as said below
Outputs:
- head_values: bfloat16 [8, 16384], P(None, 'row')
The draws below stay inside these ranges and needn't reach their ends.
Inputs may be any that keep to these rules, and one draw needn't show every extreme that they name: `lengths`: the largest length is exactly 16384. `page_table`: entry (r, p) is -1 exactly when p * 64 >= lengths[r]; all other entries are distinct cache pages, page k lying on the device of index k // 64 along row+col.
All inputs are finite; a program needn't handle non-finite values.
Results may differ from the reference program's by a relative error of at most 0.0094.
Values may be sent and summed in bfloat16 or wider, within the bound.
A program may use at most 128 MiB of HBM per device.

```python
import jax
import jax.numpy as jnp
from jax import lax

HEAD_COUNT = 128
HEAD_NOPE_WIDTH = 128
ROTARY_WIDTH = 64
LATENT_WIDTH = 512
HEAD_VALUE_WIDTH = 128
PAGE = 64
REQS = 8
SLOTS = 2048
PAGES_MAX = 256
LMAX = 16384
CACHE_ROWS = 131072


def paged_layout(key):
    leading_key, second_key, third_key = jax.random.split(key, 3)
    longest = jax.random.randint(leading_key, (), 0, REQS)
    spans = jax.random.randint(second_key, (REQS,), 1, LMAX + 1)
    spans = jnp.where(jnp.arange(REQS) == longest, LMAX, spans).astype(jnp.int32)
    order = jax.random.permutation(third_key, SLOTS).astype(jnp.int32).reshape(REQS, PAGES_MAX)
    live = jnp.arange(PAGES_MAX)[None, :] * PAGE < spans[:, None]
    return (spans, jnp.where(live, order, -1).astype(jnp.int32))


def draw_lengths(key, part):
    return paged_layout(key)[0]


def draw_page_table(key, part):
    return paged_layout(key)[1]


def draw_latent_cache(key, part):
    key = jax.random.fold_in(key, 11)
    leading_key = jax.random.fold_in(key, 0)
    return jax.random.truncated_normal(leading_key, -6.0, 6.0, (CACHE_ROWS, LATENT_WIDTH + ROTARY_WIDTH), jnp.float32).astype(jnp.bfloat16)


def draw_query_rope(key, part):
    key = jax.random.fold_in(key, 23)
    leading_key = jax.random.fold_in(key, 0)
    return (2.3 * jax.random.truncated_normal(leading_key, -4.0, 4.0, (REQS, HEAD_COUNT, ROTARY_WIDTH), jnp.float32)).astype(jnp.bfloat16)


def block_levels(key, extent, pieces, smallest, top_value):
    def one(axis_at, parts):
        steps = jax.random.uniform(jax.random.fold_in(jax.random.fold_in(key, 6), axis_at), (parts,), jnp.float32, smallest / len(pieces), top_value / len(pieces))
        return jnp.repeat(jnp.exp(steps), extent[axis_at] // parts).reshape((-1,) + (1,) * (len(extent) - axis_at - 1))

    factor_of = one(*pieces[0])
    for cut in pieces[1:]:
        factor_of = factor_of * one(*cut)
    return factor_of


def centred(rng, shape, deviation, bound, cuts=(), kind=jnp.bfloat16):
    entries = jax.random.normal(rng, shape, jnp.float32) * deviation
    if len(cuts) > 0:
        entries = block_levels(rng, shape, cuts, -0.22, 0.18) * entries
    return jnp.clip(entries, min=-bound, max=bound).astype(kind)


def setup_inputs(seed: int = 0) -> dict:
    splits = jax.random.split(jax.random.key(seed), 8)
    return {
        "query_nope": centred(splits[0], (REQS, HEAD_COUNT, HEAD_NOPE_WIDTH), 2.3, 9.0, ((1, 8),)),
        "query_rope": draw_query_rope(jax.random.fold_in(splits[7], 71), 0),
        "key_up_weight": centred(splits[2], (HEAD_COUNT, HEAD_NOPE_WIDTH, LATENT_WIDTH), HEAD_NOPE_WIDTH ** -0.5, 0.5, ((0, 8),)),
        "value_up_weight": centred(splits[3], (HEAD_COUNT, LATENT_WIDTH, HEAD_VALUE_WIDTH), LATENT_WIDTH ** -0.5, 0.25, ((0, 8),)),
        "latent_cache": draw_latent_cache(jax.random.fold_in(splits[7], 71), 0),
        "lengths": draw_lengths(jax.random.fold_in(splits[7], 71), 0),
        "page_table": draw_page_table(jax.random.fold_in(splits[7], 71), 0),
    }


MASKED = -1.0e30


def reference(query_nope, query_rope, key_up_weight, value_up_weight, latent_cache, lengths, page_table):
    scale = float(HEAD_NOPE_WIDTH + ROTARY_WIDTH) ** -0.5
    query_latent = jnp.einsum('rhn,hnc->rhc', query_nope.astype(jnp.float32), key_up_weight.astype(jnp.float32)).astype(jnp.bfloat16)
    query = jnp.concatenate([query_latent, query_rope], axis=2)
    width = latent_cache.shape[1]
    pages = latent_cache.reshape(SLOTS, PAGE, width)
    span = PAGES_MAX * PAGE

    def one_request(items):
        request_query, length, table_row = items
        key_rows = pages[jnp.maximum(table_row, 0)].reshape(span, width).astype(jnp.float32)
        position = jnp.arange(span, dtype=jnp.int32)
        live = (position < length) & jnp.repeat(table_row >= 0, PAGE)
        scores = jnp.dot(request_query.astype(jnp.float32), key_rows.T) * scale
        scores = jnp.where(live[None, :], scores, MASKED)
        page_top = jnp.max(scores.reshape(HEAD_COUNT, PAGES_MAX, PAGE), axis=2)
        expo = jnp.where(live[None, :], jnp.exp(scores - jnp.repeat(page_top, PAGE, axis=1)), 0.0)
        expo = lax.optimization_barrier(expo.astype(jnp.bfloat16)).astype(jnp.float32)
        top = jnp.max(page_top, axis=1)
        page_weight = jnp.exp(page_top - top[:, None])
        softmax_weight = (expo.reshape(HEAD_COUNT, PAGES_MAX, PAGE) * page_weight[:, :, None]).reshape(HEAD_COUNT, span)
        denom = jnp.sum(softmax_weight, axis=1)
        weighted_latent_sum = jnp.dot(softmax_weight, key_rows[:, :LATENT_WIDTH], precision=lax.Precision.HIGHEST)
        return (weighted_latent_sum / denom[:, None]).astype(jnp.bfloat16)

    attended = lax.map(one_request, (query, lengths, page_table))
    values = jnp.einsum('rhc,hcv->rhv', attended.astype(jnp.float32), value_up_weight.astype(jnp.float32))
    return values.astype(jnp.bfloat16).reshape(REQS, HEAD_COUNT * HEAD_VALUE_WIDTH)
```

```python
import functools

import jax
import jax.numpy as jnp
from jax import lax
from jax.experimental import pallas as pl
from jax.experimental.pallas import tpu as pltpu
from jax.sharding import PartitionSpec as P

HEAD_NOPE_WIDTH = 128
ROTARY_WIDTH = 64
PAGE = 64
GROUP = 4
MASKED = -1e30
MESH = pl.DeviceIdType.MESH
VMEM_LIMIT = 48 * 1024 * 1024


def place(nrh):
    row, col = lax.axis_index("row"), lax.axis_index("col")
    return row // 2, row % 2, col // 4, (col // 2) % 2, col % 2


def device(rh, rl, cg, yl, core):
    return (rh * 2 + rl, cg * 4 + yl * 2 + core)


def greet(peers):
    barrier = pltpu.get_barrier_semaphore()
    for peer in peers:
        pl.semaphore_signal(barrier, inc=1, device_id=peer, device_id_type=MESH)
    pl.semaphore_wait(barrier, len(peers))


def head_diagonal(rows, weights_ref, heads):
    count = rows.shape[0]
    head = lax.broadcasted_iota(jnp.int32, (count, weights_ref.shape[2]), 0) % heads
    total = jnp.zeros((count, weights_ref.shape[2]), jnp.float32)
    for h in range(heads):
        product = jnp.dot(rows, weights_ref[h], preferred_element_type=jnp.float32)
        total = jnp.where(head == h, product, total)
    return total


def gather_kernel(nrh, heads, nope_ref, rope_ref, weights_ref, out_ref, send, recv):
    rh, rl, cg, yl, core = place(nrh)
    q = yl * 2 + core
    qy = (1 - yl) * 2 + core
    z_peer = lambda k: device(k, rl, cg, yl, core)
    x_peer = device(rh, 1 - rl, cg, yl, core)
    y_peer = device(rh, rl, cg, 1 - yl, core)
    c_peer = device(rh, rl, cg, yl, 1 - core)
    greet([z_peer((rh + d) % nrh) for d in range(1, nrh)] + [x_peer, y_peer, c_peer])

    rows = nope_ref[pl.ds(pl.multiple_of(q * 2 * heads, 2 * heads), 2 * heads), :]
    latent = head_diagonal(rows.astype(jnp.bfloat16), weights_ref, heads)
    latent = latent.astype(jnp.bfloat16).astype(out_ref.dtype)
    width = weights_ref.shape[2]
    for i in range(2):
        out_ref[2 * q + i, rl, rh, :, 0:width] = latent[i * heads : (i + 1) * heads]
        out_ref[2 * q + i, rl, rh, :, width:] = rope_ref[2 * q + i]

    started = []

    def copy(a, k, b, slot, peer, send_slot=None):
        shard = out_ref.at[pl.ds(2 * b, 2), a, k]
        return pltpu.make_async_remote_copy(
            src_ref=shard,
            dst_ref=shard,
            send_sem=send.at[slot if send_slot is None else send_slot],
            recv_sem=recv.at[slot],
            device_id=peer,
            device_id_type=MESH,
        )

    def push(*args, **kw):
        one = copy(*args, **kw)
        one.start()
        started.append(one)

    def arrived(a, k, b, slot, peer):
        copy(a, k, b, slot, peer).wait_recv()

    Z, X, Y, D, C = 0, nrh, 2 * nrh, 3 * nrh, 4 * nrh
    half = nrh // 2

    def spread(k):
        push(rl, k, q, X + k, x_peer)
        push(rl, k, q, Y + k, y_peer)
        push(rl, k, q, C + k, c_peer)

    for d in range(1, nrh):
        push(rl, rh, q, Z + rh, z_peer((rh + d) % nrh), send_slot=Z + d)
    spread(rh)
    for d in range(1, nrh):
        k = (rh + d) % nrh
        arrived(rl, k, q, Z + k, z_peer(k))
        spread(k)
    for k in range(nrh):
        arrived(1 - rl, k, q, X + k, x_peer)
        if k >= half:
            push(1 - rl, k, q, D + k, y_peer)
        push(1 - rl, k, q, C + nrh + k, c_peer)
        arrived(rl, k, qy, Y + k, y_peer)
        if k < half:
            push(rl, k, qy, D + k, x_peer)
        push(rl, k, qy, C + 2 * nrh + k, c_peer)
    for k in range(nrh):
        arrived(1 - rl, k, qy, D + k, x_peer if k < half else y_peer)
        push(1 - rl, k, qy, C + 3 * nrh + k, c_peer)
    qc, qyc = yl * 2 + 1 - core, (1 - yl) * 2 + 1 - core
    for k in range(nrh):
        arrived(rl, k, qc, C + k, c_peer)
        arrived(1 - rl, k, qc, C + nrh + k, c_peer)
        arrived(rl, k, qyc, C + 2 * nrh + k, c_peer)
        arrived(1 - rl, k, qyc, C + 3 * nrh + k, c_peer)
    for one in started:
        one.wait_send()


def attend_kernel(
    scale, order_ref, live_ref, first_ref, query_ref, cache_ref, part_ref, stat_ref,
    keys, scores, total, sem,
):
    requests = query_ref.shape[0]
    width = part_ref.shape[2]
    count = first_ref[requests]

    def fetch(k):
        return pltpu.make_async_copy(cache_ref.at[order_ref[k]], keys.at[k], sem.at[k])

    lax.fori_loop(0, count, lambda k, c: (fetch(k).start(), c)[1], 0)
    for i in range(GROUP - 1):
        keys[count + i] = jnp.zeros(keys.shape[1:], keys.dtype)
    lax.fori_loop(0, count, lambda k, c: (fetch(k).wait(), c)[1], 0)

    token = lax.broadcasted_iota(jnp.int32, (PAGE, query_ref.shape[1]), 0)
    line = lax.broadcasted_iota(jnp.int32, stat_ref.shape[1:], 0)
    for r in range(requests):
        begin, end = first_ref[r], first_ref[r + 1]
        groups = (end - begin + GROUP - 1) // GROUP

        def score_step(g, top):
            at = begin + g * GROUP
            rows = keys[pl.ds(at, GROUP)].reshape(GROUP * PAGE, keys.shape[2])
            score = lax.dot_general(
                rows, query_ref[r], (((1,), (1,)), ((), ())), preferred_element_type=jnp.float32
            )
            for j in range(GROUP):
                live = jnp.where(at + j < end, live_ref[at + j], 0)
                piece = jnp.where(token < live, score[j * PAGE : (j + 1) * PAGE] * scale, MASKED)
                scores[g, j * PAGE : (j + 1) * PAGE, :] = piece
                top = jnp.maximum(top, jnp.max(piece, axis=0, keepdims=True))
            return top

        top = lax.fori_loop(
            0, groups, score_step, jnp.full((1, query_ref.shape[1]), MASKED, jnp.float32)
        )
        total[...] = jnp.zeros_like(total)

        def sum_step(g, denom):
            at = begin + g * GROUP
            expo = jnp.exp(scores[g] - top).astype(jnp.bfloat16)
            rows = keys[pl.ds(at, GROUP), :, 0:width].reshape(GROUP * PAGE, width)
            total[...] += lax.dot_general(
                expo, rows, (((0,), (0,)), ((), ())), preferred_element_type=jnp.float32
            )
            return denom + jnp.sum(expo.astype(jnp.float32), axis=0, keepdims=True)

        denom = lax.fori_loop(0, groups, sum_step, jnp.zeros_like(top))
        part_ref[r] = total[...].astype(part_ref.dtype)
        stat_ref[r] = jnp.where(line == 0, top, jnp.where(line == 1, denom, 0.0))


def columns(lines):
    line = lax.broadcasted_iota(jnp.int32, (128, 128), 0)
    table = jnp.zeros((128, 128), jnp.float32)
    for i, one in enumerate(lines):
        table = jnp.where(line == i, one, table)
    return table.T


def reduce_kernel(
    nrh, ncg, heads, part_ref, stat_ref, weights_ref, out_ref,
    core_part, core_stat, y_send, y_stat, y_part, y_stat_in, own, own_stat,
    row_send, row_stat, row_part, row_stat_in, mix, lines, value, send, recv, row_sem_s, row_sem_r,
):
    rh, rl, cg, yl, core = place(nrh)
    nrow = 2 * nrh
    spots = nrow * ncg
    q = yl * 2 + core
    c_peer = device(rh, rl, cg, yl, 1 - core)
    y_peer = device(rh, rl, cg, 1 - yl, core)
    d_peer = device(rh, rl, cg, 1 - yl, 1 - core)
    me = (rl * nrh + rh) * ncg + cg

    def spot(i):
        place_i = i // ncg
        return device(place_i % nrh, place_i // nrh, i % ncg, yl, core)

    barrier = pltpu.get_barrier_semaphore()
    for peer in (c_peer, y_peer, d_peer):
        pl.semaphore_signal(barrier, inc=1, device_id=peer, device_id_type=MESH)

    def hello(d, carry):
        pl.semaphore_signal(
            barrier, inc=1, device_id=spot((me + d) % spots), device_id_type=MESH
        )
        return carry

    lax.fori_loop(1, spots, hello, 0)
    pl.semaphore_wait(barrier, spots + 2)

    def remote(src, dst, slot, peer):
        return pltpu.make_async_remote_copy(
            src_ref=src, dst_ref=dst, send_sem=send.at[slot], recv_sem=recv.at[slot],
            device_id=peer, device_id_type=MESH,
        )

    started = []

    def push(*args):
        one = remote(*args)
        one.start()
        started.append(one)
        return one

    def block_of(y, c):
        return pl.ds(2 * (2 * y + c), 2)

    stat_in = push(stat_ref, core_stat, 0, c_peer)
    core_in = [
        push(part_ref.at[block_of(1 - yl, 1 - core)], core_part.at[0], 1, c_peer),
        push(part_ref.at[block_of(yl, 1 - core)], core_part.at[1], 2, c_peer),
    ]
    line = lax.broadcasted_iota(jnp.int32, (8, 128), 0)

    def merge_stats(first, second):
        top = jnp.maximum(first[0:1], second[0:1])
        one, two = jnp.exp(first[0:1] - top), jnp.exp(second[0:1] - top)
        denom = one * first[1:2] + two * second[1:2]
        return jnp.where(line == 0, top, jnp.where(line == 1, denom, 0.0)), columns((one, two))

    def merge_chunk(i, place_k, first, second):
        weight = mix[i, pl.ds(place_k * heads, heads), :]
        return weight[:, 0:1] * first.astype(jnp.float32) + weight[:, 1:2] * second.astype(
            jnp.float32
        )

    stat_in.wait_recv()
    for side in range(2):
        y = 1 - yl if side == 0 else yl
        stats = y_stat if side == 0 else own_stat
        for i in range(2):
            r = 2 * (2 * y + core) + i
            stats[i], mix[i] = merge_stats(stat_ref[r], core_stat[r])
        if side == 0:
            push(y_stat, y_stat_in, 3, y_peer)
        core_in[side].wait_recv()
        for a in range(2):
            for k in range(nrh):
                for i in range(2):
                    r = 2 * (2 * y + core) + i
                    merged = merge_chunk(
                        i, a * nrh + k, part_ref[r, a, k], core_part[side, i, a, k]
                    )
                    if side == 0:
                        y_send[a, k, i] = merged.astype(y_send.dtype)
                    else:
                        own[a, k, i] = merged
                if side == 0:
                    push(y_send.at[a, k], y_part.at[a, k], 4 + a * nrh + k, y_peer)

    remote(y_stat, y_stat_in, 3, y_peer).wait_recv()
    for i in range(2):
        row_stat[i], mix[i] = merge_stats(own_stat[i], y_stat_in[i])

    def row_copies(to, source, d):
        return (
            pltpu.make_async_remote_copy(
                src_ref=row_send.at[to // ncg], dst_ref=row_part.at[source],
                send_sem=row_sem_s.at[0, d], recv_sem=row_sem_r.at[0, source],
                device_id=spot(to), device_id_type=MESH,
            ),
            pltpu.make_async_remote_copy(
                src_ref=row_stat, dst_ref=row_stat_in.at[source],
                send_sem=row_sem_s.at[1, d], recv_sem=row_sem_r.at[1, source],
                device_id=spot(to), device_id_type=MESH,
            ),
        )

    def send_stat(d, carry):
        row_copies((me + d) % spots, me, d)[1].start()
        return carry

    lax.fori_loop(1, spots, send_stat, 0)
    row_stat_in[me] = row_stat[...]

    def chunk_step(place_k):
        a, k = place_k // nrh, place_k % nrh
        remote(y_send.at[a, k], y_part.at[a, k], 4 + place_k, y_peer).wait_recv()
        for i in range(2):
            row_send[place_k, i] = merge_chunk(
                i, place_k, own[a, k, i], y_part[a, k, i]
            ).astype(row_send.dtype)

    for place_k in range(nrow):
        chunk_step(place_k)

        def send_chunk(g, carry):
            to = place_k * ncg + g

            @pl.when(to != me)
            def _():
                row_copies(to, me, (to - me + spots) % spots)[0].start()

            return carry

        lax.fori_loop(0, ncg, send_chunk, 0)
    row_part[me] = row_send[me // ncg]

    def take_stat(d, carry):
        row_copies(me, (me + d) % spots, d)[1].wait_recv()
        return carry

    lax.fori_loop(1, spots, take_stat, 0)
    my_heads = pl.ds(pl.multiple_of((rl * nrh + rh) * heads, heads), heads)

    def top_step(s, tops):
        new = []
        for i in range(2):
            new.append(jnp.maximum(tops[i], row_stat_in[s, i][0:1]))
        return tuple(new)

    tops = lax.fori_loop(0, spots, top_step, (jnp.full((1, 128), MASKED, jnp.float32),) * 2)

    def denom_step(s, denoms):
        return tuple(
            denoms[i] + jnp.exp(row_stat_in[s, i][0:1] - tops[i]) * row_stat_in[s, i][1:2]
            for i in range(2)
        )

    denoms = lax.fori_loop(0, spots, denom_step, (jnp.zeros((1, 128), jnp.float32),) * 2)
    per = 64
    for i in range(2):
        lines[0, i] = columns((denoms[i],))

    def weight_step(s, carry):
        for i in range(2):
            lines[1 + s, i] = columns((jnp.exp(row_stat_in[s, i][0:1] - tops[i]),))
        return carry

    lax.fori_loop(0, spots, weight_step, 0)

    def take_part(d, carry):
        row_copies(me, (me + d) % spots, d)[0].wait_recv()
        return carry

    lax.fori_loop(1, spots, take_part, 0)

    def sum_step(s, sums):
        return tuple(
            sums[i]
            + lines[1 + s, i, my_heads, :][:, 0:1] * row_part[s, i].astype(jnp.float32)
            for i in range(2)
        )

    width = row_part.shape[-1]
    sums = lax.fori_loop(0, spots, sum_step, (jnp.zeros((heads, width), jnp.float32),) * 2)
    for i in range(2):
        value[i * heads : (i + 1) * heads, :] = sums[i] / lines[0, i, my_heads, :][:, 0:1]
    rows = value[...].astype(jnp.bfloat16)

    out_ref[q] = head_diagonal(rows, weights_ref, heads)
    base = 4 + nrow
    outs = ((c_peer, yl * 2 + 1 - core), (y_peer, (1 - yl) * 2 + core),
            (d_peer, (1 - yl) * 2 + 1 - core))
    for n, (peer, _) in enumerate(outs):
        push(out_ref.at[q], out_ref.at[q], base + n, peer)
    for n, (peer, owner) in enumerate(outs):
        remote(out_ref.at[owner], out_ref.at[owner], base + n, peer).wait_recv()
    for one in started:
        one.wait_send()

    def drain(d, carry):
        for one in row_copies((me + d) % spots, me, d):
            one.wait_send()
        return carry

    lax.fori_loop(1, spots, drain, 0)


def page_lists(page_table, lengths, device_at, slots):
    requests, pages = page_table.shape
    slot = jnp.arange(slots, dtype=jnp.int32)
    page = jnp.arange(pages, dtype=jnp.int32)
    matches = (page_table - device_at * slots)[:, :, None] == slot[None, None, :]
    left = jnp.clip(lengths[:, None] - page[None, :] * PAGE, 0, PAGE)
    live = jnp.sum(jnp.where(matches, left[:, :, None], 0), axis=(0, 1))
    owner = jnp.sum(
        jnp.where(matches, (jnp.arange(requests, dtype=jnp.int32) - requests)[:, None, None], 0),
        axis=(0, 1),
    ) + requests
    ahead = (owner[None, :] < owner[:, None]) | (
        (owner[None, :] == owner[:, None]) & (slot[None, :] < slot[:, None])
    )
    rank = jnp.sum(ahead.astype(jnp.int32), axis=1)
    hit = rank[None, :] == slot[:, None]
    order = jnp.sum(jnp.where(hit, slot[None, :], 0), axis=1)
    live_sorted = jnp.sum(jnp.where(hit, live[None, :], 0), axis=1)
    first = jnp.sum(
        (owner[None, :] < jnp.arange(requests + 1, dtype=jnp.int32)[:, None]).astype(jnp.int32),
        axis=1,
    )
    return order, jnp.pad(live_sorted, (0, GROUP)), first


def local(
    query_nope, query_rope, key_up_weight, value_up_weight, latent_cache, lengths, page_table
):
    scale = float(HEAD_NOPE_WIDTH + ROTARY_WIDTH) ** (-0.5)
    requests, heads, nope = query_nope.shape
    width = key_up_weight.shape[2]
    full = latent_cache.shape[1]
    nrow, ncol = lax.axis_size("row"), lax.axis_size("col")
    nrh, ncg = nrow // 2, ncol // 4
    all_heads = nrow * heads
    slots = latent_cache.shape[0] // PAGE
    wire = jnp.bfloat16 if heads % 16 == 0 else jnp.float32
    vmem = pl.BlockSpec(memory_space=pltpu.VMEM)

    device_at = lax.axis_index("row") * ncol + lax.axis_index("col")
    order, live, first = page_lists(page_table, lengths, device_at, slots)

    queries = pl.pallas_call(
        functools.partial(gather_kernel, nrh, heads),
        out_shape=jax.ShapeDtypeStruct((requests, 2, nrh, heads, full), wire),
        in_specs=[vmem] * 3,
        out_specs=vmem,
        scratch_shapes=[pltpu.SemaphoreType.DMA((8 * nrh,)), pltpu.SemaphoreType.DMA((8 * nrh,))],
        compiler_params=pltpu.CompilerParams(
            collective_id=0, has_side_effects=True, vmem_limit_bytes=VMEM_LIMIT
        ),
        name="gather_queries",
    )(
        query_nope.astype(wire).reshape(requests * heads, nope),
        query_rope.astype(wire),
        key_up_weight,
    )
    queries = queries.reshape(requests, all_heads, full).astype(jnp.bfloat16)

    part, stat = pl.pallas_call(
        functools.partial(attend_kernel, scale),
        out_shape=(
            jax.ShapeDtypeStruct((requests, all_heads, width), wire),
            jax.ShapeDtypeStruct((requests, 8, all_heads), jnp.float32),
        ),
        in_specs=[pl.BlockSpec(memory_space=pltpu.SMEM)] * 3
        + [vmem, pl.BlockSpec(memory_space=pl.ANY)],
        out_specs=(vmem, vmem),
        scratch_shapes=[
            pltpu.VMEM((slots + GROUP, PAGE, full), jnp.bfloat16),
            pltpu.VMEM((slots // GROUP + 1, GROUP * PAGE, all_heads), jnp.float32),
            pltpu.VMEM((all_heads, width), jnp.float32),
            pltpu.SemaphoreType.DMA((slots,)),
        ],
        compiler_params=pltpu.CompilerParams(vmem_limit_bytes=VMEM_LIMIT),
        name="attend_pages",
    )(order, live, first, queries, latent_cache.reshape(slots, PAGE, full))

    spots = nrow * ncg
    f32 = jnp.float32
    shape = (2, nrh, 2, heads, width)
    values = pl.pallas_call(
        functools.partial(reduce_kernel, nrh, ncg, heads),
        out_shape=jax.ShapeDtypeStruct((4, 2 * heads, value_up_weight.shape[2]), f32),
        in_specs=[vmem] * 3,
        out_specs=vmem,
        scratch_shapes=[
            pltpu.VMEM((2, 2, 2, nrh, heads, width), wire),
            pltpu.VMEM((requests, 8, all_heads), f32),
            pltpu.VMEM(shape, wire),
            pltpu.VMEM((2, 8, all_heads), f32),
            pltpu.VMEM(shape, wire),
            pltpu.VMEM((2, 8, all_heads), f32),
            pltpu.VMEM(shape, f32),
            pltpu.VMEM((2, 8, all_heads), f32),
            pltpu.VMEM((nrow, 2, heads, width), wire),
            pltpu.VMEM((2, 8, all_heads), f32),
            pltpu.VMEM((spots, 2, heads, width), wire),
            pltpu.VMEM((spots, 2, 8, all_heads), f32),
            pltpu.VMEM((2, 128, 128), f32),
            pltpu.VMEM((spots + 1, 2, 128, 128), f32),
            pltpu.VMEM((2 * heads, width), f32),
            pltpu.SemaphoreType.DMA((7 + nrow,)),
            pltpu.SemaphoreType.DMA((7 + nrow,)),
            pltpu.SemaphoreType.DMA((2, spots)),
            pltpu.SemaphoreType.DMA((2, spots)),
        ],
        compiler_params=pltpu.CompilerParams(
            collective_id=1, has_side_effects=True, vmem_limit_bytes=VMEM_LIMIT
        ),
        name="reduce_parts",
    )(part.reshape(requests, 2, nrh, heads, width), stat, value_up_weight)
    return values.reshape(requests, heads * value_up_weight.shape[2]).astype(jnp.bfloat16)


def solution(mesh):
    placed = (
        P(None, "row", None),
        P(None, "row", None),
        P("row", None, None),
        P("row", None, None),
        P(("row", "col"), None),
        P(),
        P(),
    )
    return jax.shard_map(
        local, mesh=mesh, in_specs=placed, out_specs=P(None, "row"), check_vma=False
    )
```

```python
import functools

import jax
import jax.numpy as jnp
from jax import lax
from jax.experimental import pallas as pl
from jax.experimental.pallas import tpu as pltpu
from jax.sharding import PartitionSpec as P

HEAD_NOPE_WIDTH = 128
ROTARY_WIDTH = 64
PAGE = 64
GROUP = 4
PAIR = 2
BLOCK = 128
CACHE_LOADS = 4
MASKED = -1e30
MESH = pl.DeviceIdType.MESH
VMEM_LIMIT = 48 * 1024 * 1024


def place(nrh):
    row, col = lax.axis_index("row"), lax.axis_index("col")
    return row // 2, row % 2, col // 4, (col // 2) % 2, col % 2


def device(rh, rl, cg, yl, core):
    return (rh * 2 + rl, cg * 4 + yl * 2 + core)


def greet(peers):
    barrier = pltpu.get_barrier_semaphore()
    for peer in peers:
        pl.semaphore_signal(barrier, inc=1, device_id=peer, device_id_type=MESH)
    pl.semaphore_wait(barrier, len(peers))


def head_diagonal(rows, weights_ref, heads):
    count = rows.shape[0]
    head = lax.broadcasted_iota(jnp.int32, (count, weights_ref.shape[2]), 0) % heads
    total = jnp.zeros((count, weights_ref.shape[2]), jnp.float32)
    for h in range(heads):
        product = jnp.dot(rows, weights_ref[h], preferred_element_type=jnp.float32)
        total = jnp.where(head == h, product, total)
    return total


def gather_kernel(
    nrh, heads, nope_hbm, rope_hbm, weights_hbm, cache_hbm, out_ref, keys_ref,
    nope_ref, rope_ref, weights_ref, cache_ref, local_sem, send, recv,
):
    blocks = cache_hbm.shape[1] // BLOCK
    loads = [
        pltpu.make_async_copy(nope_hbm, nope_ref, local_sem.at[0]),
        pltpu.make_async_copy(rope_hbm, rope_ref, local_sem.at[1]),
        pltpu.make_async_copy(weights_hbm, weights_ref, local_sem.at[2]),
    ]
    span = cache_hbm.shape[1] // CACHE_LOADS
    cache_loads = [
        pltpu.make_async_copy(
            cache_hbm.at[:, pl.ds(j * span, span)], cache_ref.at[:, pl.ds(j * span, span)],
            local_sem.at[3 + j],
        )
        for j in range(CACHE_LOADS)
    ]
    for one in loads + cache_loads:
        one.start()
    turned = [0]

    def turn(count):
        for _ in range(count):
            b = turned[0]
            if b >= blocks:
                return
            if b * BLOCK % span == 0:
                cache_loads[b * BLOCK // span].wait()
            block = cache_ref[:, b * BLOCK : (b + 1) * BLOCK].T
            per = BLOCK // PAGE
            keys_ref[b * per : (b + 1) * per] = block.reshape(per, PAGE, block.shape[1])
            turned[0] += 1

    rh, rl, cg, yl, core = place(nrh)
    q = yl * 2 + core
    qy = (1 - yl) * 2 + core
    z_peer = lambda k: device(k, rl, cg, yl, core)
    x_peer = device(rh, 1 - rl, cg, yl, core)
    y_peer = device(rh, rl, cg, 1 - yl, core)
    c_peer = device(rh, rl, cg, yl, 1 - core)
    greet([z_peer((rh + d) % nrh) for d in range(1, nrh)] + [x_peer, y_peer, c_peer])

    for one in loads:
        one.wait()
    rows = nope_ref[pl.ds(pl.multiple_of(q * 2 * heads, 2 * heads), 2 * heads), :]
    latent = head_diagonal(rows.astype(jnp.bfloat16), weights_ref, heads)
    latent = latent.astype(jnp.bfloat16).astype(out_ref.dtype)
    width = weights_ref.shape[2]
    for i in range(2):
        out_ref[2 * q + i, rl, rh, :, 0:width] = latent[i * heads : (i + 1) * heads]
        out_ref[2 * q + i, rl, rh, :, width:] = rope_ref[2 * q + i]

    started = []

    def copy(a, k, b, slot, peer, send_slot=None):
        shard = out_ref.at[pl.ds(2 * b, 2), a, k]
        return pltpu.make_async_remote_copy(
            src_ref=shard,
            dst_ref=shard,
            send_sem=send.at[slot if send_slot is None else send_slot],
            recv_sem=recv.at[slot],
            device_id=peer,
            device_id_type=MESH,
        )

    def push(*args, **kw):
        one = copy(*args, **kw)
        one.start()
        started.append(one)

    def arrived(a, k, b, slot, peer):
        copy(a, k, b, slot, peer).wait_recv()

    Z, X, Y, D, C = 0, nrh, 2 * nrh, 3 * nrh, 4 * nrh
    half = nrh // 2

    def spread(k):
        push(rl, k, q, X + k, x_peer)
        push(rl, k, q, Y + k, y_peer)
        push(rl, k, q, C + k, c_peer)

    for d in range(1, nrh):
        push(rl, rh, q, Z + rh, z_peer((rh + d) % nrh), send_slot=Z + d)
    spread(rh)
    for d in range(1, nrh):
        k = (rh + d) % nrh
        turn(-(-blocks // (3 * nrh)))
        arrived(rl, k, q, Z + k, z_peer(k))
        spread(k)
    for k in range(nrh):
        turn(-(-blocks // (3 * nrh)))
        arrived(1 - rl, k, q, X + k, x_peer)
        if k >= half:
            push(1 - rl, k, q, D + k, y_peer)
        push(1 - rl, k, q, C + nrh + k, c_peer)
        arrived(rl, k, qy, Y + k, y_peer)
        if k < half:
            push(rl, k, qy, D + k, x_peer)
        push(rl, k, qy, C + 2 * nrh + k, c_peer)
    for k in range(nrh):
        turn(-(-blocks // (3 * nrh)))
        arrived(1 - rl, k, qy, D + k, x_peer if k < half else y_peer)
        push(1 - rl, k, qy, C + 3 * nrh + k, c_peer)
    turn(blocks)
    qc, qyc = yl * 2 + 1 - core, (1 - yl) * 2 + 1 - core
    for k in range(nrh):
        arrived(rl, k, qc, C + k, c_peer)
        arrived(1 - rl, k, qc, C + nrh + k, c_peer)
        arrived(rl, k, qyc, C + 2 * nrh + k, c_peer)
        arrived(1 - rl, k, qyc, C + 3 * nrh + k, c_peer)
    for one in started:
        one.wait_send()


def attend_kernel(
    scale, order_ref, live_ref, first_ref, query_ref, keys_ref, part_ref, stat_ref,
    scores, tops, denoms, total, owner, start,
):
    requests, heads, _ = query_ref.shape
    width = part_ref.shape[2]

    def list_request(r, count):
        begin, end = first_ref[r], first_ref[r + 1]
        groups = (end - begin + GROUP - 1) // GROUP

        def list_group(g, carry):
            owner[count + g] = r
            start[count + g] = begin + g * GROUP
            return carry

        lax.fori_loop(0, groups, list_group, 0)
        return count + groups

    count = lax.fori_loop(0, requests, list_request, 0)
    for i in range(PAIR - 1):
        owner[count + i] = requests
        start[count + i] = 0
    rounds = (count + PAIR - 1) // PAIR

    tops[...] = jnp.full(tops.shape, MASKED, jnp.float32)
    denoms[...] = jnp.zeros(denoms.shape, jnp.float32)
    total[...] = jnp.zeros(total.shape, jnp.float32)
    token = lax.broadcasted_iota(jnp.int32, (PAGE, heads), 0)

    def pages(at, columns_kept):
        return jnp.concatenate(
            [keys_ref[order_ref[at + j], :, 0:columns_kept] for j in range(GROUP)], axis=0
        )

    def score_round(n, carry):
        products = []
        for u in range(PAIR):
            g = n * PAIR + u
            products.append(
                lax.dot_general(
                    pages(start[g], keys_ref.shape[2]),
                    query_ref[lax.rem(owner[g], requests)],
                    (((1,), (1,)), ((), ())),
                    preferred_element_type=jnp.float32,
                )
            )
        for u in range(PAIR):
            g = n * PAIR + u
            at, r = start[g], owner[g]
            end = jnp.where(r < requests, first_ref[jnp.minimum(r, requests - 1) + 1], 0)
            top = tops[r]
            for j in range(GROUP):
                live = jnp.where(at + j < end, live_ref[at + j], 0)
                rows = slice(j * PAGE, (j + 1) * PAGE)
                piece = jnp.where(token < live, products[u][rows] * scale, MASKED)
                scores[g, rows, :] = piece
                top = jnp.maximum(top, jnp.max(piece, axis=0, keepdims=True))
            tops[r] = top
        return carry

    lax.fori_loop(0, rounds, score_round, 0)

    def sum_round(n, carry):
        products = []
        for u in range(PAIR):
            g = n * PAIR + u
            r = owner[g]
            expo = jnp.exp(scores[g] - tops[r][0:1]).astype(jnp.bfloat16)
            denoms[r] += jnp.sum(expo.astype(jnp.float32), axis=0, keepdims=True)
            products.append(
                lax.dot_general(
                    expo, pages(start[g], width), (((0,), (0,)), ((), ())),
                    preferred_element_type=jnp.float32,
                )
            )
        for u in range(PAIR):
            total[owner[n * PAIR + u]] += products[u]
        return carry

    lax.fori_loop(0, rounds, sum_round, 0)
    line = lax.broadcasted_iota(jnp.int32, stat_ref.shape[1:], 0)
    for r in range(requests):
        part_ref[r] = total[r].astype(part_ref.dtype)
        stat_ref[r] = jnp.where(line == 0, tops[r], jnp.where(line == 1, denoms[r], 0.0))


def columns(lines):
    line = lax.broadcasted_iota(jnp.int32, (128, 128), 0)
    table = jnp.zeros((128, 128), jnp.float32)
    for i, one in enumerate(lines):
        table = jnp.where(line == i, one, table)
    return table.T


def reduce_kernel(
    nrh, ncg, heads, part_ref, stat_ref, weights_ref, out_ref,
    core_part, core_stat, y_send, y_stat, y_part, y_stat_in, own, own_stat,
    row_send, row_stat, row_part, row_stat_in, mix, lines, value, send, recv, row_sem_s, row_sem_r,
):
    rh, rl, cg, yl, core = place(nrh)
    nrow = 2 * nrh
    spots = nrow * ncg
    q = yl * 2 + core
    c_peer = device(rh, rl, cg, yl, 1 - core)
    y_peer = device(rh, rl, cg, 1 - yl, core)
    d_peer = device(rh, rl, cg, 1 - yl, 1 - core)
    me = (rl * nrh + rh) * ncg + cg

    def spot(i):
        place_i = i // ncg
        return device(place_i % nrh, place_i // nrh, i % ncg, yl, core)

    barrier = pltpu.get_barrier_semaphore()
    for peer in (c_peer, y_peer, d_peer):
        pl.semaphore_signal(barrier, inc=1, device_id=peer, device_id_type=MESH)

    def hello(d, carry):
        pl.semaphore_signal(
            barrier, inc=1, device_id=spot((me + d) % spots), device_id_type=MESH
        )
        return carry

    lax.fori_loop(1, spots, hello, 0)
    pl.semaphore_wait(barrier, spots + 2)

    def remote(src, dst, slot, peer):
        return pltpu.make_async_remote_copy(
            src_ref=src, dst_ref=dst, send_sem=send.at[slot], recv_sem=recv.at[slot],
            device_id=peer, device_id_type=MESH,
        )

    started = []

    def push(*args):
        one = remote(*args)
        one.start()
        started.append(one)
        return one

    def block_of(y, c):
        return pl.ds(2 * (2 * y + c), 2)

    stat_in = push(stat_ref, core_stat, 0, c_peer)
    core_in = [
        push(part_ref.at[block_of(1 - yl, 1 - core)], core_part.at[0], 1, c_peer),
        push(part_ref.at[block_of(yl, 1 - core)], core_part.at[1], 2, c_peer),
    ]
    line = lax.broadcasted_iota(jnp.int32, (8, 128), 0)

    def merge_stats(first, second):
        top = jnp.maximum(first[0:1], second[0:1])
        one, two = jnp.exp(first[0:1] - top), jnp.exp(second[0:1] - top)
        denom = one * first[1:2] + two * second[1:2]
        return jnp.where(line == 0, top, jnp.where(line == 1, denom, 0.0)), columns((one, two))

    def merge_chunk(i, place_k, first, second):
        weight = mix[i, pl.ds(pl.multiple_of(place_k * heads, heads), heads), :]
        return weight[:, 0:1] * first.astype(jnp.float32) + weight[:, 1:2] * second.astype(
            jnp.float32
        )

    stat_in.wait_recv()
    for side in range(2):
        y = 1 - yl if side == 0 else yl
        stats = y_stat if side == 0 else own_stat
        for i in range(2):
            r = 2 * (2 * y + core) + i
            stats[i], mix[i] = merge_stats(stat_ref[r], core_stat[r])
        if side == 0:
            push(y_stat, y_stat_in, 3, y_peer)
        core_in[side].wait_recv()
        for d in range(1, nrow + 1):
            place_k = (rl * nrh + rh + d) % nrow
            a, k = place_k // nrh, place_k % nrh
            for i in range(2):
                r = 2 * (2 * y + core) + i
                merged = merge_chunk(i, place_k, part_ref[r, a, k], core_part[side, i, a, k])
                if side == 0:
                    y_send[a, k, i] = merged.astype(y_send.dtype)
                else:
                    own[a, k, i] = merged
            if side == 0:
                push(y_send.at[a, k], y_part.at[a, k], 3 + d, y_peer)

    remote(y_stat, y_stat_in, 3, y_peer).wait_recv()
    for i in range(2):
        row_stat[i], mix[i] = merge_stats(own_stat[i], y_stat_in[i])

    def row_copies(to, source, d):
        return (
            pltpu.make_async_remote_copy(
                src_ref=row_send.at[to // ncg], dst_ref=row_part.at[source],
                send_sem=row_sem_s.at[0, d], recv_sem=row_sem_r.at[0, source],
                device_id=spot(to), device_id_type=MESH,
            ),
            pltpu.make_async_remote_copy(
                src_ref=row_stat, dst_ref=row_stat_in.at[source],
                send_sem=row_sem_s.at[1, d], recv_sem=row_sem_r.at[1, source],
                device_id=spot(to), device_id_type=MESH,
            ),
        )

    def send_stat(d, carry):
        row_copies((me + d) % spots, me, d)[1].start()
        return carry

    lax.fori_loop(1, spots, send_stat, 0)
    row_stat_in[me] = row_stat[...]

    def chunk_step(place_k, d):
        a, k = place_k // nrh, place_k % nrh
        remote(y_send.at[a, k], y_part.at[a, k], 3 + d, y_peer).wait_recv()
        for i in range(2):
            row_send[place_k, i] = merge_chunk(
                i, place_k, own[a, k, i], y_part[a, k, i]
            ).astype(row_send.dtype)

    for d in range(1, nrow + 1):
        place_k = (rl * nrh + rh + d) % nrow
        chunk_step(place_k, d)

        def send_chunk(g, carry, place_k=place_k):
            to = place_k * ncg + g

            @pl.when(to != me)
            def _():
                row_copies(to, me, (to - me + spots) % spots)[0].start()

            return carry

        lax.fori_loop(0, ncg, send_chunk, 0)
    row_part[me] = row_send[me // ncg]

    def take_stat(d, carry):
        row_copies(me, (me + d) % spots, d)[1].wait_recv()
        return carry

    lax.fori_loop(1, spots, take_stat, 0)
    my_heads = pl.ds(pl.multiple_of((rl * nrh + rh) * heads, heads), heads)

    def top_step(s, tops):
        new = []
        for i in range(2):
            new.append(jnp.maximum(tops[i], row_stat_in[s, i][0:1]))
        return tuple(new)

    tops = lax.fori_loop(0, spots, top_step, (jnp.full((1, 128), MASKED, jnp.float32),) * 2)

    def denom_step(s, denoms):
        return tuple(
            denoms[i] + jnp.exp(row_stat_in[s, i][0:1] - tops[i]) * row_stat_in[s, i][1:2]
            for i in range(2)
        )

    denoms = lax.fori_loop(0, spots, denom_step, (jnp.zeros((1, 128), jnp.float32),) * 2)
    per = 64
    for i in range(2):
        lines[0, i] = columns((denoms[i],))

    def weight_step(s, carry):
        for i in range(2):
            lines[1 + s, i] = columns((jnp.exp(row_stat_in[s, i][0:1] - tops[i]),))
        return carry

    lax.fori_loop(0, spots, weight_step, 0)

    def take_part(d, carry):
        row_copies(me, (me + d) % spots, d)[0].wait_recv()
        return carry

    lax.fori_loop(1, spots, take_part, 0)

    def sum_step(s, sums):
        return tuple(
            sums[i]
            + lines[1 + s, i, my_heads, :][:, 0:1] * row_part[s, i].astype(jnp.float32)
            for i in range(2)
        )

    width = row_part.shape[-1]
    sums = lax.fori_loop(0, spots, sum_step, (jnp.zeros((heads, width), jnp.float32),) * 2)
    for i in range(2):
        value[i * heads : (i + 1) * heads, :] = sums[i] / lines[0, i, my_heads, :][:, 0:1]
    rows = value[...].astype(jnp.bfloat16)

    out_ref[q] = head_diagonal(rows, weights_ref, heads)
    base = 4 + nrow
    outs = ((c_peer, yl * 2 + 1 - core), (y_peer, (1 - yl) * 2 + core),
            (d_peer, (1 - yl) * 2 + 1 - core))
    for n, (peer, _) in enumerate(outs):
        push(out_ref.at[q], out_ref.at[q], base + n, peer)
    for n, (peer, owner) in enumerate(outs):
        remote(out_ref.at[owner], out_ref.at[owner], base + n, peer).wait_recv()
    for one in started:
        one.wait_send()

    def drain(d, carry):
        for one in row_copies((me + d) % spots, me, d):
            one.wait_send()
        return carry

    lax.fori_loop(1, spots, drain, 0)


def page_lists(page_table, lengths, device_at, slots):
    requests, pages = page_table.shape
    slot = jnp.arange(slots, dtype=jnp.int32)
    page = jnp.arange(pages, dtype=jnp.int32)
    matches = (page_table - device_at * slots)[:, :, None] == slot[None, None, :]
    left = jnp.clip(lengths[:, None] - page[None, :] * PAGE, 0, PAGE)
    live = jnp.sum(jnp.where(matches, left[:, :, None], 0), axis=(0, 1))
    owner = jnp.sum(
        jnp.where(matches, (jnp.arange(requests, dtype=jnp.int32) - requests)[:, None, None], 0),
        axis=(0, 1),
    ) + requests
    ahead = (owner[None, :] < owner[:, None]) | (
        (owner[None, :] == owner[:, None]) & (slot[None, :] < slot[:, None])
    )
    rank = jnp.sum(ahead.astype(jnp.int32), axis=1)
    hit = rank[None, :] == slot[:, None]
    order = jnp.sum(jnp.where(hit, slot[None, :], 0), axis=1)
    live_sorted = jnp.sum(jnp.where(hit, live[None, :], 0), axis=1)
    first = jnp.sum(
        (owner[None, :] < jnp.arange(requests + 1, dtype=jnp.int32)[:, None]).astype(jnp.int32),
        axis=1,
    )
    return jnp.pad(order, (0, GROUP)), jnp.pad(live_sorted, (0, GROUP)), first


def local(
    query_nope, query_rope, key_up_weight, value_up_weight, latent_cache, lengths, page_table
):
    scale = float(HEAD_NOPE_WIDTH + ROTARY_WIDTH) ** (-0.5)
    requests, heads, nope = query_nope.shape
    width = key_up_weight.shape[2]
    full = latent_cache.shape[1]
    nrow, ncol = lax.axis_size("row"), lax.axis_size("col")
    nrh, ncg = nrow // 2, ncol // 4
    all_heads = nrow * heads
    slots = latent_cache.shape[0] // PAGE
    wire = jnp.bfloat16 if heads % 16 == 0 else jnp.float32
    vmem = pl.BlockSpec(memory_space=pltpu.VMEM)

    device_at = lax.axis_index("row") * ncol + lax.axis_index("col")
    order, live, first = page_lists(page_table, lengths, device_at, slots)

    queries, keys = pl.pallas_call(
        functools.partial(gather_kernel, nrh, heads),
        out_shape=(
            jax.ShapeDtypeStruct((requests, 2, nrh, heads, full), wire),
            jax.ShapeDtypeStruct((slots, PAGE, full), jnp.bfloat16),
        ),
        in_specs=[pl.BlockSpec(memory_space=pltpu.HBM)] * 4,
        out_specs=(vmem, vmem),
        scratch_shapes=[
            pltpu.VMEM((requests * heads, nope), wire),
            pltpu.VMEM(query_rope.shape, wire),
            pltpu.VMEM(key_up_weight.shape, jnp.bfloat16),
            pltpu.VMEM((full, slots * PAGE), jnp.bfloat16),
            pltpu.SemaphoreType.DMA((3 + CACHE_LOADS,)),
            pltpu.SemaphoreType.DMA((8 * nrh,)), pltpu.SemaphoreType.DMA((8 * nrh,))],
        compiler_params=pltpu.CompilerParams(
            collective_id=0, has_side_effects=True, vmem_limit_bytes=VMEM_LIMIT
        ),
        name="gather_queries",
    )(
        query_nope.astype(wire).reshape(requests * heads, nope),
        query_rope.astype(wire),
        key_up_weight,
        latent_cache.T,
    )
    queries = queries.reshape(requests, all_heads, full).astype(jnp.bfloat16)

    most = slots // GROUP + requests + PAIR
    part, stat = pl.pallas_call(
        functools.partial(attend_kernel, scale),
        out_shape=(
            jax.ShapeDtypeStruct((requests, all_heads, width), wire),
            jax.ShapeDtypeStruct((requests, 8, all_heads), jnp.float32),
        ),
        in_specs=[pl.BlockSpec(memory_space=pltpu.SMEM)] * 3
        + [vmem, vmem],
        out_specs=(vmem, vmem),
        scratch_shapes=[
            pltpu.VMEM((most, GROUP * PAGE, all_heads), jnp.float32),
            pltpu.VMEM((requests + 1, 8, all_heads), jnp.float32),
            pltpu.VMEM((requests + 1, 8, all_heads), jnp.float32),
            pltpu.VMEM((requests + 1, all_heads, width), jnp.float32),
            pltpu.SMEM((most,), jnp.int32),
            pltpu.SMEM((most,), jnp.int32),
        ],
        compiler_params=pltpu.CompilerParams(vmem_limit_bytes=VMEM_LIMIT),
        name="attend_pages",
    )(order, live, first, queries, keys)

    spots = nrow * ncg
    f32 = jnp.float32
    shape = (2, nrh, 2, heads, width)
    values = pl.pallas_call(
        functools.partial(reduce_kernel, nrh, ncg, heads),
        out_shape=jax.ShapeDtypeStruct((4, 2 * heads, value_up_weight.shape[2]), f32),
        in_specs=[vmem] * 3,
        out_specs=vmem,
        scratch_shapes=[
            pltpu.VMEM((2, 2, 2, nrh, heads, width), wire),
            pltpu.VMEM((requests, 8, all_heads), f32),
            pltpu.VMEM(shape, wire),
            pltpu.VMEM((2, 8, all_heads), f32),
            pltpu.VMEM(shape, wire),
            pltpu.VMEM((2, 8, all_heads), f32),
            pltpu.VMEM(shape, f32),
            pltpu.VMEM((2, 8, all_heads), f32),
            pltpu.VMEM((nrow, 2, heads, width), wire),
            pltpu.VMEM((2, 8, all_heads), f32),
            pltpu.VMEM((spots, 2, heads, width), wire),
            pltpu.VMEM((spots, 2, 8, all_heads), f32),
            pltpu.VMEM((2, 128, 128), f32),
            pltpu.VMEM((spots + 1, 2, 128, 128), f32),
            pltpu.VMEM((2 * heads, width), f32),
            pltpu.SemaphoreType.DMA((7 + nrow,)),
            pltpu.SemaphoreType.DMA((7 + nrow,)),
            pltpu.SemaphoreType.DMA((2, spots)),
            pltpu.SemaphoreType.DMA((2, spots)),
        ],
        compiler_params=pltpu.CompilerParams(
            collective_id=1, has_side_effects=True, vmem_limit_bytes=VMEM_LIMIT
        ),
        name="reduce_parts",
    )(part.reshape(requests, 2, nrh, heads, width), stat, value_up_weight)
    return values.reshape(requests, heads * value_up_weight.shape[2]).astype(jnp.bfloat16)


def solution(mesh):
    placed = (
        P(None, "row", None),
        P(None, "row", None),
        P("row", None, None),
        P("row", None, None),
        P(("row", "col"), None),
        P(),
        P(),
    )
    return jax.shard_map(
        local, mesh=mesh, in_specs=placed, out_specs=P(None, "row"), check_vma=False
    )
```

```python
import functools

import jax
import jax.numpy as jnp
from jax import lax
from jax.experimental import pallas as pl
from jax.experimental.pallas import tpu as pltpu
from jax.sharding import PartitionSpec as P

HEAD_NOPE_WIDTH = 128
ROTARY_WIDTH = 64
PAGE = 64
GROUP = 4
PAIR = 2
BLOCK = 128
CACHE_LOADS = 4
STORED = 4
MASKED = -1e30
MESH = pl.DeviceIdType.MESH
VMEM_LIMIT = 62 * 1024 * 1024


def place(nrh):
    row, col = lax.axis_index("row"), lax.axis_index("col")
    return row // 2, row % 2, col // 4, (col // 2) % 2, col % 2


def device(rh, rl, cg, yl, core):
    return (rh * 2 + rl, cg * 4 + yl * 2 + core)


def head_diagonal(rows, weights_ref, heads):
    count = rows.shape[0]
    head = lax.broadcasted_iota(jnp.int32, (count, weights_ref.shape[2]), 0) % heads
    total = jnp.zeros((count, weights_ref.shape[2]), jnp.float32)
    for h in range(heads):
        product = jnp.dot(rows, weights_ref[h], preferred_element_type=jnp.float32)
        total = jnp.where(head == h, product, total)
    return total


def list_pages(device_at, slots, length_ref, table_ref, meta_ref):
    requests, pages = table_ref.shape
    chunk = 128
    slot = lax.broadcasted_iota(jnp.int32, (slots, chunk), 0)
    owner = jnp.zeros((slots, chunk), jnp.int32)
    live = jnp.zeros((slots, chunk), jnp.int32)
    for r in range(requests):
        for c in range(pages // chunk):
            entry = table_ref[r : r + 1, c * chunk : (c + 1) * chunk] - device_at * slots
            page = lax.broadcasted_iota(jnp.int32, (1, chunk), 1) + c * chunk
            left = jnp.clip(length_ref[r] - page * PAGE, 0, PAGE)
            match = entry == slot
            owner += jnp.where(match, r - requests, 0)
            live += jnp.where(match, left, 0)
    f32 = jnp.float32
    owner = jnp.sum(owner.astype(f32), axis=1, keepdims=True) + float(requests)
    live = jnp.sum(live.astype(f32), axis=1, keepdims=True)
    line = lax.broadcasted_iota(jnp.int32, (128, 128), 0).astype(f32)
    lane = lax.broadcasted_iota(jnp.int32, (128, 128), 1).astype(f32)
    spare = 128 - slots

    def fill(column, last):
        wide = jnp.broadcast_to(column, (slots, 128))
        return jnp.concatenate([wide, jnp.full((spare, 128), last, f32)], axis=0)

    down = fill(owner, float(requests + 1))
    across = down.T
    ahead = (down < across) | ((down == across) & (line < lane))
    rank = jnp.sum(jnp.where(ahead, 1.0, 0.0), axis=0, keepdims=True)
    hit = rank == line
    index = jnp.where(lane < float(slots), lane, 0.0)
    order = jnp.sum(jnp.where(hit, index, 0.0), axis=1, keepdims=True)
    sorted_live = jnp.sum(jnp.where(hit, fill(live, 0.0).T, 0.0), axis=1, keepdims=True)
    first = jnp.sum(jnp.where(down < lane, 1.0, 0.0), axis=0, keepdims=True)
    both = jnp.where(lane == 0.0, order, jnp.where(lane == 1.0, sorted_live, 0.0)).T
    rows = jnp.where(line[0:8] == 2.0, first, both[0:8])
    meta_ref[...] = rows.astype(jnp.int32)


def gather_kernel(
    nrh, heads, length_ref, nope_hbm, rope_hbm, weights_hbm, cache_hbm, table_hbm,
    query_hbm, keys_hbm, meta_ref,
    nope_ref, rope_ref, weights_ref, cache_ref, table_ref, out_ref, keys_ref,
    local_sem, store_sem, send, recv,
):
    rh, rl, cg, yl, core = place(nrh)
    q = yl * 2 + core
    qy = (1 - yl) * 2 + core
    z_peer = lambda k: device(k, rl, cg, yl, core)
    x_peer = device(rh, 1 - rl, cg, yl, core)
    y_peer = device(rh, rl, cg, 1 - yl, core)
    c_peer = device(rh, rl, cg, yl, 1 - core)
    barrier = pltpu.get_barrier_semaphore()
    peers = [z_peer((rh + d) % nrh) for d in range(1, nrh)] + [x_peer, y_peer, c_peer]
    for peer in peers:
        pl.semaphore_signal(barrier, inc=1, device_id=peer, device_id_type=MESH)
    blocks = cache_hbm.shape[1] // BLOCK
    pages = BLOCK // PAGE
    loads = [
        pltpu.make_async_copy(nope_hbm, nope_ref, local_sem.at[0]),
        pltpu.make_async_copy(rope_hbm, rope_ref, local_sem.at[1]),
        pltpu.make_async_copy(weights_hbm, weights_ref, local_sem.at[2]),
    ]
    span = cache_hbm.shape[1] // CACHE_LOADS
    cache_loads = [
        pltpu.make_async_copy(
            cache_hbm.at[:, pl.ds(j * span, span)], cache_ref.at[:, pl.ds(j * span, span)],
            local_sem.at[3 + j],
        )
        for j in range(CACHE_LOADS)
    ]
    load_table = pltpu.make_async_copy(table_hbm, table_ref, local_sem.at[3 + CACHE_LOADS])
    for one in loads + [load_table] + cache_loads:
        one.start()
    stores = []

    def store(source, target):
        one = pltpu.make_async_copy(source, target, store_sem.at[len(stores)])
        one.start()
        stores.append(one)

    turned = [0]

    def turn(count):
        for _ in range(count):
            b = turned[0]
            if b >= blocks:
                return
            if b * BLOCK % span == 0:
                cache_loads[b * BLOCK // span].wait()
            block = cache_ref[:, b * BLOCK : (b + 1) * BLOCK].T
            keys_ref[b * pages : (b + 1) * pages] = block.reshape(pages, PAGE, block.shape[1])
            turned[0] += 1
            if turned[0] % STORED == 0:
                done = pl.ds((turned[0] - STORED) * pages, STORED * pages)
                store(keys_ref.at[done], keys_hbm.at[done])

    for one in loads:
        one.wait()
    rows = nope_ref[pl.ds(pl.multiple_of(q * 2 * heads, 2 * heads), 2 * heads), :]
    latent = head_diagonal(rows.astype(jnp.bfloat16), weights_ref, heads)
    latent = latent.astype(jnp.bfloat16).astype(out_ref.dtype)
    width = weights_ref.shape[2]
    for i in range(2):
        out_ref[2 * q + i, rl, rh, :, 0:width] = latent[i * heads : (i + 1) * heads]
        out_ref[2 * q + i, rl, rh, :, width:] = rope_ref[2 * q + i]
    pl.semaphore_wait(barrier, len(peers))

    started = []

    def copy(a, k, b, slot, peer, send_slot=None):
        shard = out_ref.at[pl.ds(2 * b, 2), a, k]
        return pltpu.make_async_remote_copy(
            src_ref=shard,
            dst_ref=shard,
            send_sem=send.at[slot if send_slot is None else send_slot],
            recv_sem=recv.at[slot],
            device_id=peer,
            device_id_type=MESH,
        )

    def push(*args, **kw):
        one = copy(*args, **kw)
        one.start()
        started.append(one)

    def arrived(a, k, b, slot, peer):
        copy(a, k, b, slot, peer).wait_recv()

    Z, X, Y, D, C = 0, nrh, 2 * nrh, 3 * nrh, 4 * nrh
    half = nrh // 2

    def spread(k):
        push(rl, k, q, X + k, x_peer)
        push(rl, k, q, Y + k, y_peer)
        push(rl, k, q, C + k, c_peer)

    for d in range(1, nrh):
        push(rl, rh, q, Z + rh, z_peer((rh + d) % nrh), send_slot=Z + d)
    spread(rh)
    load_table.wait()
    device_at = (rh * 2 + rl) * (lax.axis_size("col")) + cg * 4 + q
    list_pages(device_at, blocks * pages, length_ref, table_ref, meta_ref)
    for d in range(1, nrh):
        k = (rh + d) % nrh
        turn(-(-blocks // (3 * nrh)))
        arrived(rl, k, q, Z + k, z_peer(k))
        spread(k)
    for k in range(nrh):
        turn(-(-blocks // (3 * nrh)))
        arrived(1 - rl, k, q, X + k, x_peer)
        if k >= half:
            push(1 - rl, k, q, D + k, y_peer)
        push(1 - rl, k, q, C + nrh + k, c_peer)
        arrived(rl, k, qy, Y + k, y_peer)
        if k < half:
            push(rl, k, qy, D + k, x_peer)
        push(rl, k, qy, C + 2 * nrh + k, c_peer)
    for k in range(nrh):
        turn(-(-blocks // (3 * nrh)))
        arrived(1 - rl, k, qy, D + k, x_peer if k < half else y_peer)
        push(1 - rl, k, qy, C + 3 * nrh + k, c_peer)
    turn(blocks)
    for b in (q, qy):
        store(out_ref.at[pl.ds(2 * b, 2)], query_hbm.at[pl.ds(2 * b, 2)])
    qc, qyc = yl * 2 + 1 - core, (1 - yl) * 2 + 1 - core
    for k in range(nrh):
        arrived(rl, k, qc, C + k, c_peer)
        arrived(1 - rl, k, qc, C + nrh + k, c_peer)
        arrived(rl, k, qyc, C + 2 * nrh + k, c_peer)
        arrived(1 - rl, k, qyc, C + 3 * nrh + k, c_peer)
    for b in (qc, qyc):
        store(out_ref.at[pl.ds(2 * b, 2)], query_hbm.at[pl.ds(2 * b, 2)])
    for one in started:
        one.wait_send()
    for one in stores:
        one.wait()


def attend_kernel(
    scale, meta_ref, query_hbm, keys_hbm, part_hbm, stat_hbm,
    query_ref, keys_ref, part_ref, stat_ref, scores, tops, denoms, total, owner, start,
    query_sem, page_sem, out_sem,
):
    requests, heads, _ = query_ref.shape
    width = part_ref.shape[2]
    held = meta_ref[2, requests]

    def fetch(k):
        return pltpu.make_async_copy(
            keys_hbm.at[meta_ref[0, k]], keys_ref.at[k], page_sem.at[k]
        )

    def fetch_query(r):
        return pltpu.make_async_copy(query_hbm.at[r], query_ref.at[r], query_sem.at[r])

    def start_fetch(k, carry):
        fetch(k).start()
        return carry

    def end_fetch(k, carry):
        fetch(k).wait()
        return carry

    fetch_query(0).start()
    lax.fori_loop(0, jnp.minimum(held, 2 * GROUP), start_fetch, 0)
    for r in range(1, requests):
        fetch_query(r).start()
    lax.fori_loop(jnp.minimum(held, 2 * GROUP), held, start_fetch, 0)
    for i in range(GROUP):
        keys_ref[held + i] = jnp.zeros(keys_ref.shape[1:], keys_ref.dtype)

    def list_request(r, count):
        begin, end = meta_ref[2, r], meta_ref[2, r + 1]
        groups = (end - begin + GROUP - 1) // GROUP

        def list_group(g, carry):
            owner[count + g] = r
            start[count + g] = begin + g * GROUP
            return carry

        lax.fori_loop(0, groups, list_group, 0)
        return count + groups

    count = lax.fori_loop(0, requests, list_request, 0)
    for i in range(PAIR - 1):
        owner[count + i] = requests
        start[count + i] = 0
    rounds = (count + PAIR - 1) // PAIR

    tops[...] = jnp.full(tops.shape, MASKED, jnp.float32)
    denoms[...] = jnp.zeros(denoms.shape, jnp.float32)
    total[...] = jnp.zeros(total.shape, jnp.float32)
    token = lax.broadcasted_iota(jnp.int32, (PAGE, heads), 0)

    def pages(at, columns_kept):
        rows = keys_ref[pl.ds(at, GROUP), :, 0:columns_kept]
        return rows.reshape(GROUP * PAGE, columns_kept)

    for r in range(requests):
        fetch_query(r).wait()

    def score_round(n, here):
        need = jnp.maximum(start[n * PAIR], start[n * PAIR + PAIR - 1]) + GROUP
        need = jnp.maximum(jnp.minimum(need, held), here)
        lax.fori_loop(here, need, end_fetch, 0)
        products = []
        for u in range(PAIR):
            g = n * PAIR + u
            products.append(
                lax.dot_general(
                    pages(start[g], keys_ref.shape[2]),
                    query_ref[lax.rem(owner[g], requests)],
                    (((1,), (1,)), ((), ())),
                    preferred_element_type=jnp.float32,
                )
            )
        for u in range(PAIR):
            g = n * PAIR + u
            at, r = start[g], owner[g]
            end = jnp.where(r < requests, meta_ref[2, jnp.minimum(r, requests - 1) + 1], 0)
            top = tops[r]
            for j in range(GROUP):
                live = jnp.where(at + j < end, meta_ref[1, at + j], 0)
                rows = slice(j * PAGE, (j + 1) * PAGE)
                piece = jnp.where(token < live, products[u][rows] * scale, MASKED)
                scores[g, rows, :] = piece
                top = jnp.maximum(top, jnp.max(piece, axis=0, keepdims=True))
            tops[r] = top
        return need

    here = lax.fori_loop(0, rounds, score_round, 0)
    lax.fori_loop(here, held, end_fetch, 0)

    def sum_round(n, carry):
        products = []
        for u in range(PAIR):
            g = n * PAIR + u
            r = owner[g]
            expo = jnp.exp(scores[g] - tops[r][0:1]).astype(jnp.bfloat16)
            denoms[r] += jnp.sum(expo.astype(jnp.float32), axis=0, keepdims=True)
            products.append(
                lax.dot_general(
                    expo, pages(start[g], width), (((0,), (0,)), ((), ())),
                    preferred_element_type=jnp.float32,
                )
            )
        for u in range(PAIR):
            total[owner[n * PAIR + u]] += products[u]
        return carry

    lax.fori_loop(0, rounds, sum_round, 0)
    line = lax.broadcasted_iota(jnp.int32, stat_ref.shape[1:], 0)
    for r in range(requests):
        stat_ref[r] = jnp.where(line == 0, tops[r], jnp.where(line == 1, denoms[r], 0.0))
    outs = [pltpu.make_async_copy(stat_ref, stat_hbm, out_sem.at[requests])]
    outs[0].start()
    for r in range(requests):
        part_ref[r] = total[r].astype(part_ref.dtype)
        outs.append(pltpu.make_async_copy(part_ref.at[r], part_hbm.at[r], out_sem.at[r]))
        outs[-1].start()
    for one in outs:
        one.wait()


def columns(lines):
    line = lax.broadcasted_iota(jnp.int32, (128, 128), 0)
    table = jnp.zeros((128, 128), jnp.float32)
    for i, one in enumerate(lines):
        table = jnp.where(line == i, one, table)
    return table.T


def reduce_kernel(
    nrh, ncg, heads, part_hbm, stat_hbm, weights_hbm, out_ref,
    part_ref, stat_ref, weights_ref, load_sem, core_part, core_stat, y_send, y_stat, y_part, y_stat_in, own, own_stat,
    row_send, row_stat, row_part, row_stat_in, mix, lines, value, send, recv, row_sem_s, row_sem_r,
):
    rh, rl, cg, yl, core = place(nrh)
    nrow = 2 * nrh
    spots = nrow * ncg
    q = yl * 2 + core
    c_peer = device(rh, rl, cg, yl, 1 - core)
    y_peer = device(rh, rl, cg, 1 - yl, core)
    d_peer = device(rh, rl, cg, 1 - yl, 1 - core)
    me = (rl * nrh + rh) * ncg + cg

    def spot(i):
        place_i = i // ncg
        return device(place_i % nrh, place_i // nrh, i % ncg, yl, core)

    barrier = pltpu.get_barrier_semaphore()
    for peer in (c_peer, y_peer, d_peer):
        pl.semaphore_signal(barrier, inc=1, device_id=peer, device_id_type=MESH)

    def hello(d, carry):
        pl.semaphore_signal(
            barrier, inc=1, device_id=spot((me + d) % spots), device_id_type=MESH
        )
        return carry

    lax.fori_loop(1, spots, hello, 0)

    def block_of(y, c):
        return pl.ds(2 * (2 * y + c), 2)

    loads = [
        pltpu.make_async_copy(stat_hbm, stat_ref, load_sem.at[0]),
        pltpu.make_async_copy(part_hbm.at[block_of(1 - yl, core)], part_ref.at[0], load_sem.at[1]),
        pltpu.make_async_copy(part_hbm.at[block_of(yl, core)], part_ref.at[1], load_sem.at[2]),
        pltpu.make_async_copy(weights_hbm, weights_ref, load_sem.at[3]),
    ]
    for one in loads:
        one.start()
    pl.semaphore_wait(barrier, spots + 2)

    def remote(src, dst, slot, peer):
        return pltpu.make_async_remote_copy(
            src_ref=src, dst_ref=dst, send_sem=send.at[slot], recv_sem=recv.at[slot],
            device_id=peer, device_id_type=MESH,
        )

    started = []

    def push(*args):
        one = remote(*args)
        one.start()
        started.append(one)
        return one

    stat_in = push(stat_hbm, core_stat, 0, c_peer)
    core_in = [
        push(part_hbm.at[block_of(1 - yl, 1 - core)], core_part.at[0], 1, c_peer),
        push(part_hbm.at[block_of(yl, 1 - core)], core_part.at[1], 2, c_peer),
    ]
    line = lax.broadcasted_iota(jnp.int32, (8, 128), 0)

    def merge_stats(first, second):
        top = jnp.maximum(first[0:1], second[0:1])
        one, two = jnp.exp(first[0:1] - top), jnp.exp(second[0:1] - top)
        denom = one * first[1:2] + two * second[1:2]
        return jnp.where(line == 0, top, jnp.where(line == 1, denom, 0.0)), columns((one, two))

    def merge_chunk(i, place_k, first, second):
        weight = mix[i, pl.ds(pl.multiple_of(place_k * heads, heads), heads), :]
        return weight[:, 0:1] * first.astype(jnp.float32) + weight[:, 1:2] * second.astype(
            jnp.float32
        )

    for one in loads[:3]:
        one.wait()
    stat_in.wait_recv()
    for side in range(2):
        y = 1 - yl if side == 0 else yl
        stats = y_stat if side == 0 else own_stat
        for i in range(2):
            r = 2 * (2 * y + core) + i
            stats[i], mix[i] = merge_stats(stat_ref[r], core_stat[r])
        if side == 0:
            push(y_stat, y_stat_in, 3, y_peer)
        core_in[side].wait_recv()
        for d in range(1, nrow + 1):
            place_k = (rl * nrh + rh + d) % nrow
            a, k = place_k // nrh, place_k % nrh
            for i in range(2):
                merged = merge_chunk(i, place_k, part_ref[side, i, a, k], core_part[side, i, a, k])
                if side == 0:
                    y_send[a, k, i] = merged.astype(y_send.dtype)
                else:
                    own[a, k, i] = merged
            if side == 0:
                push(y_send.at[a, k], y_part.at[a, k], 3 + d, y_peer)

    remote(y_stat, y_stat_in, 3, y_peer).wait_recv()
    for i in range(2):
        row_stat[i], mix[i] = merge_stats(own_stat[i], y_stat_in[i])

    def row_copies(to, source, d):
        return (
            pltpu.make_async_remote_copy(
                src_ref=row_send.at[to // ncg], dst_ref=row_part.at[source],
                send_sem=row_sem_s.at[0, d], recv_sem=row_sem_r.at[0, source],
                device_id=spot(to), device_id_type=MESH,
            ),
            pltpu.make_async_remote_copy(
                src_ref=row_stat, dst_ref=row_stat_in.at[source],
                send_sem=row_sem_s.at[1, d], recv_sem=row_sem_r.at[1, source],
                device_id=spot(to), device_id_type=MESH,
            ),
        )

    def send_stat(d, carry):
        row_copies((me + d) % spots, me, d)[1].start()
        return carry

    lax.fori_loop(1, spots, send_stat, 0)
    row_stat_in[me] = row_stat[...]

    def chunk_step(place_k, d):
        a, k = place_k // nrh, place_k % nrh
        remote(y_send.at[a, k], y_part.at[a, k], 3 + d, y_peer).wait_recv()
        for i in range(2):
            row_send[place_k, i] = merge_chunk(
                i, place_k, own[a, k, i], y_part[a, k, i]
            ).astype(row_send.dtype)

    my_heads = pl.ds(pl.multiple_of((rl * nrh + rh) * heads, heads), heads)

    def weigh():
        def take_stat(d, carry):
            row_copies(me, (me + d) % spots, d)[1].wait_recv()
            return carry

        lax.fori_loop(1, spots, take_stat, 0)
        def top_step(s, tops):
            new = []
            for i in range(2):
                new.append(jnp.maximum(tops[i], row_stat_in[s, i][0:1]))
            return tuple(new)

        tops = lax.fori_loop(0, spots, top_step, (jnp.full((1, 128), MASKED, jnp.float32),) * 2)

        def denom_step(s, denoms):
            return tuple(
                denoms[i] + jnp.exp(row_stat_in[s, i][0:1] - tops[i]) * row_stat_in[s, i][1:2]
                for i in range(2)
            )

        denoms = lax.fori_loop(0, spots, denom_step, (jnp.zeros((1, 128), jnp.float32),) * 2)
        for i in range(2):
            lines[0, i] = columns((denoms[i],))

        def weight_step(s, carry):
            for i in range(2):
                lines[1 + s, i] = columns((jnp.exp(row_stat_in[s, i][0:1] - tops[i]),))
            return carry

        lax.fori_loop(0, spots, weight_step, 0)

    for d in range(1, nrow + 1):
        if d == max(nrow - 2, 1):
            weigh()
        place_k = (rl * nrh + rh + d) % nrow
        chunk_step(place_k, d)

        def send_chunk(g, carry, place_k=place_k):
            to = place_k * ncg + g

            @pl.when(to != me)
            def _():
                row_copies(to, me, (to - me + spots) % spots)[0].start()

            return carry

        lax.fori_loop(0, ncg, send_chunk, 0)
    row_part[me] = row_send[me // ncg]

    def take_part(d, carry):
        row_copies(me, (me + d) % spots, d)[0].wait_recv()
        return carry

    lax.fori_loop(1, spots, take_part, 0)

    def sum_step(s, sums):
        return tuple(
            sums[i]
            + lines[1 + s, i, my_heads, :][:, 0:1] * row_part[s, i].astype(jnp.float32)
            for i in range(2)
        )

    width = row_part.shape[-1]
    sums = lax.fori_loop(0, spots, sum_step, (jnp.zeros((heads, width), jnp.float32),) * 2)
    for i in range(2):
        value[i * heads : (i + 1) * heads, :] = sums[i] / lines[0, i, my_heads, :][:, 0:1]
    rows = value[...].astype(jnp.bfloat16)

    loads[3].wait()
    out_ref[q] = head_diagonal(rows, weights_ref, heads)
    base = 4 + nrow
    outs = ((c_peer, yl * 2 + 1 - core), (y_peer, (1 - yl) * 2 + core),
            (d_peer, (1 - yl) * 2 + 1 - core))
    for n, (peer, _) in enumerate(outs):
        push(out_ref.at[q], out_ref.at[q], base + n, peer)
    for n, (peer, owner) in enumerate(outs):
        remote(out_ref.at[owner], out_ref.at[owner], base + n, peer).wait_recv()
    for one in started:
        one.wait_send()

    def drain(d, carry):
        for one in row_copies((me + d) % spots, me, d):
            one.wait_send()
        return carry

    lax.fori_loop(1, spots, drain, 0)


def local(
    query_nope, query_rope, key_up_weight, value_up_weight, latent_cache, lengths, page_table
):
    scale = float(HEAD_NOPE_WIDTH + ROTARY_WIDTH) ** (-0.5)
    requests, heads, nope = query_nope.shape
    width = key_up_weight.shape[2]
    full = latent_cache.shape[1]
    nrow, ncol = lax.axis_size("row"), lax.axis_size("col")
    nrh, ncg = nrow // 2, ncol // 4
    all_heads = nrow * heads
    slots = latent_cache.shape[0] // PAGE
    wire = jnp.bfloat16 if heads % 16 == 0 else jnp.float32
    vmem = pl.BlockSpec(memory_space=pltpu.VMEM)
    smem = pl.BlockSpec(memory_space=pltpu.SMEM)
    hbm = pl.BlockSpec(memory_space=pl.ANY)

    queries, keys, meta = pl.pallas_call(
        functools.partial(gather_kernel, nrh, heads),
        out_shape=(
            jax.ShapeDtypeStruct((requests, 2, nrh, heads, full), wire),
            jax.ShapeDtypeStruct((slots, PAGE, full), jnp.bfloat16),
            jax.ShapeDtypeStruct((8, 128), jnp.int32),
        ),
        in_specs=[smem] + [hbm] * 5,
        out_specs=(hbm, hbm, vmem),
        scratch_shapes=[
            pltpu.VMEM((requests * heads, nope), wire),
            pltpu.VMEM(query_rope.shape, wire),
            pltpu.VMEM(key_up_weight.shape, jnp.bfloat16),
            pltpu.VMEM((full, slots * PAGE), jnp.bfloat16),
            pltpu.VMEM(page_table.shape, jnp.int32),
            pltpu.VMEM((requests, 2, nrh, heads, full), wire),
            pltpu.VMEM((slots, PAGE, full), jnp.bfloat16),
            pltpu.SemaphoreType.DMA((4 + CACHE_LOADS,)),
            pltpu.SemaphoreType.DMA((4 + slots * PAGE // (BLOCK * STORED),)),
            pltpu.SemaphoreType.DMA((8 * nrh,)), pltpu.SemaphoreType.DMA((8 * nrh,))],
        compiler_params=pltpu.CompilerParams(
            collective_id=0, has_side_effects=True, vmem_limit_bytes=VMEM_LIMIT
        ),
        name="gather_queries",
    )(
        lengths,
        query_nope.astype(wire).reshape(requests * heads, nope),
        query_rope.astype(wire),
        key_up_weight,
        latent_cache.T,
        page_table,
    )
    queries = queries.reshape(requests, all_heads, full).astype(jnp.bfloat16)

    most = slots // GROUP + requests + PAIR
    part, stat = pl.pallas_call(
        functools.partial(attend_kernel, scale),
        out_shape=(
            jax.ShapeDtypeStruct((requests, all_heads, width), wire),
            jax.ShapeDtypeStruct((requests, 8, all_heads), jnp.float32),
        ),
        in_specs=[smem, hbm, hbm],
        out_specs=(hbm, hbm),
        scratch_shapes=[
            pltpu.VMEM((requests, all_heads, full), jnp.bfloat16),
            pltpu.VMEM((slots + GROUP, PAGE, full), jnp.bfloat16),
            pltpu.VMEM((requests, all_heads, width), wire),
            pltpu.VMEM((requests, 8, all_heads), jnp.float32),
            pltpu.VMEM((most, GROUP * PAGE, all_heads), jnp.float32),
            pltpu.VMEM((requests + 1, 8, all_heads), jnp.float32),
            pltpu.VMEM((requests + 1, 8, all_heads), jnp.float32),
            pltpu.VMEM((requests + 1, all_heads, width), jnp.float32),
            pltpu.SMEM((most,), jnp.int32),
            pltpu.SMEM((most,), jnp.int32),
            pltpu.SemaphoreType.DMA((requests,)),
            pltpu.SemaphoreType.DMA((slots,)),
            pltpu.SemaphoreType.DMA((requests + 1,)),
        ],
        compiler_params=pltpu.CompilerParams(vmem_limit_bytes=VMEM_LIMIT),
        name="attend_pages",
    )(meta, queries, keys)

    spots = nrow * ncg
    f32 = jnp.float32
    shape = (2, nrh, 2, heads, width)
    values = pl.pallas_call(
        functools.partial(reduce_kernel, nrh, ncg, heads),
        out_shape=jax.ShapeDtypeStruct((4, 2 * heads, value_up_weight.shape[2]), f32),
        in_specs=[hbm] * 3,
        out_specs=vmem,
        scratch_shapes=[
            pltpu.VMEM((2, 2, 2, nrh, heads, width), wire),
            pltpu.VMEM((requests, 8, all_heads), f32),
            pltpu.VMEM(value_up_weight.shape, jnp.bfloat16),
            pltpu.SemaphoreType.DMA((4,)),
            pltpu.VMEM((2, 2, 2, nrh, heads, width), wire),
            pltpu.VMEM((requests, 8, all_heads), f32),
            pltpu.VMEM(shape, wire),
            pltpu.VMEM((2, 8, all_heads), f32),
            pltpu.VMEM(shape, wire),
            pltpu.VMEM((2, 8, all_heads), f32),
            pltpu.VMEM(shape, f32),
            pltpu.VMEM((2, 8, all_heads), f32),
            pltpu.VMEM((nrow, 2, heads, width), wire),
            pltpu.VMEM((2, 8, all_heads), f32),
            pltpu.VMEM((spots, 2, heads, width), wire),
            pltpu.VMEM((spots, 2, 8, all_heads), f32),
            pltpu.VMEM((2, 128, 128), f32),
            pltpu.VMEM((spots + 1, 2, 128, 128), f32),
            pltpu.VMEM((2 * heads, width), f32),
            pltpu.SemaphoreType.DMA((7 + nrow,)),
            pltpu.SemaphoreType.DMA((7 + nrow,)),
            pltpu.SemaphoreType.DMA((2, spots)),
            pltpu.SemaphoreType.DMA((2, spots)),
        ],
        compiler_params=pltpu.CompilerParams(
            collective_id=1, has_side_effects=True, vmem_limit_bytes=VMEM_LIMIT
        ),
        name="reduce_parts",
    )(part.reshape(requests, 2, nrh, heads, width), stat, value_up_weight)
    return values.reshape(requests, heads * value_up_weight.shape[2]).astype(jnp.bfloat16)


def solution(mesh):
    placed = (
        P(None, "row", None),
        P(None, "row", None),
        P("row", None, None),
        P("row", None, None),
        P(("row", "col"), None),
        P(),
        P(),
    )
    return jax.shard_map(
        local, mesh=mesh, in_specs=placed, out_specs=P(None, "row"), check_vma=False
    )
```

```python
import functools

import jax
import jax.numpy as jnp
from jax import lax
from jax.experimental import pallas as pl
from jax.experimental.pallas import tpu as pltpu
from jax.sharding import PartitionSpec as P

HEAD_NOPE_WIDTH = 128
ROTARY_WIDTH = 64
PAGE = 64
GROUP = 4
PAIR = 2
BLOCK = 128
CACHE_LOADS = 4
STORED = 4
MASKED = -1e30
MESH = pl.DeviceIdType.MESH
VMEM_LIMIT = 62 * 1024 * 1024


def place(nrh):
    row, col = lax.axis_index("row"), lax.axis_index("col")
    return row // 2, row % 2, col // 4, (col // 2) % 2, col % 2


def device(rh, rl, cg, yl, core):
    return (rh * 2 + rl, cg * 4 + yl * 2 + core)


def head_diagonal(rows, weights_ref, heads):
    count = rows.shape[0]
    head = lax.broadcasted_iota(jnp.int32, (count, weights_ref.shape[2]), 0) % heads
    total = jnp.zeros((count, weights_ref.shape[2]), jnp.float32)
    for h in range(heads):
        product = jnp.dot(rows, weights_ref[h], preferred_element_type=jnp.float32)
        total = jnp.where(head == h, product, total)
    return total


def list_pages(device_at, slots, length_ref, table_ref, meta_ref):
    requests, pages = table_ref.shape
    chunk = 128
    slot = lax.broadcasted_iota(jnp.int32, (slots, chunk), 0)
    owner = jnp.zeros((slots, chunk), jnp.int32)
    live = jnp.zeros((slots, chunk), jnp.int32)
    for r in range(requests):
        for c in range(pages // chunk):
            entry = table_ref[r : r + 1, c * chunk : (c + 1) * chunk] - device_at * slots
            page = lax.broadcasted_iota(jnp.int32, (1, chunk), 1) + c * chunk
            left = jnp.clip(length_ref[r] - page * PAGE, 0, PAGE)
            match = entry == slot
            owner += jnp.where(match, r - requests, 0)
            live += jnp.where(match, left, 0)
    f32 = jnp.float32
    owner = jnp.sum(owner.astype(f32), axis=1, keepdims=True) + float(requests)
    live = jnp.sum(live.astype(f32), axis=1, keepdims=True)
    line = lax.broadcasted_iota(jnp.int32, (128, 128), 0).astype(f32)
    lane = lax.broadcasted_iota(jnp.int32, (128, 128), 1).astype(f32)
    spare = 128 - slots

    def fill(column, last):
        wide = jnp.broadcast_to(column, (slots, 128))
        return jnp.concatenate([wide, jnp.full((spare, 128), last, f32)], axis=0)

    down = fill(owner, float(requests + 1))
    across = down.T
    ahead = (down < across) | ((down == across) & (line < lane))
    rank = jnp.sum(jnp.where(ahead, 1.0, 0.0), axis=0, keepdims=True)
    hit = rank == line
    index = jnp.where(lane < float(slots), lane, 0.0)
    order = jnp.sum(jnp.where(hit, index, 0.0), axis=1, keepdims=True)
    sorted_live = jnp.sum(jnp.where(hit, fill(live, 0.0).T, 0.0), axis=1, keepdims=True)
    first = jnp.sum(jnp.where(down < lane, 1.0, 0.0), axis=0, keepdims=True)
    both = jnp.where(lane == 0.0, order, jnp.where(lane == 1.0, sorted_live, 0.0)).T
    rows = jnp.where(line[0:8] == 2.0, first, both[0:8])
    meta_ref[...] = rows.astype(jnp.int32)


def gather_kernel(
    nrh, heads, length_ref, nope_hbm, rope_hbm, weights_hbm, cache_hbm, table_hbm,
    query_hbm, keys_hbm, meta_ref,
    nope_ref, rope_ref, weights_ref, cache_ref, table_ref, out_ref, keys_ref,
    local_sem, store_sem, send, recv,
):
    rh, rl, cg, yl, core = place(nrh)
    q = yl * 2 + core
    qy = (1 - yl) * 2 + core
    z_peer = lambda k: device(k, rl, cg, yl, core)
    x_peer = device(rh, 1 - rl, cg, yl, core)
    y_peer = device(rh, rl, cg, 1 - yl, core)
    c_peer = device(rh, rl, cg, yl, 1 - core)
    barrier = pltpu.get_barrier_semaphore()
    peers = [z_peer((rh + d) % nrh) for d in range(1, nrh)] + [x_peer, y_peer, c_peer]
    for peer in peers:
        pl.semaphore_signal(barrier, inc=1, device_id=peer, device_id_type=MESH)
    blocks = cache_hbm.shape[1] // BLOCK
    pages = BLOCK // PAGE
    loads = [
        pltpu.make_async_copy(nope_hbm, nope_ref, local_sem.at[0]),
        pltpu.make_async_copy(rope_hbm, rope_ref, local_sem.at[1]),
        pltpu.make_async_copy(weights_hbm, weights_ref, local_sem.at[2]),
    ]
    span = cache_hbm.shape[1] // CACHE_LOADS
    cache_loads = [
        pltpu.make_async_copy(
            cache_hbm.at[:, pl.ds(j * span, span)], cache_ref.at[:, pl.ds(j * span, span)],
            local_sem.at[3 + j],
        )
        for j in range(CACHE_LOADS)
    ]
    load_table = pltpu.make_async_copy(table_hbm, table_ref, local_sem.at[3 + CACHE_LOADS])
    for one in loads + [load_table]:
        one.start()
    stores = []

    def store(source, target):
        one = pltpu.make_async_copy(source, target, store_sem.at[len(stores)])
        one.start()
        stores.append(one)

    turned = [0]

    def turn(count):
        for _ in range(count):
            b = turned[0]
            if b >= blocks:
                return
            if b * BLOCK % span == 0:
                cache_loads[b * BLOCK // span].wait()
            block = cache_ref[:, b * BLOCK : (b + 1) * BLOCK].T
            keys_ref[b * pages : (b + 1) * pages] = block.reshape(pages, PAGE, block.shape[1])
            turned[0] += 1
            if turned[0] % STORED == 0:
                done = pl.ds((turned[0] - STORED) * pages, STORED * pages)
                store(keys_ref.at[done], keys_hbm.at[done])

    for one in loads:
        one.wait()
    for one in cache_loads:
        one.start()
    rows = nope_ref[pl.ds(pl.multiple_of(q * 2 * heads, 2 * heads), 2 * heads), :]
    latent = head_diagonal(rows.astype(jnp.bfloat16), weights_ref, heads)
    latent = latent.astype(jnp.bfloat16).astype(out_ref.dtype)
    width = weights_ref.shape[2]
    for i in range(2):
        out_ref[2 * q + i, rl, rh, :, 0:width] = latent[i * heads : (i + 1) * heads]
        out_ref[2 * q + i, rl, rh, :, width:] = rope_ref[2 * q + i]
    pl.semaphore_wait(barrier, len(peers))

    started = []

    def copy(a, k, b, slot, peer, send_slot=None):
        shard = out_ref.at[pl.ds(2 * b, 2), a, k]
        return pltpu.make_async_remote_copy(
            src_ref=shard,
            dst_ref=shard,
            send_sem=send.at[slot if send_slot is None else send_slot],
            recv_sem=recv.at[slot],
            device_id=peer,
            device_id_type=MESH,
        )

    def push(*args, **kw):
        one = copy(*args, **kw)
        one.start()
        started.append(one)

    def arrived(a, k, b, slot, peer):
        copy(a, k, b, slot, peer).wait_recv()

    Z, X, Y, D, C = 0, nrh, 2 * nrh, 3 * nrh, 4 * nrh
    half = nrh // 2

    def spread(k):
        push(rl, k, q, X + k, x_peer)
        push(rl, k, q, Y + k, y_peer)
        push(rl, k, q, C + k, c_peer)

    for d in range(1, nrh):
        push(rl, rh, q, Z + rh, z_peer((rh + d) % nrh), send_slot=Z + d)
    spread(rh)
    load_table.wait()
    device_at = (rh * 2 + rl) * (lax.axis_size("col")) + cg * 4 + q
    list_pages(device_at, blocks * pages, length_ref, table_ref, meta_ref)
    for d in range(1, nrh):
        k = (rh + d) % nrh
        turn(-(-blocks // (3 * nrh)))
        arrived(rl, k, q, Z + k, z_peer(k))
        spread(k)
    for k in range(nrh):
        turn(-(-blocks // (3 * nrh)))
        arrived(1 - rl, k, q, X + k, x_peer)
        if k >= half:
            push(1 - rl, k, q, D + k, y_peer)
        push(1 - rl, k, q, C + nrh + k, c_peer)
        arrived(rl, k, qy, Y + k, y_peer)
        if k < half:
            push(rl, k, qy, D + k, x_peer)
        push(rl, k, qy, C + 2 * nrh + k, c_peer)
    for k in range(nrh):
        turn(-(-blocks // (3 * nrh)))
        arrived(1 - rl, k, qy, D + k, x_peer if k < half else y_peer)
        push(1 - rl, k, qy, C + 3 * nrh + k, c_peer)
    turn(blocks)
    for b in (q, qy):
        store(out_ref.at[pl.ds(2 * b, 2)], query_hbm.at[pl.ds(2 * b, 2)])
    qc, qyc = yl * 2 + 1 - core, (1 - yl) * 2 + 1 - core
    for k in range(nrh):
        arrived(rl, k, qc, C + k, c_peer)
        arrived(1 - rl, k, qc, C + nrh + k, c_peer)
        arrived(rl, k, qyc, C + 2 * nrh + k, c_peer)
        arrived(1 - rl, k, qyc, C + 3 * nrh + k, c_peer)
    for b in (qc, qyc):
        store(out_ref.at[pl.ds(2 * b, 2)], query_hbm.at[pl.ds(2 * b, 2)])
    for one in started:
        one.wait_send()
    for one in stores:
        one.wait()


def attend_kernel(
    scale, meta_ref, query_hbm, keys_hbm, part_ref, stat_ref,
    query_ref, keys_ref, scores, tops, denoms, total, owner, start, query_sem, page_sem,
):
    requests, heads, _ = query_ref.shape
    width = part_ref.shape[2]
    held = meta_ref[2, requests]

    def fetch(k):
        return pltpu.make_async_copy(
            keys_hbm.at[meta_ref[0, k]], keys_ref.at[k], page_sem.at[k]
        )

    def fetch_query(r):
        return pltpu.make_async_copy(query_hbm.at[r], query_ref.at[r], query_sem.at[r])

    def start_fetch(k, carry):
        fetch(k).start()
        return carry

    def end_fetch(k, carry):
        fetch(k).wait()
        return carry

    fetch_query(0).start()
    lax.fori_loop(0, jnp.minimum(held, 2 * GROUP), start_fetch, 0)
    for r in range(1, requests):
        fetch_query(r).start()
    lax.fori_loop(jnp.minimum(held, 2 * GROUP), held, start_fetch, 0)
    for i in range(GROUP):
        keys_ref[held + i] = jnp.zeros(keys_ref.shape[1:], keys_ref.dtype)

    def list_request(r, count):
        begin, end = meta_ref[2, r], meta_ref[2, r + 1]
        groups = (end - begin + GROUP - 1) // GROUP

        def list_group(g, carry):
            owner[count + g] = r
            start[count + g] = begin + g * GROUP
            return carry

        lax.fori_loop(0, groups, list_group, 0)
        return count + groups

    count = lax.fori_loop(0, requests, list_request, 0)
    for i in range(PAIR - 1):
        owner[count + i] = requests
        start[count + i] = 0
    rounds = (count + PAIR - 1) // PAIR

    tops[...] = jnp.full(tops.shape, MASKED, jnp.float32)
    denoms[...] = jnp.zeros(denoms.shape, jnp.float32)
    total[...] = jnp.zeros(total.shape, jnp.float32)
    token = lax.broadcasted_iota(jnp.int32, (PAGE, heads), 0)

    def pages(at, columns_kept):
        rows = keys_ref[pl.ds(at, GROUP), :, 0:columns_kept]
        return rows.reshape(GROUP * PAGE, columns_kept)

    for r in range(requests):
        fetch_query(r).wait()

    def score_round(n, here):
        need = jnp.maximum(start[n * PAIR], start[n * PAIR + PAIR - 1]) + GROUP
        need = jnp.maximum(jnp.minimum(need, held), here)
        lax.fori_loop(here, need, end_fetch, 0)
        products = []
        for u in range(PAIR):
            g = n * PAIR + u
            products.append(
                lax.dot_general(
                    pages(start[g], keys_ref.shape[2]),
                    query_ref[lax.rem(owner[g], requests)],
                    (((1,), (1,)), ((), ())),
                    preferred_element_type=jnp.float32,
                )
            )
        for u in range(PAIR):
            g = n * PAIR + u
            at, r = start[g], owner[g]
            end = jnp.where(r < requests, meta_ref[2, jnp.minimum(r, requests - 1) + 1], 0)
            top = tops[r]
            for j in range(GROUP):
                live = jnp.where(at + j < end, meta_ref[1, at + j], 0)
                rows = slice(j * PAGE, (j + 1) * PAGE)
                piece = jnp.where(token < live, products[u][rows] * scale, MASKED)
                scores[g, rows, :] = piece
                top = jnp.maximum(top, jnp.max(piece, axis=0, keepdims=True))
            tops[r] = top
        return need

    here = lax.fori_loop(0, rounds, score_round, 0)
    lax.fori_loop(here, held, end_fetch, 0)

    def sum_round(n, carry):
        products = []
        for u in range(PAIR):
            g = n * PAIR + u
            r = owner[g]
            expo = jnp.exp(scores[g] - tops[r][0:1]).astype(jnp.bfloat16)
            denoms[r] += jnp.sum(expo.astype(jnp.float32), axis=0, keepdims=True)
            products.append(
                lax.dot_general(
                    expo, pages(start[g], width), (((0,), (0,)), ((), ())),
                    preferred_element_type=jnp.float32,
                )
            )
        for u in range(PAIR):
            total[owner[n * PAIR + u]] += products[u]
        return carry

    lax.fori_loop(0, rounds, sum_round, 0)
    line = lax.broadcasted_iota(jnp.int32, stat_ref.shape[1:], 0)
    for r in range(requests):
        stat_ref[r] = jnp.where(line == 0, tops[r], jnp.where(line == 1, denoms[r], 0.0))
        part_ref[r] = total[r].astype(part_ref.dtype)


def columns(lines):
    line = lax.broadcasted_iota(jnp.int32, (128, 128), 0)
    table = jnp.zeros((128, 128), jnp.float32)
    for i, one in enumerate(lines):
        table = jnp.where(line == i, one, table)
    return table.T


def reduce_kernel(
    nrh, ncg, heads, part_ref, stat_ref, weights_ref, out_ref, shared, core_part, core_stat, y_send, y_stat, y_part, y_stat_in, own, own_stat,
    row_send, row_stat, row_part, row_stat_in, mix, lines, value, send, recv, row_sem_s, row_sem_r,
):
    rh, rl, cg, yl, core = place(nrh)
    nrow = 2 * nrh
    spots = nrow * ncg
    q = yl * 2 + core
    c_peer = device(rh, rl, cg, yl, 1 - core)
    y_peer = device(rh, rl, cg, 1 - yl, core)
    d_peer = device(rh, rl, cg, 1 - yl, 1 - core)
    me = (rl * nrh + rh) * ncg + cg

    def spot(i):
        place_i = i // ncg
        return device(place_i % nrh, place_i // nrh, i % ncg, yl, core)

    barrier = pltpu.get_barrier_semaphore()
    for peer in (c_peer, y_peer, d_peer):
        pl.semaphore_signal(barrier, inc=1, device_id=peer, device_id_type=MESH)

    def hello(d, carry):
        pl.semaphore_signal(
            barrier, inc=1, device_id=spot((me + d) % spots), device_id_type=MESH
        )
        return carry

    lax.fori_loop(1, spots, hello, 0)

    def block_of(y, c):
        return pl.ds(2 * (2 * y + c), 2)

    pl.semaphore_wait(barrier, spots + 2)

    def remote(src, dst, slot, peer):
        return pltpu.make_async_remote_copy(
            src_ref=src, dst_ref=dst, send_sem=send.at[slot], recv_sem=recv.at[slot],
            device_id=peer, device_id_type=MESH,
        )

    started = []

    def push(*args):
        one = remote(*args)
        one.start()
        started.append(one)
        return one

    stat_in = push(stat_ref, core_stat, 0, c_peer)
    base = 4 + nrow
    core_in = []
    for d in range(1, nrow + 1):
        place_k = (rl * nrh + rh + d) % nrow
        a, k = place_k // nrh, place_k % nrh
        core_in.append(
            push(
                part_ref.at[block_of(1 - yl, 1 - core), a, k], core_part.at[0, :, a, k],
                base + 2 + d, c_peer,
            )
        )
    own_in = push(part_ref.at[block_of(yl, 1 - core)], core_part.at[1], 2, c_peer)
    line = lax.broadcasted_iota(jnp.int32, (8, 128), 0)

    def merge_stats(first, second):
        top = jnp.maximum(first[0:1], second[0:1])
        one, two = jnp.exp(first[0:1] - top), jnp.exp(second[0:1] - top)
        denom = one * first[1:2] + two * second[1:2]
        return jnp.where(line == 0, top, jnp.where(line == 1, denom, 0.0)), columns((one, two))

    def merge_chunk(i, place_k, first, second):
        weight = mix[i, pl.ds(pl.multiple_of(place_k * heads, heads), heads), :]
        return weight[:, 0:1] * first.astype(jnp.float32) + weight[:, 1:2] * second.astype(
            jnp.float32
        )

    stat_in.wait_recv()
    for side in range(2):
        y = 1 - yl if side == 0 else yl
        stats = y_stat if side == 0 else own_stat
        for i in range(2):
            r = 2 * (2 * y + core) + i
            stats[i], mix[i] = merge_stats(stat_ref[r], core_stat[r])
        if side == 0:
            push(y_stat, y_stat_in, 3, y_peer)
        if side == 1:
            own_in.wait_recv()
        for d in range(1, nrow + 1):
            place_k = (rl * nrh + rh + d) % nrow
            a, k = place_k // nrh, place_k % nrh
            if side == 0:
                core_in[d - 1].wait_recv()
            for i in range(2):
                r = 2 * (2 * y + core) + i
                merged = merge_chunk(i, place_k, part_ref[r, a, k], core_part[side, i, a, k])
                if side == 0:
                    y_send[a, k, i] = merged.astype(y_send.dtype)
                else:
                    own[a, k, i] = merged
            if side == 0:
                push(y_send.at[a, k], y_part.at[a, k], 3 + d, y_peer)

    remote(y_stat, y_stat_in, 3, y_peer).wait_recv()
    for i in range(2):
        row_stat[i], mix[i] = merge_stats(own_stat[i], y_stat_in[i])

    def row_copies(to, source, d):
        return (
            pltpu.make_async_remote_copy(
                src_ref=row_send.at[to // ncg], dst_ref=row_part.at[source],
                send_sem=row_sem_s.at[0, d], recv_sem=row_sem_r.at[0, source],
                device_id=spot(to), device_id_type=MESH,
            ),
            pltpu.make_async_remote_copy(
                src_ref=row_stat, dst_ref=row_stat_in.at[source],
                send_sem=row_sem_s.at[1, d], recv_sem=row_sem_r.at[1, source],
                device_id=spot(to), device_id_type=MESH,
            ),
        )

    def send_stat(d, carry):
        row_copies((me + d) % spots, me, d)[1].start()
        return carry

    lax.fori_loop(1, spots, send_stat, 0)
    row_stat_in[me] = row_stat[...]

    def chunk_step(place_k, d):
        a, k = place_k // nrh, place_k % nrh
        remote(y_send.at[a, k], y_part.at[a, k], 3 + d, y_peer).wait_recv()
        for i in range(2):
            row_send[place_k, i] = merge_chunk(
                i, place_k, own[a, k, i], y_part[a, k, i]
            ).astype(row_send.dtype)

    my_heads = pl.ds(pl.multiple_of((rl * nrh + rh) * heads, heads), heads)

    def weigh():
        def take_stat(d, carry):
            row_copies(me, (me + d) % spots, d)[1].wait_recv()
            return carry

        lax.fori_loop(1, spots, take_stat, 0)
        def top_step(s, tops):
            new = []
            for i in range(2):
                new.append(jnp.maximum(tops[i], row_stat_in[s, i][0:1]))
            return tuple(new)

        tops = lax.fori_loop(0, spots, top_step, (jnp.full((1, 128), MASKED, jnp.float32),) * 2)

        def denom_step(s, denoms):
            return tuple(
                denoms[i] + jnp.exp(row_stat_in[s, i][0:1] - tops[i]) * row_stat_in[s, i][1:2]
                for i in range(2)
            )

        denoms = lax.fori_loop(0, spots, denom_step, (jnp.zeros((1, 128), jnp.float32),) * 2)
        for i in range(2):
            lines[0, i] = columns((denoms[i],))

        def weight_step(s, carry):
            for i in range(2):
                lines[1 + s, i] = columns((jnp.exp(row_stat_in[s, i][0:1] - tops[i]),))
            return carry

        lax.fori_loop(0, spots, weight_step, 0)

    for d in range(1, nrow + 1):
        place_k = (rl * nrh + rh + d) % nrow
        chunk_step(place_k, d)

        def send_chunk(g, carry, place_k=place_k):
            to = place_k * ncg + g

            @pl.when(to != me)
            def _():
                row_copies(to, me, (to - me + spots) % spots)[0].start()

            return carry

        lax.fori_loop(0, ncg, send_chunk, 0)
    row_part[me] = row_send[me // ncg]

    weigh()

    def take_part(d, carry):
        row_copies(me, (me + d) % spots, d)[0].wait_recv()
        return carry

    lax.fori_loop(1, spots, take_part, 0)

    def sum_step(s, sums):
        return tuple(
            sums[i]
            + lines[1 + s, i, my_heads, :][:, 0:1] * row_part[s, i].astype(jnp.float32)
            for i in range(2)
        )

    width = row_part.shape[-1]
    sums = lax.fori_loop(0, spots, sum_step, (jnp.zeros((heads, width), jnp.float32),) * 2)
    for i in range(2):
        value[i * heads : (i + 1) * heads, :] = sums[i] / lines[0, i, my_heads, :][:, 0:1]
    rows = value[...].astype(jnp.bfloat16)

    shared[q] = head_diagonal(rows, weights_ref, heads).reshape(2, heads, shared.shape[3])
    outs = ((c_peer, yl * 2 + 1 - core), (y_peer, (1 - yl) * 2 + core),
            (d_peer, (1 - yl) * 2 + 1 - core))
    for n, (peer, _) in enumerate(outs):
        push(shared.at[q], shared.at[q], base + n, peer)
    for n, (peer, owner) in enumerate(outs):
        remote(shared.at[owner], shared.at[owner], base + n, peer).wait_recv()
    size = shared.shape[3]
    for h in range(heads):
        block = shared[:, :, h, :].reshape(8, size)
        out_ref[:, h * size : (h + 1) * size] = block.astype(out_ref.dtype)
    for one in started:
        one.wait_send()

    def drain(d, carry):
        for one in row_copies((me + d) % spots, me, d):
            one.wait_send()
        return carry

    lax.fori_loop(1, spots, drain, 0)


def local(
    query_nope, query_rope, key_up_weight, value_up_weight, latent_cache, lengths, page_table
):
    scale = float(HEAD_NOPE_WIDTH + ROTARY_WIDTH) ** (-0.5)
    requests, heads, nope = query_nope.shape
    width = key_up_weight.shape[2]
    full = latent_cache.shape[1]
    nrow, ncol = lax.axis_size("row"), lax.axis_size("col")
    nrh, ncg = nrow // 2, ncol // 4
    all_heads = nrow * heads
    slots = latent_cache.shape[0] // PAGE
    wire = jnp.bfloat16 if heads % 16 == 0 else jnp.float32
    vmem = pl.BlockSpec(memory_space=pltpu.VMEM)
    smem = pl.BlockSpec(memory_space=pltpu.SMEM)
    hbm = pl.BlockSpec(memory_space=pl.ANY)

    queries, keys, meta = pl.pallas_call(
        functools.partial(gather_kernel, nrh, heads),
        out_shape=(
            jax.ShapeDtypeStruct((requests, 2, nrh, heads, full), wire),
            jax.ShapeDtypeStruct((slots, PAGE, full), jnp.bfloat16),
            jax.ShapeDtypeStruct((8, 128), jnp.int32),
        ),
        in_specs=[smem] + [hbm] * 5,
        out_specs=(hbm, hbm, vmem),
        scratch_shapes=[
            pltpu.VMEM((requests * heads, nope), wire),
            pltpu.VMEM(query_rope.shape, wire),
            pltpu.VMEM(key_up_weight.shape, jnp.bfloat16),
            pltpu.VMEM((full, slots * PAGE), jnp.bfloat16),
            pltpu.VMEM(page_table.shape, jnp.int32),
            pltpu.VMEM((requests, 2, nrh, heads, full), wire),
            pltpu.VMEM((slots, PAGE, full), jnp.bfloat16),
            pltpu.SemaphoreType.DMA((4 + CACHE_LOADS,)),
            pltpu.SemaphoreType.DMA((4 + slots * PAGE // (BLOCK * STORED),)),
            pltpu.SemaphoreType.DMA((8 * nrh,)), pltpu.SemaphoreType.DMA((8 * nrh,))],
        compiler_params=pltpu.CompilerParams(
            collective_id=0, has_side_effects=True, vmem_limit_bytes=VMEM_LIMIT
        ),
        name="gather_queries",
    )(
        lengths,
        query_nope.astype(wire).reshape(requests * heads, nope),
        query_rope.astype(wire),
        key_up_weight,
        latent_cache.T,
        page_table,
    )
    queries = queries.reshape(requests, all_heads, full).astype(jnp.bfloat16)

    most = slots // GROUP + requests + PAIR
    part, stat = pl.pallas_call(
        functools.partial(attend_kernel, scale),
        out_shape=(
            jax.ShapeDtypeStruct((requests, all_heads, width), wire),
            jax.ShapeDtypeStruct((requests, 8, all_heads), jnp.float32),
        ),
        in_specs=[smem, hbm, hbm],
        out_specs=(vmem, vmem),
        scratch_shapes=[
            pltpu.VMEM((requests, all_heads, full), jnp.bfloat16),
            pltpu.VMEM((slots + GROUP, PAGE, full), jnp.bfloat16),
            pltpu.VMEM((most, GROUP * PAGE, all_heads), jnp.float32),
            pltpu.VMEM((requests + 1, 8, all_heads), jnp.float32),
            pltpu.VMEM((requests + 1, 8, all_heads), jnp.float32),
            pltpu.VMEM((requests + 1, all_heads, width), jnp.float32),
            pltpu.SMEM((most,), jnp.int32),
            pltpu.SMEM((most,), jnp.int32),
            pltpu.SemaphoreType.DMA((requests,)),
            pltpu.SemaphoreType.DMA((slots,)),
        ],
        compiler_params=pltpu.CompilerParams(vmem_limit_bytes=52 * 1024 * 1024),
        name="attend_pages",
    )(meta, queries, keys)

    spots = nrow * ncg
    f32 = jnp.float32
    shape = (2, nrh, 2, heads, width)
    values = pl.pallas_call(
        functools.partial(reduce_kernel, nrh, ncg, heads),
        out_shape=jax.ShapeDtypeStruct(
            (requests, heads * value_up_weight.shape[2]), jnp.bfloat16
        ),
        in_specs=[vmem] * 3,
        out_specs=vmem,
        scratch_shapes=[
            pltpu.VMEM((4, 2, heads, value_up_weight.shape[2]), f32),
            pltpu.VMEM((2, 2, 2, nrh, heads, width), wire),
            pltpu.VMEM((requests, 8, all_heads), f32),
            pltpu.VMEM(shape, wire),
            pltpu.VMEM((2, 8, all_heads), f32),
            pltpu.VMEM(shape, wire),
            pltpu.VMEM((2, 8, all_heads), f32),
            pltpu.VMEM(shape, f32),
            pltpu.VMEM((2, 8, all_heads), f32),
            pltpu.VMEM((nrow, 2, heads, width), wire),
            pltpu.VMEM((2, 8, all_heads), f32),
            pltpu.VMEM((spots, 2, heads, width), wire),
            pltpu.VMEM((spots, 2, 8, all_heads), f32),
            pltpu.VMEM((2, 128, 128), f32),
            pltpu.VMEM((spots + 1, 2, 128, 128), f32),
            pltpu.VMEM((2 * heads, width), f32),
            pltpu.SemaphoreType.DMA((7 + 2 * nrow,)),
            pltpu.SemaphoreType.DMA((7 + 2 * nrow,)),
            pltpu.SemaphoreType.DMA((2, spots)),
            pltpu.SemaphoreType.DMA((2, spots)),
        ],
        compiler_params=pltpu.CompilerParams(
            collective_id=1, has_side_effects=True, vmem_limit_bytes=40 * 1024 * 1024
        ),
        name="reduce_parts",
    )(part.reshape(requests, 2, nrh, heads, width), stat, value_up_weight)
    return values


def solution(mesh):
    placed = (
        P(None, "row", None),
        P(None, "row", None),
        P("row", None, None),
        P("row", None, None),
        P(("row", "col"), None),
        P(),
        P(),
    )
    return jax.shard_map(
        local, mesh=mesh, in_specs=placed, out_specs=P(None, "row"), check_vma=False
    )
```

```python
import functools

import jax
import jax.numpy as jnp
from jax import lax
from jax.experimental import pallas as pl
from jax.experimental.pallas import tpu as pltpu
from jax.sharding import PartitionSpec as P

HEAD_NOPE_WIDTH = 128
ROTARY_WIDTH = 64
PAGE = 64
GROUP = 4
PAIR = 2
BLOCK = 128
CACHE_LOADS = 4
STORED = 4
MASKED = -1e30
MESH = pl.DeviceIdType.MESH
VMEM_LIMIT = 62 * 1024 * 1024


def place(nrh):
    row, col = lax.axis_index("row"), lax.axis_index("col")
    return row // 2, row % 2, col // 4, (col // 2) % 2, col % 2


def device(rh, rl, cg, yl, core):
    return (rh * 2 + rl, cg * 4 + yl * 2 + core)


def head_diagonal(rows, weights_ref, heads):
    count = rows.shape[0]
    head = lax.broadcasted_iota(jnp.int32, (count, weights_ref.shape[2]), 0) % heads
    total = jnp.zeros((count, weights_ref.shape[2]), jnp.float32)
    for h in range(heads):
        product = jnp.dot(rows, weights_ref[h], preferred_element_type=jnp.float32)
        total = jnp.where(head == h, product, total)
    return total


def list_pages(device_at, slots, length_ref, table_ref, meta_ref):
    requests, pages = table_ref.shape
    chunk = 128
    slot = lax.broadcasted_iota(jnp.int32, (slots, chunk), 0)
    owner = jnp.zeros((slots, chunk), jnp.int32)
    live = jnp.zeros((slots, chunk), jnp.int32)
    for r in range(requests):
        for c in range(pages // chunk):
            entry = table_ref[r : r + 1, c * chunk : (c + 1) * chunk] - device_at * slots
            page = lax.broadcasted_iota(jnp.int32, (1, chunk), 1) + c * chunk
            left = jnp.clip(length_ref[r] - page * PAGE, 0, PAGE)
            match = entry == slot
            owner += jnp.where(match, r - requests, 0)
            live += jnp.where(match, left, 0)
    f32 = jnp.float32
    owner = jnp.sum(owner.astype(f32), axis=1, keepdims=True) + float(requests)
    live = jnp.sum(live.astype(f32), axis=1, keepdims=True)
    line = lax.broadcasted_iota(jnp.int32, (128, 128), 0).astype(f32)
    lane = lax.broadcasted_iota(jnp.int32, (128, 128), 1).astype(f32)
    spare = 128 - slots

    def fill(column, last):
        wide = jnp.broadcast_to(column, (slots, 128))
        return jnp.concatenate([wide, jnp.full((spare, 128), last, f32)], axis=0)

    down = fill(owner, float(requests + 1))
    across = down.T
    ahead = (down < across) | ((down == across) & (line < lane))
    rank = jnp.sum(jnp.where(ahead, 1.0, 0.0), axis=0, keepdims=True)
    hit = rank == line
    index = jnp.where(lane < float(slots), lane, 0.0)
    order = jnp.sum(jnp.where(hit, index, 0.0), axis=1, keepdims=True)
    sorted_live = jnp.sum(jnp.where(hit, fill(live, 0.0).T, 0.0), axis=1, keepdims=True)
    first = jnp.sum(jnp.where(down < lane, 1.0, 0.0), axis=0, keepdims=True)
    both = jnp.where(lane == 0.0, order, jnp.where(lane == 1.0, sorted_live, 0.0)).T
    rows = jnp.where(line[0:8] == 2.0, first, both[0:8])
    meta_ref[...] = rows.astype(jnp.int32)


def gather_kernel(
    nrh, heads, length_ref, nope_hbm, rope_hbm, weights_hbm, cache_hbm, table_hbm,
    query_hbm, keys_hbm, meta_ref,
    nope_ref, rope_ref, weights_ref, cache_ref, table_ref, out_ref, keys_ref,
    local_sem, store_sem, send, recv,
):
    rh, rl, cg, yl, core = place(nrh)
    q = yl * 2 + core
    qy = (1 - yl) * 2 + core
    z_peer = lambda k: device(k, rl, cg, yl, core)
    x_peer = device(rh, 1 - rl, cg, yl, core)
    y_peer = device(rh, rl, cg, 1 - yl, core)
    c_peer = device(rh, rl, cg, yl, 1 - core)
    barrier = pltpu.get_barrier_semaphore()
    peers = [z_peer((rh + d) % nrh) for d in range(1, nrh)] + [x_peer, y_peer, c_peer]
    for peer in peers:
        pl.semaphore_signal(barrier, inc=1, device_id=peer, device_id_type=MESH)
    blocks = cache_hbm.shape[1] // BLOCK
    pages = BLOCK // PAGE
    loads = [
        pltpu.make_async_copy(nope_hbm, nope_ref, local_sem.at[0]),
        pltpu.make_async_copy(rope_hbm, rope_ref, local_sem.at[1]),
        pltpu.make_async_copy(weights_hbm, weights_ref, local_sem.at[2]),
    ]
    span = cache_hbm.shape[1] // CACHE_LOADS
    cache_loads = [
        pltpu.make_async_copy(
            cache_hbm.at[:, pl.ds(j * span, span)], cache_ref.at[:, pl.ds(j * span, span)],
            local_sem.at[3 + j],
        )
        for j in range(CACHE_LOADS)
    ]
    load_table = pltpu.make_async_copy(table_hbm, table_ref, local_sem.at[3 + CACHE_LOADS])
    for one in loads + [load_table]:
        one.start()
    stores = []

    def store(source, target):
        one = pltpu.make_async_copy(source, target, store_sem.at[len(stores)])
        one.start()
        stores.append(one)

    turned = [0]

    def turn(count):
        for _ in range(count):
            b = turned[0]
            if b >= blocks:
                return
            if b * BLOCK % span == 0:
                cache_loads[b * BLOCK // span].wait()
            block = cache_ref[:, b * BLOCK : (b + 1) * BLOCK].T
            keys_ref[b * pages : (b + 1) * pages] = block.reshape(pages, PAGE, block.shape[1])
            turned[0] += 1
            if turned[0] % STORED == 0:
                done = pl.ds((turned[0] - STORED) * pages, STORED * pages)
                store(keys_ref.at[done], keys_hbm.at[done])

    for one in loads:
        one.wait()
    for one in cache_loads:
        one.start()
    rows = nope_ref[pl.ds(pl.multiple_of(q * 2 * heads, 2 * heads), 2 * heads), :]
    latent = head_diagonal(rows.astype(jnp.bfloat16), weights_ref, heads)
    latent = latent.astype(jnp.bfloat16).astype(out_ref.dtype)
    width = weights_ref.shape[2]
    for i in range(2):
        out_ref[2 * q + i, rl, rh, :, 0:width] = latent[i * heads : (i + 1) * heads]
        out_ref[2 * q + i, rl, rh, :, width:] = rope_ref[2 * q + i]
    pl.semaphore_wait(barrier, len(peers))

    started = []

    def copy(a, k, b, slot, peer, send_slot=None):
        shard = out_ref.at[pl.ds(2 * b, 2), a] if k is None else out_ref.at[pl.ds(2 * b, 2), a, k]
        return pltpu.make_async_remote_copy(
            src_ref=shard,
            dst_ref=shard,
            send_sem=send.at[slot if send_slot is None else send_slot],
            recv_sem=recv.at[slot],
            device_id=peer,
            device_id_type=MESH,
        )

    def push(*args, **kw):
        one = copy(*args, **kw)
        one.start()
        started.append(one)

    def arrived(a, k, b, slot, peer):
        copy(a, k, b, slot, peer).wait_recv()

    Z, X, Y, D, C = 0, nrh, 2 * nrh, 3 * nrh, 4 * nrh
    half = nrh // 2
    clump = -(-blocks // 4)

    def spread(k):
        push(rl, k, q, X + k, x_peer)
        push(rl, k, q, Y + k, y_peer)

    for d in range(1, nrh):
        push(rl, rh, q, Z + rh, z_peer((rh + d) % nrh), send_slot=Z + d)
    spread(rh)
    load_table.wait()
    device_at = (rh * 2 + rl) * (lax.axis_size("col")) + cg * 4 + q
    list_pages(device_at, blocks * pages, length_ref, table_ref, meta_ref)
    turn(clump)
    for d in range(1, nrh):
        k = (rh + d) % nrh
        arrived(rl, k, q, Z + k, z_peer(k))
        spread(k)
    push(rl, None, q, C, c_peer)
    turn(clump)
    for k in range(nrh):
        arrived(1 - rl, k, q, X + k, x_peer)
        if k >= half:
            push(1 - rl, k, q, D + k, y_peer)
        arrived(rl, k, qy, Y + k, y_peer)
        if k < half:
            push(rl, k, qy, D + k, x_peer)
    push(1 - rl, None, q, C + 1, c_peer)
    push(rl, None, qy, C + 2, c_peer)
    turn(clump)
    for k in range(nrh):
        arrived(1 - rl, k, qy, D + k, x_peer if k < half else y_peer)
    push(1 - rl, None, qy, C + 3, c_peer)
    turn(blocks)
    for b in (q, qy):
        store(out_ref.at[pl.ds(2 * b, 2)], query_hbm.at[pl.ds(2 * b, 2)])
    qc, qyc = yl * 2 + 1 - core, (1 - yl) * 2 + 1 - core
    arrived(rl, None, qc, C, c_peer)
    arrived(1 - rl, None, qc, C + 1, c_peer)
    arrived(rl, None, qyc, C + 2, c_peer)
    arrived(1 - rl, None, qyc, C + 3, c_peer)
    for b in (qc, qyc):
        store(out_ref.at[pl.ds(2 * b, 2)], query_hbm.at[pl.ds(2 * b, 2)])
    for one in started:
        one.wait_send()
    for one in stores:
        one.wait()


def attend_kernel(
    scale, meta_ref, query_hbm, keys_hbm, part_ref, stat_ref,
    query_ref, keys_ref, scores, tops, denoms, total, owner, start, query_sem, page_sem,
):
    requests, heads, _ = query_ref.shape
    width = part_ref.shape[2]
    held = meta_ref[2, requests]

    def fetch(k):
        return pltpu.make_async_copy(
            keys_hbm.at[meta_ref[0, k]], keys_ref.at[k], page_sem.at[k]
        )

    def fetch_query(r):
        return pltpu.make_async_copy(query_hbm.at[r], query_ref.at[r], query_sem.at[r])

    def start_fetch(k, carry):
        fetch(k).start()
        return carry

    def end_fetch(k, carry):
        fetch(k).wait()
        return carry

    fetch_query(0).start()
    lax.fori_loop(0, jnp.minimum(held, 2 * GROUP), start_fetch, 0)
    for r in range(1, requests):
        fetch_query(r).start()
    lax.fori_loop(jnp.minimum(held, 2 * GROUP), held, start_fetch, 0)
    for i in range(GROUP):
        keys_ref[held + i] = jnp.zeros(keys_ref.shape[1:], keys_ref.dtype)

    def list_request(r, count):
        begin, end = meta_ref[2, r], meta_ref[2, r + 1]
        groups = (end - begin + GROUP - 1) // GROUP

        def list_group(g, carry):
            owner[count + g] = r
            start[count + g] = begin + g * GROUP
            return carry

        lax.fori_loop(0, groups, list_group, 0)
        return count + groups

    count = lax.fori_loop(0, requests, list_request, 0)
    for i in range(PAIR - 1):
        owner[count + i] = requests
        start[count + i] = 0
    rounds = (count + PAIR - 1) // PAIR

    tops[...] = jnp.full(tops.shape, MASKED, jnp.float32)
    denoms[...] = jnp.zeros(denoms.shape, jnp.float32)
    total[...] = jnp.zeros(total.shape, jnp.float32)
    token = lax.broadcasted_iota(jnp.int32, (PAGE, heads), 0)

    def pages(at, columns_kept):
        rows = keys_ref[pl.ds(at, GROUP), :, 0:columns_kept]
        return rows.reshape(GROUP * PAGE, columns_kept)

    for r in range(requests):
        fetch_query(r).wait()

    def score_round(n, here):
        need = jnp.maximum(start[n * PAIR], start[n * PAIR + PAIR - 1]) + GROUP
        need = jnp.maximum(jnp.minimum(need, held), here)
        lax.fori_loop(here, need, end_fetch, 0)
        products = []
        for u in range(PAIR):
            g = n * PAIR + u
            products.append(
                lax.dot_general(
                    pages(start[g], keys_ref.shape[2]),
                    query_ref[lax.rem(owner[g], requests)],
                    (((1,), (1,)), ((), ())),
                    preferred_element_type=jnp.float32,
                )
            )
        for u in range(PAIR):
            g = n * PAIR + u
            at, r = start[g], owner[g]
            end = jnp.where(r < requests, meta_ref[2, jnp.minimum(r, requests - 1) + 1], 0)
            top = tops[r]
            for j in range(GROUP):
                live = jnp.where(at + j < end, meta_ref[1, at + j], 0)
                rows = slice(j * PAGE, (j + 1) * PAGE)
                piece = jnp.where(token < live, products[u][rows] * scale, MASKED)
                scores[g, rows, :] = piece
                top = jnp.maximum(top, jnp.max(piece, axis=0, keepdims=True))
            tops[r] = top
        return need

    here = lax.fori_loop(0, rounds, score_round, 0)
    lax.fori_loop(here, held, end_fetch, 0)

    def sum_round(n, carry):
        products = []
        for u in range(PAIR):
            g = n * PAIR + u
            r = owner[g]
            expo = jnp.exp(scores[g] - tops[r][0:1]).astype(jnp.bfloat16)
            denoms[r] += jnp.sum(expo.astype(jnp.float32), axis=0, keepdims=True)
            products.append(
                lax.dot_general(
                    expo, pages(start[g], width), (((0,), (0,)), ((), ())),
                    preferred_element_type=jnp.float32,
                )
            )
        for u in range(PAIR):
            total[owner[n * PAIR + u]] += products[u]
        return carry

    lax.fori_loop(0, rounds, sum_round, 0)
    line = lax.broadcasted_iota(jnp.int32, stat_ref.shape[1:], 0)
    for r in range(requests):
        stat_ref[r] = jnp.where(line == 0, tops[r], jnp.where(line == 1, denoms[r], 0.0))
        part_ref[r] = total[r].astype(part_ref.dtype)


def columns(lines):
    line = lax.broadcasted_iota(jnp.int32, (8, 128), 0)
    tiles = []
    for t in range(0, len(lines), 8):
        tile = jnp.zeros((8, 128), jnp.float32)
        for i, one in enumerate(lines[t : t + 8]):
            tile = jnp.where(line == i, one, tile)
        tiles.append(tile)
    left = 128 - 8 * len(tiles)
    if left:
        tiles.append(jnp.zeros((left, 128), jnp.float32))
    return jnp.concatenate(tiles, axis=0).T


def reduce_kernel(
    nrh, ncg, heads, part_ref, stat_ref, weights_ref, out_ref, shared, core_part, core_stat, y_send, y_stat, y_part, y_stat_in, own, own_stat,
    row_send, row_stat, row_part, row_stat_in, mix, lines, value, send, recv, row_sem_s, row_sem_r,
):
    rh, rl, cg, yl, core = place(nrh)
    nrow = 2 * nrh
    spots = nrow * ncg
    q = yl * 2 + core
    c_peer = device(rh, rl, cg, yl, 1 - core)
    y_peer = device(rh, rl, cg, 1 - yl, core)
    d_peer = device(rh, rl, cg, 1 - yl, 1 - core)
    me = (rl * nrh + rh) * ncg + cg

    def spot(i):
        place_i = i // ncg
        return device(place_i % nrh, place_i // nrh, i % ncg, yl, core)

    barrier = pltpu.get_barrier_semaphore()
    for peer in (c_peer, y_peer, d_peer):
        pl.semaphore_signal(barrier, inc=1, device_id=peer, device_id_type=MESH)

    def hello(d, carry):
        pl.semaphore_signal(
            barrier, inc=1, device_id=spot((me + d) % spots), device_id_type=MESH
        )
        return carry

    lax.fori_loop(1, spots, hello, 0)

    def block_of(y, c):
        return pl.ds(2 * (2 * y + c), 2)

    pl.semaphore_wait(barrier, spots + 2)

    def remote(src, dst, slot, peer):
        return pltpu.make_async_remote_copy(
            src_ref=src, dst_ref=dst, send_sem=send.at[slot], recv_sem=recv.at[slot],
            device_id=peer, device_id_type=MESH,
        )

    started = []

    def push(*args):
        one = remote(*args)
        one.start()
        started.append(one)
        return one

    stat_in = push(stat_ref, core_stat, 0, c_peer)
    base = 4 + nrow
    core_in = []
    for d in range(1, nrow + 1):
        place_k = (rl * nrh + rh + d) % nrow
        a, k = place_k // nrh, place_k % nrh
        core_in.append(
            push(
                part_ref.at[block_of(1 - yl, 1 - core), a, k], core_part.at[0, :, a, k],
                base + 2 + d, c_peer,
            )
        )
    own_in = push(part_ref.at[block_of(yl, 1 - core)], core_part.at[1], 2, c_peer)
    line = lax.broadcasted_iota(jnp.int32, (8, 128), 0)

    def merge_stats(first, second):
        top = jnp.maximum(first[0:1], second[0:1])
        one, two = jnp.exp(first[0:1] - top), jnp.exp(second[0:1] - top)
        denom = one * first[1:2] + two * second[1:2]
        return jnp.where(line == 0, top, jnp.where(line == 1, denom, 0.0)), [one, two]

    def merge_chunk(n, place_k, first, second):
        weight = mix[pl.ds(pl.multiple_of(place_k * heads, heads), heads), :]
        one, two = weight[:, 2 * n : 2 * n + 1], weight[:, 2 * n + 1 : 2 * n + 2]
        return one * first.astype(jnp.float32) + two * second.astype(jnp.float32)

    stat_in.wait_recv()
    weights = []
    for side in range(2):
        stats = y_stat if side == 0 else own_stat
        for i in range(2):
            r = 2 * (2 * (1 - yl if side == 0 else yl) + core) + i
            stats[i], pair = merge_stats(stat_ref[r], core_stat[r])
            weights += pair
        if side == 0:
            push(y_stat, y_stat_in, 3, y_peer)
    mix[...] = columns(weights)
    for side in range(2):
        y = 1 - yl if side == 0 else yl
        if side == 1:
            own_in.wait_recv()
        for d in range(1, nrow + 1):
            place_k = (rl * nrh + rh + d) % nrow
            a, k = place_k // nrh, place_k % nrh
            if side == 0:
                core_in[d - 1].wait_recv()
            for i in range(2):
                r = 2 * (2 * y + core) + i
                merged = merge_chunk(
                    2 * side + i, place_k, part_ref[r, a, k], core_part[side, i, a, k]
                )
                if side == 0:
                    y_send[a, k, i] = merged.astype(y_send.dtype)
                else:
                    own[a, k, i] = merged
            if side == 0:
                push(y_send.at[a, k], y_part.at[a, k], 3 + d, y_peer)

    remote(y_stat, y_stat_in, 3, y_peer).wait_recv()
    weights = []
    for i in range(2):
        row_stat[i], pair = merge_stats(own_stat[i], y_stat_in[i])
        weights += pair
    mix[...] = columns(weights)

    def row_copies(to, source, d):
        return (
            pltpu.make_async_remote_copy(
                src_ref=row_send.at[to // ncg], dst_ref=row_part.at[source],
                send_sem=row_sem_s.at[0, d], recv_sem=row_sem_r.at[0, source],
                device_id=spot(to), device_id_type=MESH,
            ),
            pltpu.make_async_remote_copy(
                src_ref=row_stat, dst_ref=row_stat_in.at[source],
                send_sem=row_sem_s.at[1, d], recv_sem=row_sem_r.at[1, source],
                device_id=spot(to), device_id_type=MESH,
            ),
        )

    def send_stat(d, carry):
        row_copies((me + d) % spots, me, d)[1].start()
        return carry

    lax.fori_loop(1, spots, send_stat, 0)
    row_stat_in[me] = row_stat[...]

    def chunk_step(place_k, d):
        a, k = place_k // nrh, place_k % nrh
        remote(y_send.at[a, k], y_part.at[a, k], 3 + d, y_peer).wait_recv()
        for i in range(2):
            row_send[place_k, i] = merge_chunk(
                i, place_k, own[a, k, i], y_part[a, k, i]
            ).astype(row_send.dtype)

    my_heads = pl.ds(pl.multiple_of((rl * nrh + rh) * heads, heads), heads)

    for d in range(1, nrow + 1):
        place_k = (rl * nrh + rh + d) % nrow
        chunk_step(place_k, d)

        def send_chunk(g, carry, place_k=place_k):
            to = place_k * ncg + g

            @pl.when(to != me)
            def _():
                row_copies(to, me, (to - me + spots) % spots)[0].start()

            return carry

        lax.fori_loop(0, ncg, send_chunk, 0)
    row_part[me] = row_send[me // ncg]

    def take_stat(d, carry):
        row_copies(me, (me + d) % spots, d)[1].wait_recv()
        return carry

    lax.fori_loop(1, spots, take_stat, 0)
    weights, denoms = [], []
    for i in range(2):
        parts = [(row_stat_in[n, i][0:1], row_stat_in[n, i][1:2]) for n in range(spots)]
        top = functools.reduce(jnp.maximum, [one for one, _ in parts])
        shares = [jnp.exp(one - top) for one, _ in parts]
        denoms.append(sum(share * denom for share, (_, denom) in zip(shares, parts)))
        weights += shares
    weights += denoms
    for n in range(0, len(weights), 128):
        lines[n // 128] = columns(weights[n : n + 128])

    def column(n):
        return lines[n // 128, my_heads, :][:, n % 128 : n % 128 + 1]

    def take_part(d, carry):
        row_copies(me, (me + d) % spots, d)[0].wait_recv()
        return carry

    lax.fori_loop(1, spots, take_part, 0)

    for i in range(2):
        total = sum(
            column(i * spots + n) * row_part[n, i].astype(jnp.float32) for n in range(spots)
        )
        value[i * heads : (i + 1) * heads, :] = total / column(2 * spots + i)
    rows = value[...].astype(jnp.bfloat16)

    shared[q] = head_diagonal(rows, weights_ref, heads).reshape(2, heads, shared.shape[3])
    outs = ((c_peer, yl * 2 + 1 - core), (y_peer, (1 - yl) * 2 + core),
            (d_peer, (1 - yl) * 2 + 1 - core))
    for n, (peer, _) in enumerate(outs):
        push(shared.at[q], shared.at[q], base + n, peer)
    for n, (peer, owner) in enumerate(outs):
        remote(shared.at[owner], shared.at[owner], base + n, peer).wait_recv()
    size = shared.shape[3]
    for h in range(heads):
        block = shared[:, :, h, :].reshape(8, size)
        out_ref[:, h * size : (h + 1) * size] = block.astype(out_ref.dtype)
    for one in started:
        one.wait_send()

    def drain(d, carry):
        for one in row_copies((me + d) % spots, me, d):
            one.wait_send()
        return carry

    lax.fori_loop(1, spots, drain, 0)


def local(
    query_nope, query_rope, key_up_weight, value_up_weight, latent_cache, lengths, page_table
):
    scale = float(HEAD_NOPE_WIDTH + ROTARY_WIDTH) ** (-0.5)
    requests, heads, nope = query_nope.shape
    width = key_up_weight.shape[2]
    full = latent_cache.shape[1]
    nrow, ncol = lax.axis_size("row"), lax.axis_size("col")
    nrh, ncg = nrow // 2, ncol // 4
    all_heads = nrow * heads
    slots = latent_cache.shape[0] // PAGE
    wire = jnp.bfloat16 if heads % 16 == 0 else jnp.float32
    vmem = pl.BlockSpec(memory_space=pltpu.VMEM)
    smem = pl.BlockSpec(memory_space=pltpu.SMEM)
    hbm = pl.BlockSpec(memory_space=pl.ANY)

    queries, keys, meta = pl.pallas_call(
        functools.partial(gather_kernel, nrh, heads),
        out_shape=(
            jax.ShapeDtypeStruct((requests, 2, nrh, heads, full), wire),
            jax.ShapeDtypeStruct((slots, PAGE, full), jnp.bfloat16),
            jax.ShapeDtypeStruct((8, 128), jnp.int32),
        ),
        in_specs=[smem] + [hbm] * 5,
        out_specs=(hbm, hbm, vmem),
        scratch_shapes=[
            pltpu.VMEM((requests * heads, nope), wire),
            pltpu.VMEM(query_rope.shape, wire),
            pltpu.VMEM(key_up_weight.shape, jnp.bfloat16),
            pltpu.VMEM((full, slots * PAGE), jnp.bfloat16),
            pltpu.VMEM(page_table.shape, jnp.int32),
            pltpu.VMEM((requests, 2, nrh, heads, full), wire),
            pltpu.VMEM((slots, PAGE, full), jnp.bfloat16),
            pltpu.SemaphoreType.DMA((4 + CACHE_LOADS,)),
            pltpu.SemaphoreType.DMA((4 + slots * PAGE // (BLOCK * STORED),)),
            pltpu.SemaphoreType.DMA((4 * nrh + 4,)), pltpu.SemaphoreType.DMA((4 * nrh + 4,))],
        compiler_params=pltpu.CompilerParams(
            collective_id=0, has_side_effects=True, vmem_limit_bytes=VMEM_LIMIT
        ),
        name="gather_queries",
    )(
        lengths,
        query_nope.astype(wire).reshape(requests * heads, nope),
        query_rope.astype(wire),
        key_up_weight,
        latent_cache.T,
        page_table,
    )
    queries = queries.reshape(requests, all_heads, full).astype(jnp.bfloat16)

    most = slots // GROUP + requests + PAIR
    part, stat = pl.pallas_call(
        functools.partial(attend_kernel, scale),
        out_shape=(
            jax.ShapeDtypeStruct((requests, all_heads, width), wire),
            jax.ShapeDtypeStruct((requests, 8, all_heads), jnp.float32),
        ),
        in_specs=[smem, hbm, hbm],
        out_specs=(vmem, vmem),
        scratch_shapes=[
            pltpu.VMEM((requests, all_heads, full), jnp.bfloat16),
            pltpu.VMEM((slots + GROUP, PAGE, full), jnp.bfloat16),
            pltpu.VMEM((most, GROUP * PAGE, all_heads), jnp.float32),
            pltpu.VMEM((requests + 1, 8, all_heads), jnp.float32),
            pltpu.VMEM((requests + 1, 8, all_heads), jnp.float32),
            pltpu.VMEM((requests + 1, all_heads, width), jnp.float32),
            pltpu.SMEM((most,), jnp.int32),
            pltpu.SMEM((most,), jnp.int32),
            pltpu.SemaphoreType.DMA((requests,)),
            pltpu.SemaphoreType.DMA((slots,)),
        ],
        compiler_params=pltpu.CompilerParams(vmem_limit_bytes=52 * 1024 * 1024),
        name="attend_pages",
    )(meta, queries, keys)

    spots = nrow * ncg
    f32 = jnp.float32
    shape = (2, nrh, 2, heads, width)
    values = pl.pallas_call(
        functools.partial(reduce_kernel, nrh, ncg, heads),
        out_shape=jax.ShapeDtypeStruct(
            (requests, heads * value_up_weight.shape[2]), jnp.bfloat16
        ),
        in_specs=[vmem] * 3,
        out_specs=vmem,
        scratch_shapes=[
            pltpu.VMEM((4, 2, heads, value_up_weight.shape[2]), f32),
            pltpu.VMEM((2, 2, 2, nrh, heads, width), wire),
            pltpu.VMEM((requests, 8, all_heads), f32),
            pltpu.VMEM(shape, wire),
            pltpu.VMEM((2, 8, all_heads), f32),
            pltpu.VMEM(shape, wire),
            pltpu.VMEM((2, 8, all_heads), f32),
            pltpu.VMEM(shape, f32),
            pltpu.VMEM((2, 8, all_heads), f32),
            pltpu.VMEM((nrow, 2, heads, width), wire),
            pltpu.VMEM((2, 8, all_heads), f32),
            pltpu.VMEM((spots, 2, heads, width), wire),
            pltpu.VMEM((spots, 2, 8, all_heads), f32),
            pltpu.VMEM((128, 128), f32),
            pltpu.VMEM((-(-(2 * spots + 2) // 128), 128, 128), f32),
            pltpu.VMEM((2 * heads, width), f32),
            pltpu.SemaphoreType.DMA((7 + 2 * nrow,)),
            pltpu.SemaphoreType.DMA((7 + 2 * nrow,)),
            pltpu.SemaphoreType.DMA((2, spots)),
            pltpu.SemaphoreType.DMA((2, spots)),
        ],
        compiler_params=pltpu.CompilerParams(
            collective_id=1, has_side_effects=True, vmem_limit_bytes=40 * 1024 * 1024
        ),
        name="reduce_parts",
    )(part.reshape(requests, 2, nrh, heads, width), stat, value_up_weight)
    return values


def solution(mesh):
    placed = (
        P(None, "row", None),
        P(None, "row", None),
        P("row", None, None),
        P("row", None, None),
        P(("row", "col"), None),
        P(),
        P(),
    )
    return jax.shard_map(
        local, mesh=mesh, in_specs=placed, out_specs=P(None, "row"), check_vma=False
    )
```

```python
import functools

import jax
import jax.numpy as jnp
from jax import lax
from jax.experimental import pallas as pl
from jax.experimental.pallas import tpu as pltpu
from jax.sharding import PartitionSpec as P

HEAD_NOPE_WIDTH = 128
ROTARY_WIDTH = 64
PAGE = 64
GROUP = 4
PAIR = 2
BLOCK = 128
CACHE_LOADS = 4
STORED = 4
LIST_ROWS = 8192
MASKED = -1e30
MESH = pl.DeviceIdType.MESH
VMEM_LIMIT = 62 * 1024 * 1024


def place(nrh):
    row, col = lax.axis_index("row"), lax.axis_index("col")
    return row // 2, row % 2, col // 4, (col // 2) % 2, col % 2


def device(rh, rl, cg, yl, core):
    return (rh * 2 + rl, cg * 4 + yl * 2 + core)


def head_diagonal(rows, weights_ref, heads, ready=lambda h: None):
    count = rows.shape[0]
    head = lax.broadcasted_iota(jnp.int32, (count, weights_ref.shape[2]), 0) % heads
    total = jnp.zeros((count, weights_ref.shape[2]), jnp.float32)
    for h in range(heads):
        ready(h)
        product = jnp.dot(rows, weights_ref[h], preferred_element_type=jnp.float32)
        total = jnp.where(head == h, product, total)
    return total


def list_pages(device_at, slots, length_ref, table_ref, meta_ref):
    requests, pages = table_ref.shape
    chunk = 128
    slot = lax.broadcasted_iota(jnp.int32, (slots, chunk), 0)
    owner = jnp.zeros((slots, chunk), jnp.int32)
    live = jnp.zeros((slots, chunk), jnp.int32)
    for r in range(requests):
        for c in range(pages // chunk):
            entry = table_ref[r : r + 1, c * chunk : (c + 1) * chunk] - device_at * slots
            page = lax.broadcasted_iota(jnp.int32, (1, chunk), 1) + c * chunk
            left = jnp.clip(length_ref[r] - page * PAGE, 0, PAGE)
            match = entry == slot
            owner += jnp.where(match, r - requests, 0)
            live += jnp.where(match, left, 0)
    f32 = jnp.float32
    owner = jnp.sum(owner.astype(f32), axis=1, keepdims=True) + float(requests)
    live = jnp.sum(live.astype(f32), axis=1, keepdims=True)
    line = lax.broadcasted_iota(jnp.int32, (128, 128), 0).astype(f32)
    lane = lax.broadcasted_iota(jnp.int32, (128, 128), 1).astype(f32)
    spare = 128 - slots

    def fill(column, last):
        wide = jnp.broadcast_to(column, (slots, 128))
        return jnp.concatenate([wide, jnp.full((spare, 128), last, f32)], axis=0)

    down = fill(owner, float(requests + 1))
    across = down.T
    ahead = (down < across) | ((down == across) & (line < lane))
    rank = jnp.sum(jnp.where(ahead, 1.0, 0.0), axis=0, keepdims=True)
    hit = rank == line
    index = jnp.where(lane < float(slots), lane, 0.0)
    order = jnp.sum(jnp.where(hit, index, 0.0), axis=1, keepdims=True)
    sorted_live = jnp.sum(jnp.where(hit, fill(live, 0.0).T, 0.0), axis=1, keepdims=True)
    first = jnp.sum(jnp.where(down < lane, 1.0, 0.0), axis=0, keepdims=True)
    both = jnp.where(lane == 0.0, order, jnp.where(lane == 1.0, sorted_live, 0.0)).T
    rows = jnp.where(line[0:8] == 2.0, first, both[0:8])
    meta_ref[...] = rows.astype(jnp.int32)


def gather_kernel(
    nrh, heads, length_ref, nope_hbm, rope_hbm, weights_hbm, cache_hbm, table_hbm,
    query_hbm, keys_hbm, meta_hbm, meta_ref,
    nope_ref, rope_ref, weights_ref, cache_ref, table_ref, out_ref, keys_ref,
    local_sem, store_sem, send, recv,
):
    rh, rl, cg, yl, core = place(nrh)
    q = yl * 2 + core
    qy = (1 - yl) * 2 + core
    z_peer = lambda k: device(k, rl, cg, yl, core)
    x_peer = device(rh, 1 - rl, cg, yl, core)
    y_peer = device(rh, rl, cg, 1 - yl, core)
    c_peer = device(rh, rl, cg, yl, 1 - core)
    barrier = pltpu.get_barrier_semaphore()
    peers = [z_peer((rh + d) % nrh) for d in range(1, nrh)] + [x_peer, y_peer, c_peer]
    for peer in peers:
        pl.semaphore_signal(barrier, inc=1, device_id=peer, device_id_type=MESH)
    blocks = cache_hbm.shape[1] // BLOCK
    pages = BLOCK // PAGE
    loads = [
        pltpu.make_async_copy(nope_hbm, nope_ref, local_sem.at[0]),
        pltpu.make_async_copy(rope_hbm, rope_ref, local_sem.at[1]),
    ]
    quarter = heads // 4
    weight_loads = [
        pltpu.make_async_copy(
            weights_hbm.at[pl.ds(n * quarter, quarter)], weights_ref.at[pl.ds(n * quarter, quarter)],
            local_sem.at[4 + CACHE_LOADS + n],
        )
        for n in range(4)
    ]
    span = cache_hbm.shape[1] // CACHE_LOADS
    cache_loads = [
        pltpu.make_async_copy(
            cache_hbm.at[:, pl.ds(j * span, span)], cache_ref.at[:, pl.ds(j * span, span)],
            local_sem.at[3 + j],
        )
        for j in range(CACHE_LOADS)
    ]
    load_table = pltpu.make_async_copy(table_hbm, table_ref, local_sem.at[3 + CACHE_LOADS])
    for one in loads + weight_loads + [load_table]:
        one.start()
    stores = []

    def store(source, target):
        one = pltpu.make_async_copy(source, target, store_sem.at[len(stores)])
        one.start()
        stores.append(one)

    turned = [0]

    def turn(count):
        for _ in range(count):
            b = turned[0]
            if b >= blocks:
                return
            if b * BLOCK % span == 0:
                cache_loads[b * BLOCK // span].wait()
            block = cache_ref[:, b * BLOCK : (b + 1) * BLOCK].T
            keys_ref[b * pages : (b + 1) * pages] = block.reshape(pages, PAGE, block.shape[1])
            turned[0] += 1
            if turned[0] % STORED == 0:
                done = pl.ds((turned[0] - STORED) * pages, STORED * pages)
                store(keys_ref.at[done], keys_hbm.at[done])

    for one in loads:
        one.wait()

    def ready(h):
        if h % quarter == 0:
            weight_loads[h // quarter].wait()
        if h == 3 * quarter:
            for one in cache_loads:
                one.start()

    rows = nope_ref[pl.ds(pl.multiple_of(q * 2 * heads, 2 * heads), 2 * heads), :]
    latent = head_diagonal(rows.astype(jnp.bfloat16), weights_ref, heads, ready)
    latent = latent.astype(jnp.bfloat16).astype(out_ref.dtype)
    width = weights_ref.shape[2]
    for i in range(2):
        out_ref[2 * q + i, rl, rh, :, 0:width] = latent[i * heads : (i + 1) * heads]
        out_ref[2 * q + i, rl, rh, :, width:] = rope_ref[2 * q + i]
    pl.semaphore_wait(barrier, len(peers))

    started = []

    def copy(a, k, b, slot, peer, send_slot=None):
        shard = out_ref.at[pl.ds(2 * b, 2), a] if k is None else out_ref.at[pl.ds(2 * b, 2), a, k]
        return pltpu.make_async_remote_copy(
            src_ref=shard,
            dst_ref=shard,
            send_sem=send.at[slot if send_slot is None else send_slot],
            recv_sem=recv.at[slot],
            device_id=peer,
            device_id_type=MESH,
        )

    def push(*args, **kw):
        one = copy(*args, **kw)
        one.start()
        started.append(one)

    def arrived(a, k, b, slot, peer):
        copy(a, k, b, slot, peer).wait_recv()

    def put(a, b):
        store(out_ref.at[pl.ds(2 * b, 2), a], query_hbm.at[pl.ds(2 * b, 2), a])

    Z, X, Y, D, C = 0, nrh, 2 * nrh, 3 * nrh, 4 * nrh
    half = nrh // 2
    clump = -(-blocks // 4)

    def spread(k):
        push(rl, k, q, X + k, x_peer)
        push(rl, k, q, Y + k, y_peer)

    for d in range(1, nrh):
        push(rl, rh, q, Z + rh, z_peer((rh + d) % nrh), send_slot=Z + d)
    spread(rh)
    load_table.wait()
    device_at = (rh * 2 + rl) * (lax.axis_size("col")) + cg * 4 + q
    list_pages(device_at, blocks * pages, length_ref, table_ref, meta_ref)
    store(meta_ref, meta_hbm.at[pl.ds(0, 8)])
    turn(clump)
    for d in range(1, nrh):
        k = (rh + d) % nrh
        arrived(rl, k, q, Z + k, z_peer(k))
        spread(k)
    push(rl, None, q, C, c_peer)
    put(rl, q)
    turn(clump)
    for k in range(nrh):
        arrived(1 - rl, k, q, X + k, x_peer)
        if k >= half:
            push(1 - rl, k, q, D + k, y_peer)
        arrived(rl, k, qy, Y + k, y_peer)
        if k < half:
            push(rl, k, qy, D + k, x_peer)
    push(1 - rl, None, q, C + 1, c_peer)
    push(rl, None, qy, C + 2, c_peer)
    put(1 - rl, q)
    put(rl, qy)
    turn(clump)
    for k in range(nrh):
        arrived(1 - rl, k, qy, D + k, x_peer if k < half else y_peer)
    push(1 - rl, None, qy, C + 3, c_peer)
    turn(blocks)
    put(1 - rl, qy)
    qc, qyc = yl * 2 + 1 - core, (1 - yl) * 2 + 1 - core
    for n, (a, b) in enumerate(((rl, qc), (1 - rl, qc), (rl, qyc), (1 - rl, qyc))):
        arrived(a, None, b, C + n, c_peer)
        put(a, b)
    for one in started:
        one.wait_send()
    for one in stores:
        one.wait()


def attend_kernel(
    scale, meta_hbm, query_hbm, keys_hbm, part_ref, stat_ref,
    meta_ref, query_ref, keys_ref, scores, tops, denoms, total, owner, start,
    query_sem, page_sem,
):
    requests, heads, _ = query_ref.shape
    width = part_ref.shape[2]
    fetch_lists = pltpu.make_async_copy(
        meta_hbm.at[pl.ds(0, 8)], meta_ref, query_sem.at[requests]
    )
    fetch_lists.start()

    def fetch(k):
        return pltpu.make_async_copy(
            keys_hbm.at[meta_ref[0, k]], keys_ref.at[k], page_sem.at[k]
        )

    def fetch_query(r):
        return pltpu.make_async_copy(query_hbm.at[r], query_ref.at[r], query_sem.at[r])

    def start_fetch(k, carry):
        fetch(k).start()
        return carry

    def end_fetch(k, carry):
        fetch(k).wait()
        return carry

    for r in range(requests):
        fetch_query(r).start()
    tops[...] = jnp.full(tops.shape, MASKED, jnp.float32)
    denoms[...] = jnp.zeros(denoms.shape, jnp.float32)
    total[...] = jnp.zeros(total.shape, jnp.float32)
    fetch_lists.wait()
    held = meta_ref[2, requests]
    lax.fori_loop(0, held, start_fetch, 0)
    for i in range(GROUP):
        keys_ref[held + i] = jnp.zeros(keys_ref.shape[1:], keys_ref.dtype)

    def list_request(r, count):
        begin, end = meta_ref[2, r], meta_ref[2, r + 1]
        groups = (end - begin + GROUP - 1) // GROUP

        def list_group(g, carry):
            owner[count + g] = r
            start[count + g] = begin + g * GROUP
            return carry

        lax.fori_loop(0, groups, list_group, 0)
        return count + groups

    count = lax.fori_loop(0, requests, list_request, 0)
    for i in range(PAIR - 1):
        owner[count + i] = requests
        start[count + i] = 0
    rounds = (count + PAIR - 1) // PAIR
    token = lax.broadcasted_iota(jnp.int32, (PAGE, heads), 0)

    def pages(at, columns_kept):
        rows = keys_ref[pl.ds(at, GROUP), :, 0:columns_kept]
        return rows.reshape(GROUP * PAGE, columns_kept)

    def end_query(r, carry):
        fetch_query(r).wait()
        return carry

    def score_round(n, carry):
        here, asked = carry
        wanted = jnp.maximum(owner[n * PAIR], owner[n * PAIR + PAIR - 1]) + 1
        wanted = jnp.minimum(wanted, requests)
        lax.fori_loop(asked, wanted, end_query, 0)
        need = jnp.maximum(start[n * PAIR], start[n * PAIR + PAIR - 1]) + GROUP
        need = jnp.maximum(jnp.minimum(need, held), here)
        lax.fori_loop(here, need, end_fetch, 0)
        products = []
        for u in range(PAIR):
            g = n * PAIR + u
            products.append(
                lax.dot_general(
                    pages(start[g], keys_ref.shape[2]),
                    query_ref[lax.rem(owner[g], requests)],
                    (((1,), (1,)), ((), ())),
                    preferred_element_type=jnp.float32,
                )
            )
        for u in range(PAIR):
            g = n * PAIR + u
            at, r = start[g], owner[g]
            end = jnp.where(r < requests, meta_ref[2, jnp.minimum(r, requests - 1) + 1], 0)
            top = tops[r]
            for j in range(GROUP):
                live = jnp.where(at + j < end, meta_ref[1, at + j], 0)
                rows = slice(j * PAGE, (j + 1) * PAGE)
                piece = jnp.where(token < live, products[u][rows] * scale, MASKED)
                scores[g, rows, :] = piece
                top = jnp.maximum(top, jnp.max(piece, axis=0, keepdims=True))
            tops[r] = top
        return need, wanted

    here, asked = lax.fori_loop(0, rounds, score_round, (0, 0))
    lax.fori_loop(here, held, end_fetch, 0)
    lax.fori_loop(asked, requests, end_query, 0)

    def sum_round(n, carry):
        products = []
        for u in range(PAIR):
            g = n * PAIR + u
            r = owner[g]
            expo = jnp.exp(scores[g] - tops[r][0:1]).astype(jnp.bfloat16)
            denoms[r] += jnp.sum(expo.astype(jnp.float32), axis=0, keepdims=True)
            products.append(
                lax.dot_general(
                    expo, pages(start[g], width), (((0,), (0,)), ((), ())),
                    preferred_element_type=jnp.float32,
                )
            )
        for u in range(PAIR):
            total[owner[n * PAIR + u]] += products[u]
        return carry

    lax.fori_loop(0, rounds, sum_round, 0)
    line = lax.broadcasted_iota(jnp.int32, stat_ref.shape[1:], 0)
    for r in range(requests):
        stat_ref[r] = jnp.where(line == 0, tops[r], jnp.where(line == 1, denoms[r], 0.0))
        part_ref[r] = total[r].astype(part_ref.dtype)


def columns(lines):
    line = lax.broadcasted_iota(jnp.int32, (8, 128), 0)
    tiles = []
    for t in range(0, len(lines), 8):
        tile = jnp.zeros((8, 128), jnp.float32)
        for i, one in enumerate(lines[t : t + 8]):
            tile = jnp.where(line == i, one, tile)
        tiles.append(tile)
    left = 128 - 8 * len(tiles)
    if left:
        tiles.append(jnp.zeros((left, 128), jnp.float32))
    return jnp.concatenate(tiles, axis=0).T


def reduce_kernel(
    nrh, ncg, heads, part_ref, stat_ref, weights_ref, out_ref, shared, core_part, core_stat, y_send, y_stat, y_part, y_stat_in, own, own_stat,
    row_send, row_stat, row_part, row_stat_in, mix, lines, value, send, recv, row_sem_s, row_sem_r,
):
    rh, rl, cg, yl, core = place(nrh)
    nrow = 2 * nrh
    spots = nrow * ncg
    q = yl * 2 + core
    c_peer = device(rh, rl, cg, yl, 1 - core)
    y_peer = device(rh, rl, cg, 1 - yl, core)
    d_peer = device(rh, rl, cg, 1 - yl, 1 - core)
    me = (rl * nrh + rh) * ncg + cg

    def spot(i):
        place_i = i // ncg
        return device(place_i % nrh, place_i // nrh, i % ncg, yl, core)

    barrier = pltpu.get_barrier_semaphore()
    for peer in (c_peer, y_peer, d_peer):
        pl.semaphore_signal(barrier, inc=1, device_id=peer, device_id_type=MESH)

    def hello(d, carry):
        pl.semaphore_signal(
            barrier, inc=1, device_id=spot((me + d) % spots), device_id_type=MESH
        )
        return carry

    lax.fori_loop(1, spots, hello, 0)

    def block_of(y, c):
        return pl.ds(2 * (2 * y + c), 2)

    pl.semaphore_wait(barrier, spots + 2)

    def remote(src, dst, slot, peer):
        return pltpu.make_async_remote_copy(
            src_ref=src, dst_ref=dst, send_sem=send.at[slot], recv_sem=recv.at[slot],
            device_id=peer, device_id_type=MESH,
        )

    started = []

    def push(*args):
        one = remote(*args)
        one.start()
        started.append(one)
        return one

    stat_in = push(stat_ref, core_stat, 0, c_peer)
    base = 4 + nrow
    core_in = []
    for d in range(1, nrow + 1):
        place_k = (rl * nrh + rh + d) % nrow
        a, k = place_k // nrh, place_k % nrh
        core_in.append(
            push(
                part_ref.at[block_of(1 - yl, 1 - core), a, k], core_part.at[0, :, a, k],
                base + 2 + d, c_peer,
            )
        )
    own_in = push(part_ref.at[block_of(yl, 1 - core)], core_part.at[1], 2, c_peer)
    line = lax.broadcasted_iota(jnp.int32, (8, 128), 0)

    def merge_stats(first, second):
        top = jnp.maximum(first[0:1], second[0:1])
        one, two = jnp.exp(first[0:1] - top), jnp.exp(second[0:1] - top)
        denom = one * first[1:2] + two * second[1:2]
        return jnp.where(line == 0, top, jnp.where(line == 1, denom, 0.0)), [one, two]

    def merge_chunk(n, place_k, first, second):
        weight = mix[pl.ds(pl.multiple_of(place_k * heads, heads), heads), :]
        one, two = weight[:, 2 * n : 2 * n + 1], weight[:, 2 * n + 1 : 2 * n + 2]
        return one * first.astype(jnp.float32) + two * second.astype(jnp.float32)

    stat_in.wait_recv()
    weights = []
    for side in range(2):
        stats = y_stat if side == 0 else own_stat
        for i in range(2):
            r = 2 * (2 * (1 - yl if side == 0 else yl) + core) + i
            stats[i], pair = merge_stats(stat_ref[r], core_stat[r])
            weights += pair
        if side == 0:
            push(y_stat, y_stat_in, 3, y_peer)
    mix[...] = columns(weights)
    for side in range(2):
        y = 1 - yl if side == 0 else yl
        if side == 1:
            own_in.wait_recv()
        for d in range(1, nrow + 1):
            place_k = (rl * nrh + rh + d) % nrow
            a, k = place_k // nrh, place_k % nrh
            if side == 0:
                core_in[d - 1].wait_recv()
            for i in range(2):
                r = 2 * (2 * y + core) + i
                merged = merge_chunk(
                    2 * side + i, place_k, part_ref[r, a, k], core_part[side, i, a, k]
                )
                if side == 0:
                    y_send[a, k, i] = merged.astype(y_send.dtype)
                else:
                    own[a, k, i] = merged
            if side == 0:
                push(y_send.at[a, k], y_part.at[a, k], 3 + d, y_peer)

    remote(y_stat, y_stat_in, 3, y_peer).wait_recv()
    weights = []
    for i in range(2):
        row_stat[i], pair = merge_stats(own_stat[i], y_stat_in[i])
        weights += pair
    mix[...] = columns(weights)

    def row_copies(to, source, d):
        return (
            pltpu.make_async_remote_copy(
                src_ref=row_send.at[to // ncg], dst_ref=row_part.at[source],
                send_sem=row_sem_s.at[0, d], recv_sem=row_sem_r.at[0, source],
                device_id=spot(to), device_id_type=MESH,
            ),
            pltpu.make_async_remote_copy(
                src_ref=row_stat, dst_ref=row_stat_in.at[source],
                send_sem=row_sem_s.at[1, d], recv_sem=row_sem_r.at[1, source],
                device_id=spot(to), device_id_type=MESH,
            ),
        )

    def send_stat(d, carry):
        row_copies((me + d) % spots, me, d)[1].start()
        return carry

    lax.fori_loop(1, spots, send_stat, 0)
    row_stat_in[me] = row_stat[...]

    def chunk_step(place_k, d):
        a, k = place_k // nrh, place_k % nrh
        remote(y_send.at[a, k], y_part.at[a, k], 3 + d, y_peer).wait_recv()
        for i in range(2):
            row_send[place_k, i] = merge_chunk(
                i, place_k, own[a, k, i], y_part[a, k, i]
            ).astype(row_send.dtype)

    my_heads = pl.ds(pl.multiple_of((rl * nrh + rh) * heads, heads), heads)

    for d in range(1, nrow + 1):
        place_k = (rl * nrh + rh + d) % nrow
        chunk_step(place_k, d)

        def send_chunk(g, carry, place_k=place_k):
            to = place_k * ncg + g

            @pl.when(to != me)
            def _():
                row_copies(to, me, (to - me + spots) % spots)[0].start()

            return carry

        lax.fori_loop(0, ncg, send_chunk, 0)
    row_part[me] = row_send[me // ncg]

    def take_stat(d, carry):
        row_copies(me, (me + d) % spots, d)[1].wait_recv()
        return carry

    lax.fori_loop(1, spots, take_stat, 0)
    weights, denoms = [], []
    for i in range(2):
        parts = [(row_stat_in[n, i][0:1], row_stat_in[n, i][1:2]) for n in range(spots)]
        top = functools.reduce(jnp.maximum, [one for one, _ in parts])
        shares = [jnp.exp(one - top) for one, _ in parts]
        denoms.append(sum(share * denom for share, (_, denom) in zip(shares, parts)))
        weights += shares
    weights += denoms
    for n in range(0, len(weights), 128):
        lines[n // 128] = columns(weights[n : n + 128])

    def column(n):
        return lines[n // 128, my_heads, :][:, n % 128 : n % 128 + 1]

    def take_part(d, carry):
        row_copies(me, (me + d) % spots, d)[0].wait_recv()
        return carry

    lax.fori_loop(1, spots, take_part, 0)

    for i in range(2):
        total = sum(
            column(i * spots + n) * row_part[n, i].astype(jnp.float32) for n in range(spots)
        )
        value[i * heads : (i + 1) * heads, :] = total / column(2 * spots + i)
    rows = value[...].astype(jnp.bfloat16)

    shared[q] = head_diagonal(rows, weights_ref, heads).reshape(2, heads, shared.shape[3])
    outs = ((c_peer, yl * 2 + 1 - core), (y_peer, (1 - yl) * 2 + core),
            (d_peer, (1 - yl) * 2 + 1 - core))
    for n, (peer, _) in enumerate(outs):
        push(shared.at[q], shared.at[q], base + n, peer)
    for n, (peer, owner) in enumerate(outs):
        remote(shared.at[owner], shared.at[owner], base + n, peer).wait_recv()
    size = shared.shape[3]
    for h in range(heads):
        block = shared[:, :, h, :].reshape(8, size)
        out_ref[:, h * size : (h + 1) * size] = block.astype(out_ref.dtype)
    for one in started:
        one.wait_send()

    def drain(d, carry):
        for one in row_copies((me + d) % spots, me, d):
            one.wait_send()
        return carry

    lax.fori_loop(1, spots, drain, 0)


def local(
    query_nope, query_rope, key_up_weight, value_up_weight, latent_cache, lengths, page_table
):
    scale = float(HEAD_NOPE_WIDTH + ROTARY_WIDTH) ** (-0.5)
    requests, heads, nope = query_nope.shape
    width = key_up_weight.shape[2]
    full = latent_cache.shape[1]
    nrow, ncol = lax.axis_size("row"), lax.axis_size("col")
    nrh, ncg = nrow // 2, ncol // 4
    all_heads = nrow * heads
    slots = latent_cache.shape[0] // PAGE
    wire = jnp.bfloat16 if heads % 16 == 0 else jnp.float32
    vmem = pl.BlockSpec(memory_space=pltpu.VMEM)
    smem = pl.BlockSpec(memory_space=pltpu.SMEM)
    hbm = pl.BlockSpec(memory_space=pl.ANY)

    queries, keys, meta = pl.pallas_call(
        functools.partial(gather_kernel, nrh, heads),
        out_shape=(
            jax.ShapeDtypeStruct((requests, 2, nrh, heads, full), wire),
            jax.ShapeDtypeStruct((slots, PAGE, full), jnp.bfloat16),
            jax.ShapeDtypeStruct((LIST_ROWS, 128), jnp.int32),
        ),
        in_specs=[smem] + [hbm] * 5,
        out_specs=(hbm, hbm, hbm),
        scratch_shapes=[
            pltpu.VMEM((8, 128), jnp.int32),
            pltpu.VMEM((requests * heads, nope), wire),
            pltpu.VMEM(query_rope.shape, wire),
            pltpu.VMEM(key_up_weight.shape, jnp.bfloat16),
            pltpu.VMEM((full, slots * PAGE), jnp.bfloat16),
            pltpu.VMEM(page_table.shape, jnp.int32),
            pltpu.VMEM((requests, 2, nrh, heads, full), wire),
            pltpu.VMEM((slots, PAGE, full), jnp.bfloat16),
            pltpu.SemaphoreType.DMA((8 + CACHE_LOADS,)),
            pltpu.SemaphoreType.DMA((9 + slots * PAGE // (BLOCK * STORED),)),
            pltpu.SemaphoreType.DMA((4 * nrh + 4,)), pltpu.SemaphoreType.DMA((4 * nrh + 4,))],
        compiler_params=pltpu.CompilerParams(
            collective_id=0, has_side_effects=True, vmem_limit_bytes=VMEM_LIMIT
        ),
        name="gather_queries",
    )(
        lengths,
        query_nope.astype(wire).reshape(requests * heads, nope),
        query_rope.astype(wire),
        key_up_weight,
        latent_cache.T,
        page_table,
    )
    queries = queries.reshape(requests, all_heads, full).astype(jnp.bfloat16)

    most = slots // GROUP + requests + PAIR
    part, stat = pl.pallas_call(
        functools.partial(attend_kernel, scale),
        out_shape=(
            jax.ShapeDtypeStruct((requests, all_heads, width), wire),
            jax.ShapeDtypeStruct((requests, 8, all_heads), jnp.float32),
        ),
        in_specs=[hbm, hbm, hbm],
        out_specs=(vmem, vmem),
        scratch_shapes=[
            pltpu.SMEM((8, 128), jnp.int32),
            pltpu.VMEM((requests, all_heads, full), jnp.bfloat16),
            pltpu.VMEM((slots + GROUP, PAGE, full), jnp.bfloat16),
            pltpu.VMEM((most, GROUP * PAGE, all_heads), jnp.float32),
            pltpu.VMEM((requests + 1, 8, all_heads), jnp.float32),
            pltpu.VMEM((requests + 1, 8, all_heads), jnp.float32),
            pltpu.VMEM((requests + 1, all_heads, width), jnp.float32),
            pltpu.SMEM((most,), jnp.int32),
            pltpu.SMEM((most,), jnp.int32),
            pltpu.SemaphoreType.DMA((requests + 1,)),
            pltpu.SemaphoreType.DMA((slots,)),
        ],
        compiler_params=pltpu.CompilerParams(vmem_limit_bytes=52 * 1024 * 1024),
        name="attend_pages",
    )(meta, queries, keys)

    spots = nrow * ncg
    f32 = jnp.float32
    shape = (2, nrh, 2, heads, width)
    values = pl.pallas_call(
        functools.partial(reduce_kernel, nrh, ncg, heads),
        out_shape=jax.ShapeDtypeStruct(
            (requests, heads * value_up_weight.shape[2]), jnp.bfloat16
        ),
        in_specs=[vmem] * 3,
        out_specs=vmem,
        scratch_shapes=[
            pltpu.VMEM((4, 2, heads, value_up_weight.shape[2]), f32),
            pltpu.VMEM((2, 2, 2, nrh, heads, width), wire),
            pltpu.VMEM((requests, 8, all_heads), f32),
            pltpu.VMEM(shape, wire),
            pltpu.VMEM((2, 8, all_heads), f32),
            pltpu.VMEM(shape, wire),
            pltpu.VMEM((2, 8, all_heads), f32),
            pltpu.VMEM(shape, f32),
            pltpu.VMEM((2, 8, all_heads), f32),
            pltpu.VMEM((nrow, 2, heads, width), wire),
            pltpu.VMEM((2, 8, all_heads), f32),
            pltpu.VMEM((spots, 2, heads, width), wire),
            pltpu.VMEM((spots, 2, 8, all_heads), f32),
            pltpu.VMEM((128, 128), f32),
            pltpu.VMEM((-(-(2 * spots + 2) // 128), 128, 128), f32),
            pltpu.VMEM((2 * heads, width), f32),
            pltpu.SemaphoreType.DMA((7 + 2 * nrow,)),
            pltpu.SemaphoreType.DMA((7 + 2 * nrow,)),
            pltpu.SemaphoreType.DMA((2, spots)),
            pltpu.SemaphoreType.DMA((2, spots)),
        ],
        compiler_params=pltpu.CompilerParams(
            collective_id=1, has_side_effects=True, vmem_limit_bytes=40 * 1024 * 1024
        ),
        name="reduce_parts",
    )(part.reshape(requests, 2, nrh, heads, width), stat, value_up_weight)
    return values


def solution(mesh):
    placed = (
        P(None, "row", None),
        P(None, "row", None),
        P("row", None, None),
        P("row", None, None),
        P(("row", "col"), None),
        P(),
        P(),
    )
    return jax.shard_map(
        local, mesh=mesh, in_specs=placed, out_specs=P(None, "row"), check_vma=False
    )
```

```python
import functools

import jax
import jax.numpy as jnp
from jax import lax
from jax.experimental import pallas as pl
from jax.experimental.pallas import tpu as pltpu
from jax.sharding import PartitionSpec as P

HEAD_NOPE_WIDTH = 128
ROTARY_WIDTH = 64
PAGE = 64
GROUP = 4
PAIR = 2
BLOCK = 128
CACHE_LOADS = 4
STORED = 4
LIST_ROWS = 8192
MASKED = -1e30
MESH = pl.DeviceIdType.MESH
VMEM_LIMIT = 62 * 1024 * 1024


def place(nrh):
    row, col = lax.axis_index("row"), lax.axis_index("col")
    return row // 2, row % 2, col // 4, (col // 2) % 2, col % 2


def device(rh, rl, cg, yl, core):
    return (rh * 2 + rl, cg * 4 + yl * 2 + core)


def head_diagonal(rows, weights_ref, heads, ready=lambda h: None):
    count = rows.shape[0]
    head = lax.broadcasted_iota(jnp.int32, (count, weights_ref.shape[2]), 0) % heads
    total = jnp.zeros((count, weights_ref.shape[2]), jnp.float32)
    for h in range(heads):
        ready(h)
        product = jnp.dot(rows, weights_ref[h], preferred_element_type=jnp.float32)
        total = jnp.where(head == h, product, total)
    return total


def list_pages(device_at, slots, length_ref, table_ref, meta_ref):
    requests, pages = table_ref.shape
    chunk = 128
    slot = lax.broadcasted_iota(jnp.int32, (slots, chunk), 0)
    owner = jnp.zeros((slots, chunk), jnp.int32)
    live = jnp.zeros((slots, chunk), jnp.int32)
    for r in range(requests):
        for c in range(pages // chunk):
            entry = table_ref[r : r + 1, c * chunk : (c + 1) * chunk] - device_at * slots
            page = lax.broadcasted_iota(jnp.int32, (1, chunk), 1) + c * chunk
            left = jnp.clip(length_ref[r] - page * PAGE, 0, PAGE)
            match = entry == slot
            owner += jnp.where(match, r - requests, 0)
            live += jnp.where(match, left, 0)
    f32 = jnp.float32
    owner = jnp.sum(owner.astype(f32), axis=1, keepdims=True) + float(requests)
    live = jnp.sum(live.astype(f32), axis=1, keepdims=True)
    line = lax.broadcasted_iota(jnp.int32, (128, 128), 0).astype(f32)
    lane = lax.broadcasted_iota(jnp.int32, (128, 128), 1).astype(f32)
    spare = 128 - slots

    def fill(column, last):
        wide = jnp.broadcast_to(column, (slots, 128))
        return jnp.concatenate([wide, jnp.full((spare, 128), last, f32)], axis=0)

    down = fill(owner, float(requests + 1))
    across = down.T
    ahead = (down < across) | ((down == across) & (line < lane))
    rank = jnp.sum(jnp.where(ahead, 1.0, 0.0), axis=0, keepdims=True)
    hit = rank == line
    index = jnp.where(lane < float(slots), lane, 0.0)
    order = jnp.sum(jnp.where(hit, index, 0.0), axis=1, keepdims=True)
    sorted_live = jnp.sum(jnp.where(hit, fill(live, 0.0).T, 0.0), axis=1, keepdims=True)
    first = jnp.sum(jnp.where(down < lane, 1.0, 0.0), axis=0, keepdims=True)
    both = jnp.where(lane == 0.0, order, jnp.where(lane == 1.0, sorted_live, 0.0)).T
    rows = jnp.where(line[0:8] == 2.0, first, both[0:8])
    meta_ref[...] = rows.astype(jnp.int32)


def gather_kernel(
    nrh, heads, length_ref, nope_hbm, rope_hbm, weights_hbm, cache_hbm, table_hbm,
    query_hbm, keys_hbm, meta_hbm, meta_ref,
    nope_ref, rope_ref, weights_ref, cache_ref, table_ref, out_ref, keys_ref,
    local_sem, store_sem, send, recv,
):
    rh, rl, cg, yl, core = place(nrh)
    q = yl * 2 + core
    qy = (1 - yl) * 2 + core
    z_peer = lambda k: device(k, rl, cg, yl, core)
    x_peer = device(rh, 1 - rl, cg, yl, core)
    y_peer = device(rh, rl, cg, 1 - yl, core)
    c_peer = device(rh, rl, cg, yl, 1 - core)
    barrier = pltpu.get_barrier_semaphore()
    peers = [z_peer((rh + d) % nrh) for d in range(1, nrh)] + [x_peer, y_peer, c_peer]
    for peer in peers:
        pl.semaphore_signal(barrier, inc=1, device_id=peer, device_id_type=MESH)
    blocks = cache_hbm.shape[1] // BLOCK
    pages = BLOCK // PAGE
    loads = [
        pltpu.make_async_copy(nope_hbm, nope_ref, local_sem.at[0]),
        pltpu.make_async_copy(rope_hbm, rope_ref, local_sem.at[1]),
    ]
    quarter = heads // 4
    weight_loads = [
        pltpu.make_async_copy(
            weights_hbm.at[pl.ds(n * quarter, quarter)], weights_ref.at[pl.ds(n * quarter, quarter)],
            local_sem.at[4 + CACHE_LOADS + n],
        )
        for n in range(4)
    ]
    span = cache_hbm.shape[1] // CACHE_LOADS
    cache_loads = [
        pltpu.make_async_copy(
            cache_hbm.at[:, pl.ds(j * span, span)], cache_ref.at[:, pl.ds(j * span, span)],
            local_sem.at[3 + j],
        )
        for j in range(CACHE_LOADS)
    ]
    load_table = pltpu.make_async_copy(table_hbm, table_ref, local_sem.at[3 + CACHE_LOADS])
    for one in loads + weight_loads + [load_table]:
        one.start()
    stores = []

    def store(source, target):
        one = pltpu.make_async_copy(source, target, store_sem.at[len(stores)])
        one.start()
        stores.append(one)

    turned = [0]

    def turn(count):
        for _ in range(count):
            b = turned[0]
            if b >= blocks:
                return
            if b * BLOCK % span == 0:
                cache_loads[b * BLOCK // span].wait()
            block = cache_ref[:, b * BLOCK : (b + 1) * BLOCK].T
            keys_ref[b * pages : (b + 1) * pages] = block.reshape(pages, PAGE, block.shape[1])
            turned[0] += 1
            if turned[0] % STORED == 0:
                done = pl.ds((turned[0] - STORED) * pages, STORED * pages)
                store(keys_ref.at[done], keys_hbm.at[done])

    for one in loads:
        one.wait()

    def ready(h):
        if h % quarter == 0:
            weight_loads[h // quarter].wait()
        if h == 3 * quarter:
            for one in cache_loads:
                one.start()

    rows = nope_ref[pl.ds(pl.multiple_of(q * 2 * heads, 2 * heads), 2 * heads), :]
    latent = head_diagonal(rows.astype(jnp.bfloat16), weights_ref, heads, ready)
    latent = latent.astype(jnp.bfloat16).astype(out_ref.dtype)
    width = weights_ref.shape[2]
    for i in range(2):
        out_ref[2 * q + i, rl, rh, :, 0:width] = latent[i * heads : (i + 1) * heads]
        out_ref[2 * q + i, rl, rh, :, width:] = rope_ref[2 * q + i]
    pl.semaphore_wait(barrier, len(peers))

    started = []

    def copy(a, k, b, slot, peer, send_slot=None):
        shard = out_ref.at[pl.ds(2 * b, 2), a] if k is None else out_ref.at[pl.ds(2 * b, 2), a, k]
        return pltpu.make_async_remote_copy(
            src_ref=shard,
            dst_ref=shard,
            send_sem=send.at[slot if send_slot is None else send_slot],
            recv_sem=recv.at[slot],
            device_id=peer,
            device_id_type=MESH,
        )

    def push(*args, **kw):
        one = copy(*args, **kw)
        one.start()
        started.append(one)

    def arrived(a, k, b, slot, peer):
        copy(a, k, b, slot, peer).wait_recv()

    def put(a, b):
        store(out_ref.at[pl.ds(2 * b, 2), a], query_hbm.at[pl.ds(2 * b, 2), a])

    Z, X, Y, D, C = 0, nrh, 2 * nrh, 3 * nrh, 4 * nrh
    half = nrh // 2
    clump = -(-blocks // 4)

    def spread(k):
        push(rl, k, q, X + k, x_peer)
        push(rl, k, q, Y + k, y_peer)

    step = 1 - 2 * (rh // half)
    for d in range(1, nrh):
        push(rl, rh, q, Z + rh, z_peer((rh + step * d + nrh) % nrh), send_slot=Z + d)
    spread(rh)
    load_table.wait()
    device_at = (rh * 2 + rl) * (lax.axis_size("col")) + cg * 4 + q
    list_pages(device_at, blocks * pages, length_ref, table_ref, meta_ref)
    store(meta_ref, meta_hbm.at[pl.ds(0, 8)])
    turn(clump)
    for d in range(1, nrh):
        k = (rh + step * d + nrh) % nrh
        arrived(rl, k, q, Z + k, z_peer(k))
        spread(k)
    push(rl, None, q, C, c_peer)
    put(rl, q)
    turn(clump)
    for k in range(nrh):
        arrived(1 - rl, k, q, X + k, x_peer)
        if k >= half:
            push(1 - rl, k, q, D + k, y_peer)
        arrived(rl, k, qy, Y + k, y_peer)
        if k < half:
            push(rl, k, qy, D + k, x_peer)
    push(1 - rl, None, q, C + 1, c_peer)
    push(rl, None, qy, C + 2, c_peer)
    put(1 - rl, q)
    put(rl, qy)
    turn(clump)
    for k in range(nrh):
        arrived(1 - rl, k, qy, D + k, x_peer if k < half else y_peer)
    push(1 - rl, None, qy, C + 3, c_peer)
    turn(blocks)
    put(1 - rl, qy)
    qc, qyc = yl * 2 + 1 - core, (1 - yl) * 2 + 1 - core
    for n, (a, b) in enumerate(((rl, qc), (1 - rl, qc), (rl, qyc), (1 - rl, qyc))):
        arrived(a, None, b, C + n, c_peer)
        put(a, b)
    for one in started:
        one.wait_send()
    for one in stores:
        one.wait()


def attend_kernel(
    scale, meta_hbm, query_hbm, keys_hbm, part_ref, stat_ref,
    meta_ref, query_ref, keys_ref, scores, tops, denoms, total, owner, start,
    query_sem, page_sem,
):
    requests, heads, _ = query_ref.shape
    width = part_ref.shape[2]
    fetch_lists = pltpu.make_async_copy(
        meta_hbm.at[pl.ds(0, 8)], meta_ref, query_sem.at[requests]
    )
    fetch_lists.start()

    def fetch(k):
        return pltpu.make_async_copy(
            keys_hbm.at[meta_ref[0, k]], keys_ref.at[k], page_sem.at[k]
        )

    def fetch_query(r):
        return pltpu.make_async_copy(query_hbm.at[r], query_ref.at[r], query_sem.at[r])

    def start_fetch(k, carry):
        fetch(k).start()
        return carry

    def end_fetch(k, carry):
        fetch(k).wait()
        return carry

    for r in range(requests):
        fetch_query(r).start()
    tops[...] = jnp.full(tops.shape, MASKED, jnp.float32)
    denoms[...] = jnp.zeros(denoms.shape, jnp.float32)
    total[...] = jnp.zeros(total.shape, jnp.float32)
    fetch_lists.wait()
    held = meta_ref[2, requests]
    lax.fori_loop(0, held, start_fetch, 0)
    for i in range(GROUP):
        keys_ref[held + i] = jnp.zeros(keys_ref.shape[1:], keys_ref.dtype)

    def list_request(r, count):
        begin, end = meta_ref[2, r], meta_ref[2, r + 1]
        groups = (end - begin + GROUP - 1) // GROUP

        def list_group(g, carry):
            owner[count + g] = r
            start[count + g] = begin + g * GROUP
            return carry

        lax.fori_loop(0, groups, list_group, 0)
        return count + groups

    count = lax.fori_loop(0, requests, list_request, 0)
    for i in range(PAIR - 1):
        owner[count + i] = requests
        start[count + i] = 0
    rounds = (count + PAIR - 1) // PAIR
    token = lax.broadcasted_iota(jnp.int32, (PAGE, heads), 0)

    def pages(at, columns_kept):
        rows = keys_ref[pl.ds(at, GROUP), :, 0:columns_kept]
        return rows.reshape(GROUP * PAGE, columns_kept)

    def end_query(r, carry):
        fetch_query(r).wait()
        return carry

    def score_round(n, carry):
        here, asked = carry
        wanted = jnp.maximum(owner[n * PAIR], owner[n * PAIR + PAIR - 1]) + 1
        wanted = jnp.minimum(wanted, requests)
        lax.fori_loop(asked, wanted, end_query, 0)
        need = jnp.maximum(start[n * PAIR], start[n * PAIR + PAIR - 1]) + GROUP
        need = jnp.maximum(jnp.minimum(need, held), here)
        lax.fori_loop(here, need, end_fetch, 0)
        products = []
        for u in range(PAIR):
            g = n * PAIR + u
            products.append(
                lax.dot_general(
                    pages(start[g], keys_ref.shape[2]),
                    query_ref[lax.rem(owner[g], requests)],
                    (((1,), (1,)), ((), ())),
                    preferred_element_type=jnp.float32,
                )
            )
        for u in range(PAIR):
            g = n * PAIR + u
            at, r = start[g], owner[g]
            end = jnp.where(r < requests, meta_ref[2, jnp.minimum(r, requests - 1) + 1], 0)
            top = tops[r]
            for j in range(GROUP):
                live = jnp.where(at + j < end, meta_ref[1, at + j], 0)
                rows = slice(j * PAGE, (j + 1) * PAGE)
                piece = jnp.where(token < live, products[u][rows] * scale, MASKED)
                scores[g, rows, :] = piece
                top = jnp.maximum(top, jnp.max(piece, axis=0, keepdims=True))
            tops[r] = top
        return need, wanted

    here, asked = lax.fori_loop(0, rounds, score_round, (0, 0))
    lax.fori_loop(here, held, end_fetch, 0)
    lax.fori_loop(asked, requests, end_query, 0)

    def sum_round(n, carry):
        products = []
        for u in range(PAIR):
            g = n * PAIR + u
            r = owner[g]
            expo = jnp.exp(scores[g] - tops[r][0:1]).astype(jnp.bfloat16)
            denoms[r] += jnp.sum(expo.astype(jnp.float32), axis=0, keepdims=True)
            products.append(
                lax.dot_general(
                    expo, pages(start[g], width), (((0,), (0,)), ((), ())),
                    preferred_element_type=jnp.float32,
                )
            )
        for u in range(PAIR):
            total[owner[n * PAIR + u]] += products[u]
        return carry

    lax.fori_loop(0, rounds, sum_round, 0)
    line = lax.broadcasted_iota(jnp.int32, stat_ref.shape[1:], 0)
    for r in range(requests):
        stat_ref[r] = jnp.where(line == 0, tops[r], jnp.where(line == 1, denoms[r], 0.0))
        part_ref[r] = total[r].astype(part_ref.dtype)


def columns(lines):
    line = lax.broadcasted_iota(jnp.int32, (8, 128), 0)
    tiles = []
    for t in range(0, len(lines), 8):
        tile = jnp.zeros((8, 128), jnp.float32)
        for i, one in enumerate(lines[t : t + 8]):
            tile = jnp.where(line == i, one, tile)
        tiles.append(tile)
    left = 128 - 8 * len(tiles)
    if left:
        tiles.append(jnp.zeros((left, 128), jnp.float32))
    return jnp.concatenate(tiles, axis=0).T


def reduce_kernel(
    nrh, ncg, heads, part_ref, stat_ref, weights_ref, out_ref, shared, core_part, core_stat, y_send, y_stat, y_part, y_stat_in, own_stat,
    row_send, row_stat, row_part, row_stat_in, mix, y_mix, lines, value, send, recv, row_sem_s, row_sem_r,
):
    rh, rl, cg, yl, core = place(nrh)
    nrow = 2 * nrh
    spots = nrow * ncg
    q = yl * 2 + core
    c_peer = device(rh, rl, cg, yl, 1 - core)
    y_peer = device(rh, rl, cg, 1 - yl, core)
    d_peer = device(rh, rl, cg, 1 - yl, 1 - core)
    me = (rl * nrh + rh) * ncg + cg

    def spot(i):
        place_i = i // ncg
        return device(place_i % nrh, place_i // nrh, i % ncg, yl, core)

    barrier = pltpu.get_barrier_semaphore()
    for peer in (c_peer, y_peer, d_peer):
        pl.semaphore_signal(barrier, inc=1, device_id=peer, device_id_type=MESH)

    def hello(d, carry):
        pl.semaphore_signal(
            barrier, inc=1, device_id=spot((me + d) % spots), device_id_type=MESH
        )
        return carry

    lax.fori_loop(1, spots, hello, 0)

    def block_of(y, c):
        return pl.ds(2 * (2 * y + c), 2)

    pl.semaphore_wait(barrier, spots + 2)

    def remote(src, dst, slot, peer):
        return pltpu.make_async_remote_copy(
            src_ref=src, dst_ref=dst, send_sem=send.at[slot], recv_sem=recv.at[slot],
            device_id=peer, device_id_type=MESH,
        )

    started = []

    def push(*args):
        one = remote(*args)
        one.start()
        started.append(one)
        return one

    stat_in = push(stat_ref, core_stat, 0, c_peer)
    base = 4 + nrow
    core_in = []
    for d in range(1, nrow + 1):
        place_k = (rl * nrh + rh + d) % nrow
        a, k = place_k // nrh, place_k % nrh
        core_in.append(
            push(
                part_ref.at[block_of(1 - yl, 1 - core), a, k], core_part.at[0, :, a, k],
                base + 2 + d, c_peer,
            )
        )
    own_in = push(part_ref.at[block_of(yl, 1 - core)], core_part.at[1], 2, c_peer)
    line = lax.broadcasted_iota(jnp.int32, (8, 128), 0)

    def merge_stats(first, second):
        top = jnp.maximum(first[0:1], second[0:1])
        one, two = jnp.exp(first[0:1] - top), jnp.exp(second[0:1] - top)
        denom = one * first[1:2] + two * second[1:2]
        return jnp.where(line == 0, top, jnp.where(line == 1, denom, 0.0)), [one, two]

    def merge_chunk(table, n, place_k, first, second):
        weight = table[pl.ds(pl.multiple_of(place_k * heads, heads), heads), :]
        one, two = weight[:, 2 * n : 2 * n + 1], weight[:, 2 * n + 1 : 2 * n + 2]
        return one * first.astype(jnp.float32) + two * second.astype(jnp.float32)

    stat_in.wait_recv()
    weights = []
    for side in range(2):
        stats = y_stat if side == 0 else own_stat
        for i in range(2):
            r = 2 * (2 * (1 - yl if side == 0 else yl) + core) + i
            stats[i], pair = merge_stats(stat_ref[r], core_stat[r])
            weights += pair
        if side == 0:
            push(y_stat, y_stat_in, 3, y_peer)
    mix[...] = columns(weights)

    def core_merge(side, i, place_k):
        y = 1 - yl if side == 0 else yl
        a, k = place_k // nrh, place_k % nrh
        return merge_chunk(
            mix, 2 * side + i, place_k, part_ref[2 * (2 * y + core) + i, a, k],
            core_part[side, i, a, k],
        )

    for d in range(1, nrow + 1):
        place_k = (rl * nrh + rh + d) % nrow
        a, k = place_k // nrh, place_k % nrh
        core_in[d - 1].wait_recv()
        for i in range(2):
            y_send[a, k, i] = core_merge(0, i, place_k).astype(y_send.dtype)
        push(y_send.at[a, k], y_part.at[a, k], 3 + d, y_peer)

    remote(y_stat, y_stat_in, 3, y_peer).wait_recv()
    weights = []
    for i in range(2):
        row_stat[i], pair = merge_stats(own_stat[i], y_stat_in[i])
        weights += pair
    y_mix[...] = columns(weights)

    def row_copies(to, source, d):
        return (
            pltpu.make_async_remote_copy(
                src_ref=row_send.at[to // ncg], dst_ref=row_part.at[source],
                send_sem=row_sem_s.at[0, d], recv_sem=row_sem_r.at[0, source],
                device_id=spot(to), device_id_type=MESH,
            ),
            pltpu.make_async_remote_copy(
                src_ref=row_stat, dst_ref=row_stat_in.at[source],
                send_sem=row_sem_s.at[1, d], recv_sem=row_sem_r.at[1, source],
                device_id=spot(to), device_id_type=MESH,
            ),
        )

    def send_stat(d, carry):
        row_copies((me + d) % spots, me, d)[1].start()
        return carry

    lax.fori_loop(1, spots, send_stat, 0)
    row_stat_in[me] = row_stat[...]

    def chunk_step(place_k, d):
        a, k = place_k // nrh, place_k % nrh
        remote(y_send.at[a, k], y_part.at[a, k], 3 + d, y_peer).wait_recv()
        for i in range(2):
            row_send[place_k, i] = merge_chunk(
                y_mix, i, place_k, core_merge(1, i, place_k), y_part[a, k, i]
            ).astype(row_send.dtype)

    own_in.wait_recv()
    my_heads = pl.ds(pl.multiple_of((rl * nrh + rh) * heads, heads), heads)

    for d in range(1, nrow + 1):
        place_k = (rl * nrh + rh + d) % nrow
        chunk_step(place_k, d)

        def send_chunk(g, carry, place_k=place_k):
            to = place_k * ncg + g

            @pl.when(to != me)
            def _():
                row_copies(to, me, (to - me + spots) % spots)[0].start()

            return carry

        lax.fori_loop(0, ncg, send_chunk, 0)
    row_part[me] = row_send[me // ncg]

    def take_stat(d, carry):
        row_copies(me, (me + d) % spots, d)[1].wait_recv()
        return carry

    lax.fori_loop(1, spots, take_stat, 0)
    weights, denoms = [], []
    for i in range(2):
        parts = [(row_stat_in[n, i][0:1], row_stat_in[n, i][1:2]) for n in range(spots)]
        top = functools.reduce(jnp.maximum, [one for one, _ in parts])
        shares = [jnp.exp(one - top) for one, _ in parts]
        denoms.append(sum(share * denom for share, (_, denom) in zip(shares, parts)))
        weights += shares
    weights += denoms
    for n in range(0, len(weights), 128):
        lines[n // 128] = columns(weights[n : n + 128])

    def column(n):
        return lines[n // 128, my_heads, :][:, n % 128 : n % 128 + 1]

    def take_part(d, carry):
        row_copies(me, (me + d) % spots, d)[0].wait_recv()
        return carry

    lax.fori_loop(1, spots, take_part, 0)

    for i in range(2):
        total = sum(
            column(i * spots + n) * row_part[n, i].astype(jnp.float32) for n in range(spots)
        )
        value[i * heads : (i + 1) * heads, :] = total / column(2 * spots + i)
    rows = value[...].astype(jnp.bfloat16)

    shared[q] = head_diagonal(rows, weights_ref, heads).reshape(2, heads, shared.shape[3])
    outs = ((c_peer, yl * 2 + 1 - core), (y_peer, (1 - yl) * 2 + core),
            (d_peer, (1 - yl) * 2 + 1 - core))
    for n, (peer, _) in enumerate(outs):
        push(shared.at[q], shared.at[q], base + n, peer)
    for n, (peer, owner) in enumerate(outs):
        remote(shared.at[owner], shared.at[owner], base + n, peer).wait_recv()
    size = shared.shape[3]
    for h in range(heads):
        block = shared[:, :, h, :].reshape(8, size)
        out_ref[:, h * size : (h + 1) * size] = block.astype(out_ref.dtype)
    for one in started:
        one.wait_send()

    def drain(d, carry):
        for one in row_copies((me + d) % spots, me, d):
            one.wait_send()
        return carry

    lax.fori_loop(1, spots, drain, 0)


def local(
    query_nope, query_rope, key_up_weight, value_up_weight, latent_cache, lengths, page_table
):
    scale = float(HEAD_NOPE_WIDTH + ROTARY_WIDTH) ** (-0.5)
    requests, heads, nope = query_nope.shape
    width = key_up_weight.shape[2]
    full = latent_cache.shape[1]
    nrow, ncol = lax.axis_size("row"), lax.axis_size("col")
    nrh, ncg = nrow // 2, ncol // 4
    all_heads = nrow * heads
    slots = latent_cache.shape[0] // PAGE
    wire = jnp.bfloat16 if heads % 16 == 0 else jnp.float32
    vmem = pl.BlockSpec(memory_space=pltpu.VMEM)
    smem = pl.BlockSpec(memory_space=pltpu.SMEM)
    hbm = pl.BlockSpec(memory_space=pl.ANY)

    queries, keys, meta = pl.pallas_call(
        functools.partial(gather_kernel, nrh, heads),
        out_shape=(
            jax.ShapeDtypeStruct((requests, 2, nrh, heads, full), wire),
            jax.ShapeDtypeStruct((slots, PAGE, full), jnp.bfloat16),
            jax.ShapeDtypeStruct((LIST_ROWS, 128), jnp.int32),
        ),
        in_specs=[smem] + [hbm] * 5,
        out_specs=(hbm, hbm, hbm),
        scratch_shapes=[
            pltpu.VMEM((8, 128), jnp.int32),
            pltpu.VMEM((requests * heads, nope), wire),
            pltpu.VMEM(query_rope.shape, wire),
            pltpu.VMEM(key_up_weight.shape, jnp.bfloat16),
            pltpu.VMEM((full, slots * PAGE), jnp.bfloat16),
            pltpu.VMEM(page_table.shape, jnp.int32),
            pltpu.VMEM((requests, 2, nrh, heads, full), wire),
            pltpu.VMEM((slots, PAGE, full), jnp.bfloat16),
            pltpu.SemaphoreType.DMA((8 + CACHE_LOADS,)),
            pltpu.SemaphoreType.DMA((9 + slots * PAGE // (BLOCK * STORED),)),
            pltpu.SemaphoreType.DMA((4 * nrh + 4,)), pltpu.SemaphoreType.DMA((4 * nrh + 4,))],
        compiler_params=pltpu.CompilerParams(
            collective_id=0, has_side_effects=True, vmem_limit_bytes=VMEM_LIMIT
        ),
        name="gather_queries",
    )(
        lengths,
        query_nope.astype(wire).reshape(requests * heads, nope),
        query_rope.astype(wire),
        key_up_weight,
        latent_cache.T,
        page_table,
    )
    queries = queries.reshape(requests, all_heads, full).astype(jnp.bfloat16)

    most = slots // GROUP + requests + PAIR
    part, stat = pl.pallas_call(
        functools.partial(attend_kernel, scale),
        out_shape=(
            jax.ShapeDtypeStruct((requests, all_heads, width), wire),
            jax.ShapeDtypeStruct((requests, 8, all_heads), jnp.float32),
        ),
        in_specs=[hbm, hbm, hbm],
        out_specs=(vmem, vmem),
        scratch_shapes=[
            pltpu.SMEM((8, 128), jnp.int32),
            pltpu.VMEM((requests, all_heads, full), jnp.bfloat16),
            pltpu.VMEM((slots + GROUP, PAGE, full), jnp.bfloat16),
            pltpu.VMEM((most, GROUP * PAGE, all_heads), jnp.float32),
            pltpu.VMEM((requests + 1, 8, all_heads), jnp.float32),
            pltpu.VMEM((requests + 1, 8, all_heads), jnp.float32),
            pltpu.VMEM((requests + 1, all_heads, width), jnp.float32),
            pltpu.SMEM((most,), jnp.int32),
            pltpu.SMEM((most,), jnp.int32),
            pltpu.SemaphoreType.DMA((requests + 1,)),
            pltpu.SemaphoreType.DMA((slots,)),
        ],
        compiler_params=pltpu.CompilerParams(vmem_limit_bytes=52 * 1024 * 1024),
        name="attend_pages",
    )(meta, queries, keys)

    spots = nrow * ncg
    f32 = jnp.float32
    shape = (2, nrh, 2, heads, width)
    values = pl.pallas_call(
        functools.partial(reduce_kernel, nrh, ncg, heads),
        out_shape=jax.ShapeDtypeStruct(
            (requests, heads * value_up_weight.shape[2]), jnp.bfloat16
        ),
        in_specs=[vmem] * 3,
        out_specs=vmem,
        scratch_shapes=[
            pltpu.VMEM((4, 2, heads, value_up_weight.shape[2]), f32),
            pltpu.VMEM((2, 2, 2, nrh, heads, width), wire),
            pltpu.VMEM((requests, 8, all_heads), f32),
            pltpu.VMEM(shape, wire),
            pltpu.VMEM((2, 8, all_heads), f32),
            pltpu.VMEM(shape, wire),
            pltpu.VMEM((2, 8, all_heads), f32),
            pltpu.VMEM((2, 8, all_heads), f32),
            pltpu.VMEM((nrow, 2, heads, width), wire),
            pltpu.VMEM((2, 8, all_heads), f32),
            pltpu.VMEM((spots, 2, heads, width), wire),
            pltpu.VMEM((spots, 2, 8, all_heads), f32),
            pltpu.VMEM((128, 128), f32),
            pltpu.VMEM((128, 128), f32),
            pltpu.VMEM((-(-(2 * spots + 2) // 128), 128, 128), f32),
            pltpu.VMEM((2 * heads, width), f32),
            pltpu.SemaphoreType.DMA((7 + 2 * nrow,)),
            pltpu.SemaphoreType.DMA((7 + 2 * nrow,)),
            pltpu.SemaphoreType.DMA((2, spots)),
            pltpu.SemaphoreType.DMA((2, spots)),
        ],
        compiler_params=pltpu.CompilerParams(
            collective_id=1, has_side_effects=True, vmem_limit_bytes=40 * 1024 * 1024
        ),
        name="reduce_parts",
    )(part.reshape(requests, 2, nrh, heads, width), stat, value_up_weight)
    return values


def solution(mesh):
    placed = (
        P(None, "row", None),
        P(None, "row", None),
        P("row", None, None),
        P("row", None, None),
        P(("row", "col"), None),
        P(),
        P(),
    )
    return jax.shard_map(
        local, mesh=mesh, in_specs=placed, out_specs=P(None, "row"), check_vma=False
    )
```

```python
import functools

import jax
import jax.numpy as jnp
from jax import lax
from jax.experimental import pallas as pl
from jax.experimental.pallas import tpu as pltpu
from jax.sharding import PartitionSpec as P

HEAD_NOPE_WIDTH = 128
ROTARY_WIDTH = 64
PAGE = 64
GROUP = 4
PAIR = 2
BLOCK = 128
CACHE_LOADS = 4
STORED = 4
LIST_ROWS = 8192
MASKED = -1e30
MESH = pl.DeviceIdType.MESH
VMEM_LIMIT = 62 * 1024 * 1024


def place(nrh):
    row, col = lax.axis_index("row"), lax.axis_index("col")
    return row // 2, row % 2, col // 4, (col // 2) % 2, col % 2


def device(rh, rl, cg, yl, core):
    return (rh * 2 + rl, cg * 4 + yl * 2 + core)


def head_diagonal(rows, weights_ref, heads, ready=lambda h: None):
    count = rows.shape[0]
    head = lax.broadcasted_iota(jnp.int32, (count, weights_ref.shape[2]), 0) % heads
    total = jnp.zeros((count, weights_ref.shape[2]), jnp.float32)
    for h in range(heads):
        ready(h)
        product = jnp.dot(rows, weights_ref[h], preferred_element_type=jnp.float32)
        total = jnp.where(head == h, product, total)
    return total


def list_pages(device_at, slots, length_ref, table_ref, meta_ref):
    requests, pages = table_ref.shape
    chunk = 128
    slot = lax.broadcasted_iota(jnp.int32, (slots, chunk), 0)
    owner = jnp.zeros((slots, chunk), jnp.int32)
    live = jnp.zeros((slots, chunk), jnp.int32)
    for r in range(requests):
        for c in range(pages // chunk):
            entry = table_ref[r : r + 1, c * chunk : (c + 1) * chunk] - device_at * slots
            page = lax.broadcasted_iota(jnp.int32, (1, chunk), 1) + c * chunk
            left = jnp.clip(length_ref[r] - page * PAGE, 0, PAGE)
            match = entry == slot
            owner += jnp.where(match, r - requests, 0)
            live += jnp.where(match, left, 0)
    f32 = jnp.float32
    owner = jnp.sum(owner.astype(f32), axis=1, keepdims=True) + float(requests)
    live = jnp.sum(live.astype(f32), axis=1, keepdims=True)
    line = lax.broadcasted_iota(jnp.int32, (128, 128), 0).astype(f32)
    lane = lax.broadcasted_iota(jnp.int32, (128, 128), 1).astype(f32)
    spare = 128 - slots

    def fill(column, last):
        wide = jnp.broadcast_to(column, (slots, 128))
        return jnp.concatenate([wide, jnp.full((spare, 128), last, f32)], axis=0)

    down = fill(owner, float(requests + 1))
    across = down.T
    ahead = (down < across) | ((down == across) & (line < lane))
    rank = jnp.sum(jnp.where(ahead, 1.0, 0.0), axis=0, keepdims=True)
    hit = rank == line
    index = jnp.where(lane < float(slots), lane, 0.0)
    order = jnp.sum(jnp.where(hit, index, 0.0), axis=1, keepdims=True)
    sorted_live = jnp.sum(jnp.where(hit, fill(live, 0.0).T, 0.0), axis=1, keepdims=True)
    first = jnp.sum(jnp.where(down < lane, 1.0, 0.0), axis=0, keepdims=True)
    both = jnp.where(lane == 0.0, order, jnp.where(lane == 1.0, sorted_live, 0.0)).T
    rows = jnp.where(line[0:8] == 2.0, first, both[0:8])
    meta_ref[...] = rows.astype(jnp.int32)


def gather_kernel(
    nrh, heads, length_ref, nope_hbm, rope_hbm, weights_hbm, cache_hbm, table_hbm,
    query_hbm, keys_hbm, meta_hbm, meta_ref,
    nope_ref, rope_ref, weights_ref, cache_ref, table_ref, out_ref, keys_ref,
    local_sem, store_sem, send, recv,
):
    rh, rl, cg, yl, core = place(nrh)
    q = yl * 2 + core
    qy = (1 - yl) * 2 + core
    z_peer = lambda k: device(k, rl, cg, yl, core)
    x_peer = device(rh, 1 - rl, cg, yl, core)
    y_peer = device(rh, rl, cg, 1 - yl, core)
    c_peer = device(rh, rl, cg, yl, 1 - core)
    barrier = pltpu.get_barrier_semaphore()
    peers = [z_peer((rh + d) % nrh) for d in range(1, nrh)] + [x_peer, y_peer, c_peer]
    for peer in peers:
        pl.semaphore_signal(barrier, inc=1, device_id=peer, device_id_type=MESH)
    blocks = cache_hbm.shape[1] // BLOCK
    pages = BLOCK // PAGE
    loads = [
        pltpu.make_async_copy(nope_hbm, nope_ref, local_sem.at[0]),
        pltpu.make_async_copy(rope_hbm, rope_ref, local_sem.at[1]),
    ]
    quarter = heads // 4
    weight_loads = [
        pltpu.make_async_copy(
            weights_hbm.at[pl.ds(n * quarter, quarter)], weights_ref.at[pl.ds(n * quarter, quarter)],
            local_sem.at[4 + CACHE_LOADS + n],
        )
        for n in range(4)
    ]
    span = cache_hbm.shape[1] // CACHE_LOADS
    cache_loads = [
        pltpu.make_async_copy(
            cache_hbm.at[:, pl.ds(j * span, span)], cache_ref.at[:, pl.ds(j * span, span)],
            local_sem.at[3 + j],
        )
        for j in range(CACHE_LOADS)
    ]
    load_table = pltpu.make_async_copy(table_hbm, table_ref, local_sem.at[3 + CACHE_LOADS])
    for one in loads + weight_loads + [load_table]:
        one.start()
    stores = []

    def store(source, target):
        one = pltpu.make_async_copy(source, target, store_sem.at[len(stores)])
        one.start()
        stores.append(one)

    turned = [0]

    def turn(count):
        for _ in range(count):
            b = turned[0]
            if b >= blocks:
                return
            if b * BLOCK % span == 0:
                cache_loads[b * BLOCK // span].wait()
            block = cache_ref[:, b * BLOCK : (b + 1) * BLOCK].T
            keys_ref[b * pages : (b + 1) * pages] = block.reshape(pages, PAGE, block.shape[1])
            turned[0] += 1
            if turned[0] % STORED == 0:
                done = pl.ds((turned[0] - STORED) * pages, STORED * pages)
                store(keys_ref.at[done], keys_hbm.at[done])

    for one in loads:
        one.wait()

    def ready(h):
        if h % quarter == 0:
            weight_loads[h // quarter].wait()
        if h == 3 * quarter:
            for one in cache_loads:
                one.start()

    rows = nope_ref[pl.ds(pl.multiple_of(q * 2 * heads, 2 * heads), 2 * heads), :]
    latent = head_diagonal(rows.astype(jnp.bfloat16), weights_ref, heads, ready)
    latent = latent.astype(jnp.bfloat16).astype(out_ref.dtype)
    width = weights_ref.shape[2]
    for i in range(2):
        out_ref[2 * q + i, rl, rh, :, 0:width] = latent[i * heads : (i + 1) * heads]
        out_ref[2 * q + i, rl, rh, :, width:] = rope_ref[2 * q + i]
    pl.semaphore_wait(barrier, len(peers))

    started = []

    def copy(a, k, b, slot, peer, send_slot=None):
        shard = out_ref.at[pl.ds(2 * b, 2), a] if k is None else out_ref.at[pl.ds(2 * b, 2), a, k]
        return pltpu.make_async_remote_copy(
            src_ref=shard,
            dst_ref=shard,
            send_sem=send.at[slot if send_slot is None else send_slot],
            recv_sem=recv.at[slot],
            device_id=peer,
            device_id_type=MESH,
        )

    def push(*args, **kw):
        one = copy(*args, **kw)
        one.start()
        started.append(one)

    def arrived(a, k, b, slot, peer):
        copy(a, k, b, slot, peer).wait_recv()

    def put(a, b):
        store(out_ref.at[pl.ds(2 * b, 2), a], query_hbm.at[pl.ds(2 * b, 2), a])

    Z, X, Y, D, C = 0, nrh, 2 * nrh, 3 * nrh, 4 * nrh
    half = nrh // 2
    clump = -(-blocks // 4)

    def spread(k):
        push(rl, k, q, X + k, x_peer)
        push(rl, k, q, Y + k, y_peer)

    step = 1 - 2 * (rh // half)
    for d in range(1, nrh):
        push(rl, rh, q, Z + rh, z_peer((rh + step * d + nrh) % nrh), send_slot=Z + d)
    spread(rh)
    load_table.wait()
    device_at = (rh * 2 + rl) * (lax.axis_size("col")) + cg * 4 + q
    list_pages(device_at, blocks * pages, length_ref, table_ref, meta_ref)
    store(meta_ref, meta_hbm.at[pl.ds(0, 8)])
    turn(clump)
    for d in range(1, nrh):
        k = (rh + step * d + nrh) % nrh
        arrived(rl, k, q, Z + k, z_peer(k))
        spread(k)
    push(rl, None, q, C, c_peer)
    put(rl, q)
    turn(clump)
    order = [(rh + step * d + nrh) % nrh for d in range(nrh)]
    for d, k in enumerate(order):
        arrived(1 - rl, k, q, X + k, x_peer)
        if d >= half:
            push(1 - rl, k, q, D + k, y_peer)
        arrived(rl, k, qy, Y + k, y_peer)
        if d < half:
            push(rl, k, qy, D + k, x_peer)
    push(1 - rl, None, q, C + 1, c_peer)
    push(rl, None, qy, C + 2, c_peer)
    put(1 - rl, q)
    put(rl, qy)
    turn(clump)
    for d, k in enumerate(order):
        arrived(1 - rl, k, qy, D + k, x_peer if d < half else y_peer)
    push(1 - rl, None, qy, C + 3, c_peer)
    turn(blocks)
    put(1 - rl, qy)
    qc, qyc = yl * 2 + 1 - core, (1 - yl) * 2 + 1 - core
    for n, (a, b) in enumerate(((rl, qc), (1 - rl, qc), (rl, qyc), (1 - rl, qyc))):
        arrived(a, None, b, C + n, c_peer)
        put(a, b)
    for one in started:
        one.wait_send()
    for one in stores:
        one.wait()


def attend_kernel(
    scale, meta_hbm, query_hbm, keys_hbm, part_ref, stat_ref,
    meta_ref, query_ref, keys_ref, scores, tops, denoms, total, owner, start,
    query_sem, page_sem,
):
    requests, heads, _ = query_ref.shape
    width = part_ref.shape[2]
    fetch_lists = pltpu.make_async_copy(
        meta_hbm.at[pl.ds(0, 8)], meta_ref, query_sem.at[requests]
    )
    fetch_lists.start()

    def fetch(k):
        return pltpu.make_async_copy(
            keys_hbm.at[meta_ref[0, k]], keys_ref.at[k], page_sem.at[k]
        )

    def fetch_query(r):
        return pltpu.make_async_copy(query_hbm.at[r], query_ref.at[r], query_sem.at[r])

    def start_fetch(k, carry):
        fetch(k).start()
        return carry

    def end_fetch(k, carry):
        fetch(k).wait()
        return carry

    for r in range(requests):
        fetch_query(r).start()
    tops[...] = jnp.full(tops.shape, MASKED, jnp.float32)
    denoms[...] = jnp.zeros(denoms.shape, jnp.float32)
    total[...] = jnp.zeros(total.shape, jnp.float32)
    fetch_lists.wait()
    held = meta_ref[2, requests]
    lax.fori_loop(0, held, start_fetch, 0)
    for i in range(GROUP):
        keys_ref[held + i] = jnp.zeros(keys_ref.shape[1:], keys_ref.dtype)

    def list_request(r, count):
        begin, end = meta_ref[2, r], meta_ref[2, r + 1]
        groups = (end - begin + GROUP - 1) // GROUP

        def list_group(g, carry):
            owner[count + g] = r
            start[count + g] = begin + g * GROUP
            return carry

        lax.fori_loop(0, groups, list_group, 0)
        return count + groups

    count = lax.fori_loop(0, requests, list_request, 0)
    for i in range(PAIR - 1):
        owner[count + i] = requests
        start[count + i] = 0
    rounds = (count + PAIR - 1) // PAIR
    token = lax.broadcasted_iota(jnp.int32, (PAGE, heads), 0)

    def pages(at, columns_kept):
        rows = keys_ref[pl.ds(at, GROUP), :, 0:columns_kept]
        return rows.reshape(GROUP * PAGE, columns_kept)

    def end_query(r, carry):
        fetch_query(r).wait()
        return carry

    def score_round(n, carry):
        here, asked = carry
        wanted = jnp.maximum(owner[n * PAIR], owner[n * PAIR + PAIR - 1]) + 1
        wanted = jnp.minimum(wanted, requests)
        lax.fori_loop(asked, wanted, end_query, 0)
        need = jnp.maximum(start[n * PAIR], start[n * PAIR + PAIR - 1]) + GROUP
        need = jnp.maximum(jnp.minimum(need, held), here)
        lax.fori_loop(here, need, end_fetch, 0)
        products = []
        for u in range(PAIR):
            g = n * PAIR + u
            products.append(
                lax.dot_general(
                    pages(start[g], keys_ref.shape[2]),
                    query_ref[lax.rem(owner[g], requests)],
                    (((1,), (1,)), ((), ())),
                    preferred_element_type=jnp.float32,
                )
            )
        for u in range(PAIR):
            g = n * PAIR + u
            at, r = start[g], owner[g]
            end = jnp.where(r < requests, meta_ref[2, jnp.minimum(r, requests - 1) + 1], 0)
            top = tops[r]
            for j in range(GROUP):
                live = jnp.where(at + j < end, meta_ref[1, at + j], 0)
                rows = slice(j * PAGE, (j + 1) * PAGE)
                piece = jnp.where(token < live, products[u][rows] * scale, MASKED)
                scores[g, rows, :] = piece
                top = jnp.maximum(top, jnp.max(piece, axis=0, keepdims=True))
            tops[r] = top
        return need, wanted

    here, asked = lax.fori_loop(0, rounds, score_round, (0, 0))
    lax.fori_loop(here, held, end_fetch, 0)
    lax.fori_loop(asked, requests, end_query, 0)

    def sum_round(n, carry):
        products = []
        for u in range(PAIR):
            g = n * PAIR + u
            r = owner[g]
            expo = jnp.exp(scores[g] - tops[r][0:1]).astype(jnp.bfloat16)
            denoms[r] += jnp.sum(expo.astype(jnp.float32), axis=0, keepdims=True)
            products.append(
                lax.dot_general(
                    expo, pages(start[g], width), (((0,), (0,)), ((), ())),
                    preferred_element_type=jnp.float32,
                )
            )
        for u in range(PAIR):
            total[owner[n * PAIR + u]] += products[u]
        return carry

    lax.fori_loop(0, rounds, sum_round, 0)
    line = lax.broadcasted_iota(jnp.int32, stat_ref.shape[1:], 0)
    for r in range(requests):
        stat_ref[r] = jnp.where(line == 0, tops[r], jnp.where(line == 1, denoms[r], 0.0))
        part_ref[r] = total[r].astype(part_ref.dtype)


def columns(lines):
    line = lax.broadcasted_iota(jnp.int32, (8, 128), 0)
    tiles = []
    for t in range(0, len(lines), 8):
        tile = jnp.zeros((8, 128), jnp.float32)
        for i, one in enumerate(lines[t : t + 8]):
            tile = jnp.where(line == i, one, tile)
        tiles.append(tile)
    left = 128 - 8 * len(tiles)
    if left:
        tiles.append(jnp.zeros((left, 128), jnp.float32))
    return jnp.concatenate(tiles, axis=0).T


def reduce_kernel(
    nrh, ncg, heads, part_ref, stat_ref, weights_ref, out_ref, shared, core_part, core_stat, y_send, y_stat, y_part, y_stat_in, own_stat,
    row_send, row_stat, row_part, row_stat_in, mix, y_mix, lines, value, send, recv, row_sem_s, row_sem_r,
):
    rh, rl, cg, yl, core = place(nrh)
    nrow = 2 * nrh
    spots = nrow * ncg
    q = yl * 2 + core
    c_peer = device(rh, rl, cg, yl, 1 - core)
    y_peer = device(rh, rl, cg, 1 - yl, core)
    d_peer = device(rh, rl, cg, 1 - yl, 1 - core)
    me = (rl * nrh + rh) * ncg + cg

    def spot(i):
        place_i = i // ncg
        return device(place_i % nrh, place_i // nrh, i % ncg, yl, core)

    barrier = pltpu.get_barrier_semaphore()
    for peer in (c_peer, y_peer, d_peer):
        pl.semaphore_signal(barrier, inc=1, device_id=peer, device_id_type=MESH)

    def hello(d, carry):
        pl.semaphore_signal(
            barrier, inc=1, device_id=spot((me + d) % spots), device_id_type=MESH
        )
        return carry

    lax.fori_loop(1, spots, hello, 0)

    def block_of(y, c):
        return pl.ds(2 * (2 * y + c), 2)

    pl.semaphore_wait(barrier, spots + 2)

    def remote(src, dst, slot, peer):
        return pltpu.make_async_remote_copy(
            src_ref=src, dst_ref=dst, send_sem=send.at[slot], recv_sem=recv.at[slot],
            device_id=peer, device_id_type=MESH,
        )

    started = []

    def push(*args):
        one = remote(*args)
        one.start()
        started.append(one)
        return one

    stat_in = push(stat_ref, core_stat, 0, c_peer)
    base = 4 + nrow
    core_in = []
    for d in range(1, nrow + 1):
        place_k = (rl * nrh + rh + d) % nrow
        a, k = place_k // nrh, place_k % nrh
        core_in.append(
            push(
                part_ref.at[block_of(1 - yl, 1 - core), a, k], core_part.at[0, :, a, k],
                base + 2 + d, c_peer,
            )
        )
    own_in = push(part_ref.at[block_of(yl, 1 - core)], core_part.at[1], 2, c_peer)
    line = lax.broadcasted_iota(jnp.int32, (8, 128), 0)

    def merge_stats(first, second):
        top = jnp.maximum(first[0:1], second[0:1])
        one, two = jnp.exp(first[0:1] - top), jnp.exp(second[0:1] - top)
        denom = one * first[1:2] + two * second[1:2]
        return jnp.where(line == 0, top, jnp.where(line == 1, denom, 0.0)), [one, two]

    def merge_chunk(table, n, place_k, first, second):
        weight = table[pl.ds(pl.multiple_of(place_k * heads, heads), heads), :]
        one, two = weight[:, 2 * n : 2 * n + 1], weight[:, 2 * n + 1 : 2 * n + 2]
        return one * first.astype(jnp.float32) + two * second.astype(jnp.float32)

    stat_in.wait_recv()
    weights = []
    for side in range(2):
        stats = y_stat if side == 0 else own_stat
        for i in range(2):
            r = 2 * (2 * (1 - yl if side == 0 else yl) + core) + i
            stats[i], pair = merge_stats(stat_ref[r], core_stat[r])
            weights += pair
        if side == 0:
            push(y_stat, y_stat_in, 3, y_peer)
    mix[...] = columns(weights)

    def core_merge(side, i, place_k):
        y = 1 - yl if side == 0 else yl
        a, k = place_k // nrh, place_k % nrh
        return merge_chunk(
            mix, 2 * side + i, place_k, part_ref[2 * (2 * y + core) + i, a, k],
            core_part[side, i, a, k],
        )

    for d in range(1, nrow + 1):
        place_k = (rl * nrh + rh + d) % nrow
        a, k = place_k // nrh, place_k % nrh
        core_in[d - 1].wait_recv()
        for i in range(2):
            y_send[a, k, i] = core_merge(0, i, place_k).astype(y_send.dtype)
        push(y_send.at[a, k], y_part.at[a, k], 3 + d, y_peer)

    remote(y_stat, y_stat_in, 3, y_peer).wait_recv()
    weights = []
    for i in range(2):
        row_stat[i], pair = merge_stats(own_stat[i], y_stat_in[i])
        weights += pair
    y_mix[...] = columns(weights)

    def row_copies(to, source, d):
        return (
            pltpu.make_async_remote_copy(
                src_ref=row_send.at[to // ncg], dst_ref=row_part.at[source],
                send_sem=row_sem_s.at[0, d], recv_sem=row_sem_r.at[0, source],
                device_id=spot(to), device_id_type=MESH,
            ),
            pltpu.make_async_remote_copy(
                src_ref=row_stat, dst_ref=row_stat_in.at[source],
                send_sem=row_sem_s.at[1, d], recv_sem=row_sem_r.at[1, source],
                device_id=spot(to), device_id_type=MESH,
            ),
        )

    def send_stat(d, carry):
        row_copies((me + d) % spots, me, d)[1].start()
        return carry

    lax.fori_loop(1, spots, send_stat, 0)
    row_stat_in[me] = row_stat[...]

    def chunk_step(place_k, d):
        a, k = place_k // nrh, place_k % nrh
        remote(y_send.at[a, k], y_part.at[a, k], 3 + d, y_peer).wait_recv()
        for i in range(2):
            row_send[place_k, i] = merge_chunk(
                y_mix, i, place_k, core_merge(1, i, place_k), y_part[a, k, i]
            ).astype(row_send.dtype)

    own_in.wait_recv()
    my_heads = pl.ds(pl.multiple_of((rl * nrh + rh) * heads, heads), heads)

    for d in range(1, nrow + 1):
        place_k = (rl * nrh + rh + d) % nrow
        chunk_step(place_k, d)

        def send_chunk(g, carry, place_k=place_k):
            to = place_k * ncg + g

            @pl.when(to != me)
            def _():
                row_copies(to, me, (to - me + spots) % spots)[0].start()

            return carry

        lax.fori_loop(0, ncg, send_chunk, 0)
    row_part[me] = row_send[me // ncg]

    def take_stat(d, carry):
        row_copies(me, (me + d) % spots, d)[1].wait_recv()
        return carry

    lax.fori_loop(1, spots, take_stat, 0)
    weights, denoms = [], []
    for i in range(2):
        parts = [(row_stat_in[n, i][0:1], row_stat_in[n, i][1:2]) for n in range(spots)]
        top = functools.reduce(jnp.maximum, [one for one, _ in parts])
        shares = [jnp.exp(one - top) for one, _ in parts]
        denoms.append(sum(share * denom for share, (_, denom) in zip(shares, parts)))
        weights += shares
    weights += denoms
    for n in range(0, len(weights), 128):
        lines[n // 128] = columns(weights[n : n + 128])

    def column(n):
        return lines[n // 128, my_heads, :][:, n % 128 : n % 128 + 1]

    def take_part(d, carry):
        row_copies(me, (me + d) % spots, d)[0].wait_recv()
        return carry

    lax.fori_loop(1, spots, take_part, 0)

    for i in range(2):
        total = sum(
            column(i * spots + n) * row_part[n, i].astype(jnp.float32) for n in range(spots)
        )
        value[i * heads : (i + 1) * heads, :] = total / column(2 * spots + i)
    rows = value[...].astype(jnp.bfloat16)

    shared[q] = head_diagonal(rows, weights_ref, heads).reshape(2, heads, shared.shape[3])
    outs = ((c_peer, yl * 2 + 1 - core), (y_peer, (1 - yl) * 2 + core),
            (d_peer, (1 - yl) * 2 + 1 - core))
    for n, (peer, _) in enumerate(outs):
        push(shared.at[q], shared.at[q], base + n, peer)
    for n, (peer, owner) in enumerate(outs):
        remote(shared.at[owner], shared.at[owner], base + n, peer).wait_recv()
    size = shared.shape[3]
    for h in range(heads):
        block = shared[:, :, h, :].reshape(8, size)
        out_ref[:, h * size : (h + 1) * size] = block.astype(out_ref.dtype)
    for one in started:
        one.wait_send()

    def drain(d, carry):
        for one in row_copies((me + d) % spots, me, d):
            one.wait_send()
        return carry

    lax.fori_loop(1, spots, drain, 0)


def local(
    query_nope, query_rope, key_up_weight, value_up_weight, latent_cache, lengths, page_table
):
    scale = float(HEAD_NOPE_WIDTH + ROTARY_WIDTH) ** (-0.5)
    requests, heads, nope = query_nope.shape
    width = key_up_weight.shape[2]
    full = latent_cache.shape[1]
    nrow, ncol = lax.axis_size("row"), lax.axis_size("col")
    nrh, ncg = nrow // 2, ncol // 4
    all_heads = nrow * heads
    slots = latent_cache.shape[0] // PAGE
    wire = jnp.bfloat16 if heads % 16 == 0 else jnp.float32
    vmem = pl.BlockSpec(memory_space=pltpu.VMEM)
    smem = pl.BlockSpec(memory_space=pltpu.SMEM)
    hbm = pl.BlockSpec(memory_space=pl.ANY)

    queries, keys, meta = pl.pallas_call(
        functools.partial(gather_kernel, nrh, heads),
        out_shape=(
            jax.ShapeDtypeStruct((requests, 2, nrh, heads, full), wire),
            jax.ShapeDtypeStruct((slots, PAGE, full), jnp.bfloat16),
            jax.ShapeDtypeStruct((LIST_ROWS, 128), jnp.int32),
        ),
        in_specs=[smem] + [hbm] * 5,
        out_specs=(hbm, hbm, hbm),
        scratch_shapes=[
            pltpu.VMEM((8, 128), jnp.int32),
            pltpu.VMEM((requests * heads, nope), wire),
            pltpu.VMEM(query_rope.shape, wire),
            pltpu.VMEM(key_up_weight.shape, jnp.bfloat16),
            pltpu.VMEM((full, slots * PAGE), jnp.bfloat16),
            pltpu.VMEM(page_table.shape, jnp.int32),
            pltpu.VMEM((requests, 2, nrh, heads, full), wire),
            pltpu.VMEM((slots, PAGE, full), jnp.bfloat16),
            pltpu.SemaphoreType.DMA((8 + CACHE_LOADS,)),
            pltpu.SemaphoreType.DMA((9 + slots * PAGE // (BLOCK * STORED),)),
            pltpu.SemaphoreType.DMA((4 * nrh + 4,)), pltpu.SemaphoreType.DMA((4 * nrh + 4,))],
        compiler_params=pltpu.CompilerParams(
            collective_id=0, has_side_effects=True, vmem_limit_bytes=VMEM_LIMIT
        ),
        name="gather_queries",
    )(
        lengths,
        query_nope.astype(wire).reshape(requests * heads, nope),
        query_rope.astype(wire),
        key_up_weight,
        latent_cache.T,
        page_table,
    )
    queries = queries.reshape(requests, all_heads, full).astype(jnp.bfloat16)

    most = slots // GROUP + requests + PAIR
    part, stat = pl.pallas_call(
        functools.partial(attend_kernel, scale),
        out_shape=(
            jax.ShapeDtypeStruct((requests, all_heads, width), wire),
            jax.ShapeDtypeStruct((requests, 8, all_heads), jnp.float32),
        ),
        in_specs=[hbm, hbm, hbm],
        out_specs=(vmem, vmem),
        scratch_shapes=[
            pltpu.SMEM((8, 128), jnp.int32),
            pltpu.VMEM((requests, all_heads, full), jnp.bfloat16),
            pltpu.VMEM((slots + GROUP, PAGE, full), jnp.bfloat16),
            pltpu.VMEM((most, GROUP * PAGE, all_heads), jnp.float32),
            pltpu.VMEM((requests + 1, 8, all_heads), jnp.float32),
            pltpu.VMEM((requests + 1, 8, all_heads), jnp.float32),
            pltpu.VMEM((requests + 1, all_heads, width), jnp.float32),
            pltpu.SMEM((most,), jnp.int32),
            pltpu.SMEM((most,), jnp.int32),
            pltpu.SemaphoreType.DMA((requests + 1,)),
            pltpu.SemaphoreType.DMA((slots,)),
        ],
        compiler_params=pltpu.CompilerParams(vmem_limit_bytes=52 * 1024 * 1024),
        name="attend_pages",
    )(meta, queries, keys)

    spots = nrow * ncg
    f32 = jnp.float32
    shape = (2, nrh, 2, heads, width)
    values = pl.pallas_call(
        functools.partial(reduce_kernel, nrh, ncg, heads),
        out_shape=jax.ShapeDtypeStruct(
            (requests, heads * value_up_weight.shape[2]), jnp.bfloat16
        ),
        in_specs=[vmem] * 3,
        out_specs=vmem,
        scratch_shapes=[
            pltpu.VMEM((4, 2, heads, value_up_weight.shape[2]), f32),
            pltpu.VMEM((2, 2, 2, nrh, heads, width), wire),
            pltpu.VMEM((requests, 8, all_heads), f32),
            pltpu.VMEM(shape, wire),
            pltpu.VMEM((2, 8, all_heads), f32),
            pltpu.VMEM(shape, wire),
            pltpu.VMEM((2, 8, all_heads), f32),
            pltpu.VMEM((2, 8, all_heads), f32),
            pltpu.VMEM((nrow, 2, heads, width), wire),
            pltpu.VMEM((2, 8, all_heads), f32),
            pltpu.VMEM((spots, 2, heads, width), wire),
            pltpu.VMEM((spots, 2, 8, all_heads), f32),
            pltpu.VMEM((128, 128), f32),
            pltpu.VMEM((128, 128), f32),
            pltpu.VMEM((-(-(2 * spots + 2) // 128), 128, 128), f32),
            pltpu.VMEM((2 * heads, width), f32),
            pltpu.SemaphoreType.DMA((7 + 2 * nrow,)),
            pltpu.SemaphoreType.DMA((7 + 2 * nrow,)),
            pltpu.SemaphoreType.DMA((2, spots)),
            pltpu.SemaphoreType.DMA((2, spots)),
        ],
        compiler_params=pltpu.CompilerParams(
            collective_id=1, has_side_effects=True, vmem_limit_bytes=40 * 1024 * 1024
        ),
        name="reduce_parts",
    )(part.reshape(requests, 2, nrh, heads, width), stat, value_up_weight)
    return values


def solution(mesh):
    placed = (
        P(None, "row", None),
        P(None, "row", None),
        P("row", None, None),
        P("row", None, None),
        P(("row", "col"), None),
        P(),
        P(),
    )
    return jax.shard_map(
        local, mesh=mesh, in_specs=placed, out_specs=P(None, "row"), check_vma=False
    )
```
